32 devices in a mesh: dp: 8 (over z, core), chan: 4 (over y, x).
Axes of the slice: x: 2, y: 2, z: 4, core: 2. Of those that a mesh axis runs over, the one named last changes fastest.
Arguments:
- feat_in: bfloat16 [512, 32, 1024], P('chan', 'dp'), may hold values from -6 to 6
- rgb_in: float32 [32, 3, 1024], P('dp'), may hold values from -6 to 6
- latent: float32 [32, 512], P('dp'), may hold values from -6 to 6
- noise_first: float32 [32, 4096], P('dp'), may hold values from -6 to 6
- noise_second: float32 [32, 4096], P('dp'), may hold values from -6 to 6
- live_count: int32 [8], P('dp'), may hold values from 1 to 4, 24 in all
- conv_first: bfloat16 [9, 512, 512], P(None, 'chan'), may hold values from -0.09375 to 0.09375
- conv_second: bfloat16 [9, 512, 512], P(None, 'chan'), may hold values from -0.09375 to 0.09375
- style_weight: float32 [3, 512, 512], P(None, None, 'chan'), may hold values from -0.25 to 0.25
- style_bias: float32 [3, 512], P(None, 'chan'), may hold values from 0.5 to 1.5
- rgb_weight: bfloat16 [3, 512], P(None, 'chan'), may hold values from -0.25 to 0.25
- conv_bias: float32 [2, 512], P(None, 'chan'), may hold values from -3 to 3
- rgb_bias: float32 [3], replicated, may hold values from -3 to 3
- noise_gain: float32 [2], replicated, may hold values from 0.2 to 1
- feat_grad: bfloat16 [512, 32, 4096], P('chan', 'dp'), may hold values from -6 to 6
- rgb_grad: float32 [32, 3, 4096], P('dp'), may hold values from -6 to 6
Outputs:
- feat_out: bfloat16 [512, 32, 4096], P('chan', 'dp')
- rgb_out: float32 [32, 3, 4096], P('dp', None, 'chan')
- feat_in_grad: float32 [512, 32, 1024], P('chan', 'dp')
- rgb_in_grad: float32 [32, 3, 1024], P('dp')
- latent_grad: float32 [32, 512], P('dp')
- conv_first_grad: float32 [9, 512, 512], P(None, 'chan')
- conv_second_grad: float32 [9, 512, 512], P(None, 'chan')
- style_weight_grad: float32 [3, 512, 512], P(None, None, 'chan')
- style_bias_grad: float32 [3, 512], P(None, 'chan')
- rgb_weight_grad: float32 [3, 512], P(None, 'chan')
- conv_bias_grad: float32 [2, 512], P(None, 'chan')
- rgb_bias_grad: float32 [3], replicated
- noise_gain_grad: float32 [2], replicated
The draws below stay inside these ranges and needn't reach their ends.
Inputs may be any that keep to these rules, and one draw needn't show every extreme that they name: Shard s holds images in its first live_count[s] slots of 4; its other slots are empty. The counts add up to 24, and some shard is full.
All inputs are finite; a program needn't handle non-finite values.
Results may differ from the reference program's by a relative error of at most 0.0059.
Values may be sent and summed in bfloat16 or wider, within the bound.
A program may use at most 320 MiB of HBM per device.

```python
import math
import jax
import jax.numpy as jnp
import numpy as np
from jax import lax

CH = 512
LATENT = 512
SIDE = 64
IMG_DEV = 4
HALF = 32
PIX = 4096
HALF_PIX = 1024
IMAGES = 32
TOTAL_LIVE = 24
N_DP = 8


def levels(stream_key, shape, cuts, low, largest):
    factor_of, own = 1.0, jax.random.fold_in(stream_key, 6)
    for position, parts in cuts:
        heights = jnp.exp(jax.random.uniform(jax.random.fold_in(own, position), (parts,), jnp.float32, low / len(cuts), largest / len(cuts)))
        factor_of = factor_of * jnp.repeat(heights, shape[position] // parts).reshape([-1 if axis == position else 1 for axis in range(len(shape))])
    return factor_of


def length_profile(number_of, total, limit, skew):
    loads = [(1 << 20) // math.isqrt(grade ** skew) + 1 for grade in range(2, number_of + 1)]
    rest, holding = total - limit - (number_of - 1), [1] * (number_of - 1)
    while rest > 0:
        movable = [i for i in range(number_of - 1) if holding[i] < limit]
        mass, left = sum([loads[i] for i in movable]), rest
        for i in movable:
            more = min(limit - holding[i], max(1, left * loads[i] // mass), rest)
            holding[i] = holding[i] + more
            rest = rest - more
    return np.array([limit] + holding)


def uneven_parts(own_key, count, total, most, slope):
    if count == 2:
        one = jax.random.randint(own_key, (), max(1, total - most), min(most, total - 1) + 1)
        return jnp.stack([one, total - one])
    tallies = jnp.asarray(length_profile(count, total, most, slope), jnp.int32)
    couples = (count - 1) // 2
    donor, receiver = tallies[1:1 + 2 * couples:2], tallies[2:2 + 2 * couples:2]
    room = jnp.minimum(donor - 1, most - receiver)
    passed = jax.random.randint(jax.random.fold_in(own_key, 1), (couples,), 0, 1 << 20) % (room + 1)
    tallies = tallies.at[1:1 + 2 * couples:2].set(donor - passed).at[2:2 + 2 * couples:2].set(receiver + passed)
    return tallies[jax.random.permutation(jax.random.fold_in(own_key, 2), count)]


def noise(own_key, extent, scale, most, split=(), held_as=jnp.bfloat16):
    values = scale * jax.random.normal(own_key, extent, jnp.float32)
    if split:
        values = values * levels(own_key, extent, split, -0.22, 0.18)
    return jnp.clip(values, -most, most).astype(held_as)


def setup_inputs(seed: int = 0) -> dict:
    key_list = jax.random.split(jax.random.key(seed), 17)
    return {
        "feat_in": noise(key_list[0], (CH, IMAGES, HALF_PIX), 1.0, 6.0, ((0, 4), (1, 8))),
        "rgb_in": noise(key_list[1], (IMAGES, 3, HALF_PIX), 1.0, 6.0, ((0, 8),), jnp.float32),
        "latent": noise(key_list[2], (IMAGES, LATENT), 1.0, 6.0, ((0, 8),), jnp.float32),
        "noise_first": noise(key_list[3], (IMAGES, PIX), 1.0, 6.0, ((0, 8),), jnp.float32),
        "noise_second": noise(key_list[4], (IMAGES, PIX), 1.0, 6.0, ((0, 8),), jnp.float32),
        "live_count": uneven_parts(key_list[5], N_DP, TOTAL_LIVE, IMG_DEV, 0).astype(jnp.int32),
        "conv_first": noise(key_list[6], (9, CH, CH), (9 * CH) ** -0.5, 0.09375, ((1, 4),)),
        "conv_second": noise(key_list[7], (9, CH, CH), (9 * CH) ** -0.5, 0.09375, ((1, 4),)),
        "style_weight": noise(key_list[8], (3, LATENT, CH), LATENT ** -0.5, 0.25, ((2, 4),), jnp.float32),
        "style_bias": jnp.clip(1.0 + 0.1 * jax.random.normal(key_list[9], (3, CH), jnp.float32), 0.5, 1.5),
        "rgb_weight": noise(key_list[10], (3, CH), CH ** -0.5, 0.25, ((1, 4),)),
        "conv_bias": noise(key_list[11], (2, CH), 0.5, 3.0, ((1, 4),), jnp.float32),
        "rgb_bias": noise(key_list[12], (3,), 0.5, 3.0, (), jnp.float32),
        "noise_gain": jnp.clip(jax.random.uniform(key_list[13], (2,), jnp.float32, 0.2, 1.0), 0.2, 1.0),
        "feat_grad": noise(key_list[14], (CH, IMAGES, PIX), 1.0, 6.0, ((0, 4), (1, 8))),
        "rgb_grad": noise(key_list[15], (IMAGES, 3, PIX), 1.0, 6.0, ((0, 8),), jnp.float32),
    }


@jax.custom_vjp
def low(v):
    return lax.optimization_barrier(v.astype(jnp.bfloat16)).astype(jnp.float32)

@jax.custom_vjp
def low_back(v):
    return v

def low_keep(v):
    return (low(v), None)

def low_pass(kept, grad):
    return (grad,)

def back_keep(v):
    return (v, None)

def back_low(kept, grad):
    return (low(grad),)
low.defvjp(low_keep, low_pass)
low_back.defvjp(back_keep, back_low)
precise = lax.Precision.HIGHEST
epsilon = 1e-08
root_two = 1.4142135623730951
phase_taps = (((1, 0),), ((2, 0), (0, 1)))
phase_pairs = ((0, 0), (0, 1), (1, 0), (1, 1))

def leaky_silu(value):
    return root_two * (0.2 * value + 0.8 * jax.nn.silu(value))

def shifted(field, row_shift, col_shift, width):
    cells = field.shape[-1]
    offset = row_shift * width + col_shift
    if offset > 0:
        result = jnp.concatenate([field[..., offset:], jnp.zeros(field.shape[:-1] + (offset,), field.dtype)], axis=-1)
    elif offset < 0:
        result = jnp.concatenate([jnp.zeros(field.shape[:-1] + (-offset,), field.dtype), field[..., :cells + offset]], axis=-1)
    else:
        result = field
    if col_shift != 0:
        column = jnp.arange(cells) % width
        inside = (column + col_shift >= 0) & (column + col_shift < width)
        result = jnp.where(inside, result, jnp.zeros((), field.dtype))
    return result

def upsample_matrix(half_side):
    rows_out = jnp.arange(2 * half_side)[:, None]
    cols_in = jnp.arange(half_side)[None, :]
    centre = rows_out // 2
    beside = centre - 1 + 2 * (rows_out % 2)
    return (jnp.where(cols_in == centre, 0.75, 0.0) + jnp.where(cols_in == beside, 0.25, 0.0)).astype(jnp.float32)

def up_conv(inputs, weight, half_side):
    shifted_inputs = {}
    for row_shift in (0, 1):
        for col_shift in (0, 1):
            shifted_inputs[row_shift, col_shift] = shifted(inputs, row_shift, col_shift, half_side)
    phases = []
    for row_phase, col_phase in phase_pairs:
        summed = 0.0
        for row_tap, row_shift in phase_taps[row_phase]:
            for col_tap, col_shift in phase_taps[col_phase]:
                summed = summed + jnp.dot(weight[row_tap * 3 + col_tap], shifted_inputs[row_shift, col_shift], precision=precise)
        phases.append(summed)
    out_rows = weight.shape[1]
    blocked = jnp.stack(phases).reshape(2, 2, out_rows, half_side, half_side)
    return blocked.transpose(2, 3, 0, 4, 1).reshape(out_rows, 4 * half_side * half_side)

def flat_conv(inputs, weight, width):
    summed = 0.0
    for tap_index in range(9):
        summed = summed + jnp.dot(weight[tap_index], shifted(inputs, tap_index // 3 - 1, tap_index % 3 - 1, width), precision=precise)
    return summed

def image_forward(features, skip_rgb, latent_row, noise_one, noise_two, live_one, params, lift_matrix):
    conv_one, conv_two, style_weight, style_bias, rgb_one, conv_bias, rgb_bias, noise_gain = params
    styles = jnp.einsum('w,jwc->jc', latent_row, style_weight, precision=precise) + style_bias
    demod_one = lax.rsqrt(jnp.dot(lax.optimization_barrier(jnp.sum(conv_one * conv_one, axis=0)), styles[0] * styles[0], precision=precise) + epsilon)
    demod_two = lax.rsqrt(jnp.dot(lax.optimization_barrier(jnp.sum(conv_two * conv_two, axis=0)), styles[1] * styles[1], precision=precise) + epsilon)
    scaled_one = low(features * styles[0][:, None])
    raised = low_back(up_conv(scaled_one, conv_one, HALF))
    act_one = leaky_silu(raised * demod_one[:, None] + noise_gain[0] * noise_one[None, :] + conv_bias[0][:, None])
    scaled_two = low(act_one * styles[1][:, None])
    convolved = low_back(flat_conv(scaled_two, conv_two, SIDE))
    act_two = leaky_silu(convolved * demod_two[:, None] + noise_gain[1] * noise_two[None, :] + conv_bias[1][:, None])
    scaled_rgb = low(act_two * styles[2][:, None])
    color = low_back(jnp.dot(rgb_one, scaled_rgb, precision=precise))
    skip_up = jnp.einsum('up,kpq,vq->kuv', lift_matrix, skip_rgb.reshape(3, HALF, HALF), lift_matrix, precision=precise).reshape(3, SIDE * SIDE)
    rgb_image = color + rgb_bias[:, None] + skip_up
    return (act_two * live_one, rgb_image * live_one)

def reference(feat_in, rgb_in, latent, noise_first, noise_second, live_count, conv_first, conv_second, style_weight, style_bias, rgb_weight, conv_bias, rgb_bias, noise_gain, feat_grad, rgb_grad):
    images = feat_in.shape[1]
    image_index = jnp.arange(images)
    live_mask = (image_index % IMG_DEV < live_count[image_index // IMG_DEV]).astype(jnp.float32)
    params = (conv_first.astype(jnp.float32), conv_second.astype(jnp.float32), style_weight, style_bias, rgb_weight.astype(jnp.float32), conv_bias, rgb_bias, noise_gain)
    lift_matrix = upsample_matrix(HALF)

    def one_image(totals, carried):
        features, skip_rgb, latent_row, noise_one, noise_two, live_one, feat_cot, rgb_cot = carried

        def forward(feat_value, skip_value, latent_value, param_value):
            return image_forward(feat_value, skip_value, latent_value, noise_one, noise_two, live_one, param_value, lift_matrix)
        outputs, pullback = jax.vjp(forward, features.astype(jnp.float32), skip_rgb, latent_row, params)
        feat_back, skip_back, latent_back, params_back = pullback((feat_cot.astype(jnp.float32), rgb_cot))
        totals = jax.tree.map(jnp.add, totals, params_back)
        return (totals, (outputs[0].astype(jnp.bfloat16), outputs[1], feat_back, skip_back, latent_back))
    zeros = jax.tree.map(jnp.zeros_like, params)
    totals, stacked = lax.scan(one_image, zeros, (jnp.moveaxis(feat_in, 1, 0), rgb_in, latent, noise_first, noise_second, live_mask, jnp.moveaxis(feat_grad, 1, 0), rgb_grad))
    return (jnp.moveaxis(stacked[0], 0, 1), stacked[1], jnp.moveaxis(stacked[2], 0, 1), stacked[3], stacked[4], totals[0], totals[1], totals[2], totals[3], totals[4], totals[5], totals[6], totals[7])
```

```python
import functools

import jax
import jax.numpy as jnp
from jax import lax
from jax.experimental import pallas as pl
from jax.experimental.pallas import tpu as pltpu
from jax.sharding import PartitionSpec as P

SIDE = 64
HALF = 32


precise = lax.Precision.HIGHEST
epsilon = 1e-08
root_two = 1.4142135623730951
phase_taps = (((1, 0),), ((2, 0), (0, 1)))
phase_pairs = ((0, 0), (0, 1), (1, 0), (1, 1))


def leaky_silu(value):
    return root_two * (0.2 * value + 0.8 * jax.nn.silu(value))


def leaky_slope(value):
    sigma = jax.nn.sigmoid(value)
    return root_two * (0.2 + 0.8 * sigma * (1.0 + value * (1.0 - sigma)))


def shifted(field, row_shift, col_shift, width):
    cells = field.shape[-1]
    offset = row_shift * width + col_shift
    if offset > 0:
        result = jnp.concatenate(
            [field[..., offset:], jnp.zeros(field.shape[:-1] + (offset,), field.dtype)], axis=-1
        )
    elif offset < 0:
        result = jnp.concatenate(
            [jnp.zeros(field.shape[:-1] + (-offset,), field.dtype), field[..., : cells + offset]],
            axis=-1,
        )
    else:
        result = field
    if col_shift != 0:
        column = jnp.arange(cells) % width
        inside = (column + col_shift >= 0) & (column + col_shift < width)
        result = jnp.where(inside, result, jnp.zeros((), field.dtype))
    return result


def upsample_matrix(half_side):
    rows_out = jnp.arange(2 * half_side)[:, None]
    cols_in = jnp.arange(half_side)[None, :]
    centre = rows_out // 2
    beside = centre - 1 + 2 * (rows_out % 2)
    return (
        jnp.where(cols_in == centre, 0.75, 0.0) + jnp.where(cols_in == beside, 0.25, 0.0)
    ).astype(jnp.float32)


def alternate(phases, half_side):
    stacked = jnp.stack(phases)
    out_rows, batch_count = (stacked.shape[1], stacked.shape[2])
    blocked = stacked.reshape(2, 2, out_rows, batch_count, half_side, half_side)
    return blocked.transpose(2, 3, 4, 0, 5, 1).reshape(
        out_rows, batch_count, 4 * half_side * half_side
    )


def split_phases(field, half_side):
    out_rows, batch_count = (field.shape[0], field.shape[1])
    blocked = field.reshape(out_rows, batch_count, half_side, 2, half_side, 2)
    return [
        blocked[:, :, :, row_phase, :, col_phase].reshape(
            out_rows, batch_count, half_side * half_side
        )
        for row_phase, col_phase in phase_pairs
    ]


def up_conv(inputs, weight, half_side):
    shifted_inputs = {}
    for row_shift in (0, 1):
        for col_shift in (0, 1):
            shifted_inputs[row_shift, col_shift] = shifted(inputs, row_shift, col_shift, half_side)
    phases = []
    for row_phase, col_phase in phase_pairs:
        summed = None
        for row_tap, row_shift in phase_taps[row_phase]:
            for col_tap, col_shift in phase_taps[col_phase]:
                product = jnp.einsum(
                    "oc,cbp->obp",
                    weight[row_tap * 3 + col_tap],
                    shifted_inputs[row_shift, col_shift],
                    preferred_element_type=jnp.float32,
                )
                summed = product if summed is None else summed + product
        phases.append(summed)
    return alternate(phases, half_side)


def phase_grads(grad_field, half_side):
    grad_phases = split_phases(grad_field, half_side)
    shifted_grads = [None] * 9
    for phase_index in range(4):
        row_phase, col_phase = phase_pairs[phase_index]
        for row_tap, row_shift in phase_taps[row_phase]:
            for col_tap, col_shift in phase_taps[col_phase]:
                shifted_grads[row_tap * 3 + col_tap] = shifted(
                    grad_phases[phase_index], -row_shift, -col_shift, half_side
                )
    return shifted_grads


def flat_conv(inputs, weight, width):
    summed = None
    for tap_index in range(9):
        product = jnp.einsum(
            "oc,cbp->obp", weight[tap_index], inputs, preferred_element_type=jnp.float32
        )
        product = shifted(product, tap_index // 3 - 1, tap_index % 3 - 1, width)
        summed = product if summed is None else summed + product
    return summed


def body(
    feat_in,
    rgb_in,
    latent,
    noise_first,
    noise_second,
    live_count,
    conv_first,
    conv_second,
    style_weight,
    style_bias,
    rgb_weight,
    conv_bias,
    rgb_bias,
    noise_gain,
    feat_grad,
    rgb_grad,
):
    local_ch, images, half_pix = feat_in.shape
    pixels = feat_grad.shape[2]
    half_side = HALF
    full_side = SIDE
    chan_rank = lax.axis_index("chan")
    live_mask = (jnp.arange(images) < live_count[0]).astype(jnp.float32)
    styles = (
        jnp.einsum("bw,jwc->jbc", latent, style_weight, precision=precise) + style_bias[:, None, :]
    )
    first_all, second_all = (
        lax.all_gather(styles[0], "chan", axis=1, tiled=True),
        lax.all_gather(styles[1], "chan", axis=1, tiled=True),
    )
    weight_one = conv_first.astype(jnp.float32)
    weight_two = conv_second.astype(jnp.float32)
    squares_one = jnp.sum(weight_one * weight_one, axis=0)
    squares_two = jnp.sum(weight_two * weight_two, axis=0)
    demod_one = lax.rsqrt(
        jnp.dot(first_all * first_all, squares_one.T, precision=precise) + epsilon
    )
    demod_two = lax.rsqrt(
        jnp.dot(second_all * second_all, squares_two.T, precision=precise) + epsilon
    )
    scaled_one = (feat_in.astype(jnp.float32) * styles[0].T[:, :, None]).astype(jnp.bfloat16)
    gathered_one = lax.all_gather(scaled_one, "chan", axis=0, tiled=True)
    raised = up_conv(gathered_one, conv_first, half_side)
    pre_one = (
        raised * demod_one.T[:, :, None]
        + noise_gain[0] * noise_first[None, :, :]
        + conv_bias[0][:, None, None]
    )
    act_one = leaky_silu(pre_one)
    scaled_two = (act_one * styles[1].T[:, :, None]).astype(jnp.bfloat16)
    gathered_two = lax.all_gather(scaled_two, "chan", axis=0, tiled=True)
    convolved = flat_conv(gathered_two, conv_second, full_side)
    pre_two = (
        convolved * demod_two.T[:, :, None]
        + noise_gain[1] * noise_second[None, :, :]
        + conv_bias[1][:, None, None]
    )
    act_two = leaky_silu(pre_two)
    feat_out = (act_two * live_mask[None, :, None]).astype(jnp.bfloat16)
    scaled_rgb = (act_two * styles[2].T[:, :, None]).astype(jnp.bfloat16)
    color_part = jnp.einsum(
        "ko,obp->bkp", rgb_weight, scaled_rgb, preferred_element_type=jnp.float32
    )
    color = lax.psum_scatter(color_part, "chan", scatter_dimension=2, tiled=True)
    shard_pix = color.shape[2]
    lift_matrix = upsample_matrix(half_side)
    skip_up = jnp.einsum(
        "up,bkpq,vq->bkuv",
        lift_matrix,
        rgb_in.reshape(images, 3, half_side, half_side),
        lift_matrix,
        precision=precise,
    ).reshape(images, 3, pixels)
    skip_mine = lax.dynamic_slice_in_dim(skip_up, chan_rank * shard_pix, shard_pix, 2)
    rgb_out = (color + rgb_bias[None, :, None] + skip_mine) * live_mask[:, None, None]
    rgb_cot = rgb_grad * live_mask[:, None, None]
    color_cot = rgb_cot.astype(jnp.bfloat16)
    rgb_in_grad = jnp.einsum(
        "up,bkuv,vq->bkpq",
        lift_matrix,
        rgb_cot.reshape(images, 3, full_side, full_side),
        lift_matrix,
        precision=precise,
    ).reshape(images, 3, half_pix)
    rgb_bias_part = jnp.sum(rgb_cot, axis=(0, 2))
    rgb_weight_part = jnp.einsum(
        "bkp,obp->ko", color_cot, scaled_rgb, preferred_element_type=jnp.float32
    )
    back_rgb = jnp.einsum("ko,bkp->obp", rgb_weight, color_cot, preferred_element_type=jnp.float32)
    style_rgb_grad = jnp.sum(back_rgb * act_two, axis=2).T
    grad_pre_two = (
        feat_grad.astype(jnp.float32) * live_mask[None, :, None]
        + back_rgb * styles[2].T[:, :, None]
    ) * leaky_slope(pre_two)
    cot_two = (grad_pre_two * demod_two.T[:, :, None]).astype(jnp.bfloat16)
    inner_two = (
        -0.5 * demod_two * demod_two * demod_two * jnp.sum(grad_pre_two * convolved, axis=2).T
    )
    taps_two = jnp.stack(
        [
            shifted(cot_two, 1 - tap_index // 3, 1 - tap_index % 3, full_side)
            for tap_index in range(9)
        ]
    )
    squares_two_grad = jnp.dot(inner_two.T, second_all * second_all, precision=precise)
    conv_two_grad = (
        jnp.einsum("tobp,cbp->toc", taps_two, gathered_two, preferred_element_type=jnp.float32)
        + 2.0 * weight_two * squares_two_grad[None]
    )
    style_two_demod = 2.0 * second_all * jnp.dot(inner_two, squares_two, precision=precise)
    columns = conv_second
    back_two = lax.psum_scatter(
        jnp.einsum("toc,tobp->cbp", columns, taps_two, preferred_element_type=jnp.float32),
        "chan",
        scatter_dimension=0,
        tiled=True,
    )
    style_two_conv = jnp.sum(back_two * act_one, axis=2).T
    grad_pre_one = back_two * styles[1].T[:, :, None] * leaky_slope(pre_one)
    cot_one = (grad_pre_one * demod_one.T[:, :, None]).astype(jnp.bfloat16)
    inner_one = -0.5 * demod_one * demod_one * demod_one * jnp.sum(grad_pre_one * raised, axis=2).T
    taps_one = jnp.stack(phase_grads(cot_one, half_side))
    squares_one_grad = jnp.dot(inner_one.T, first_all * first_all, precision=precise)
    conv_one_grad = (
        jnp.einsum("tobp,cbp->toc", taps_one, gathered_one, preferred_element_type=jnp.float32)
        + 2.0 * weight_one * squares_one_grad[None]
    )
    style_one_demod = 2.0 * first_all * jnp.dot(inner_one, squares_one, precision=precise)
    columns = conv_first
    back_one = lax.psum_scatter(
        jnp.einsum("toc,tobp->cbp", columns, taps_one, preferred_element_type=jnp.float32),
        "chan",
        scatter_dimension=0,
        tiled=True,
    )
    feat_in_grad = back_one * styles[0].T[:, :, None]
    style_one_conv = jnp.sum(back_one * feat_in.astype(jnp.float32), axis=2).T
    demod_one_sum, demod_two_sum = (
        lax.psum_scatter(style_one_demod, "chan", scatter_dimension=1, tiled=True),
        lax.psum_scatter(style_two_demod, "chan", scatter_dimension=1, tiled=True),
    )
    style_grads = jnp.stack(
        [style_one_conv + demod_one_sum, style_two_conv + demod_two_sum, style_rgb_grad]
    )
    latent_part = jnp.einsum("jbc,jwc->bw", style_grads, style_weight, precision=precise)
    gain_part = jnp.stack(
        [
            jnp.sum(grad_pre_one * noise_first[None, :, :]),
            jnp.sum(grad_pre_two * noise_second[None, :, :]),
        ]
    )
    latent_grad, gain_chan = lax.psum((latent_part, gain_part), "chan")
    style_weight_part = jnp.einsum("bw,jbc->jwc", latent, style_grads, precision=precise)
    style_bias_part = jnp.sum(style_grads, axis=1)
    conv_bias_part = jnp.stack(
        [jnp.sum(grad_pre_one, axis=(1, 2)), jnp.sum(grad_pre_two, axis=(1, 2))]
    )
    totals = lax.psum(
        (
            conv_one_grad,
            conv_two_grad,
            style_weight_part,
            style_bias_part,
            rgb_weight_part,
            conv_bias_part,
            rgb_bias_part,
            gain_chan,
        ),
        "dp",
    )
    return (feat_out, rgb_out, feat_in_grad, rgb_in_grad, latent_grad) + tuple(totals)


BF = jnp.bfloat16
F32 = jnp.float32
TILE = 256
ROWS = 64
ANY = pl.BlockSpec(memory_space=pl.ANY)
SMEM = pl.BlockSpec(memory_space=pltpu.SMEM)
LIMIT = 56 * 1024 * 1024


def whole(shape):
    return pl.BlockSpec(shape, lambda j: (0,) * len(shape))


def dot(a, b):
    return jnp.dot(a, b, preferred_element_type=F32)


def dot_nt(a, b):
    return lax.dot_general(a, b, (((1,), (1,)), ((), ())), preferred_element_type=F32)


def wide(column):
    return jnp.concatenate([column] * (TILE // 128), axis=1)


def move(field, row_shift, col_shift):
    offset = row_shift * HALF + col_shift
    if offset == 0:
        return field
    cells = field.shape[1]
    lane = lax.broadcasted_iota(jnp.int32, field.shape, 1)
    row, col = lane // HALF, lane % HALF
    inside = (row + row_shift >= 0) & (row + row_shift < HALF)
    inside = inside & (col + col_shift >= 0) & (col + col_shift < HALF)
    rolled = pltpu.roll(field.astype(F32), (-offset) % cells, 1)
    return jnp.where(inside, rolled, 0.0).astype(field.dtype)


def near(parity, step):
    other = (parity + step) % 2
    return other, (parity + step - other) // 2


def copy_index(phase, row_step, col_step):
    a, r = near(phase // 2, row_step)
    b, q = near(phase % 2, col_step)
    return ((a * 2 + b) * 2 + abs(r)) * 2 + abs(q)


def make_copies(source, copies):
    chunk = 32

    @pl.loop(0, source.shape[1] // chunk)
    def _(i):
        rows = pl.ds(pl.multiple_of(i * chunk, chunk), chunk)
        for phase in range(4):
            field = source[phase, rows, :]
            row_sign = 1 if phase // 2 == 0 else -1
            col_sign = 1 if phase % 2 == 0 else -1
            for r in (0, 1):
                for q in (0, 1):
                    copies[(phase * 2 + r) * 2 + q, rows, :] = move(
                        field, row_sign * r, col_sign * q
                    )


def weight_copies(me, core, own, others, swapped, full, sem):
    result = [(own, pl.ds(pl.multiple_of(me * 128, 128), 128))]
    for k in (1, 2, 3):
        base = jnp.bitwise_xor(me, k) * 128
        result.append((others[k - 1], pl.ds(pl.multiple_of(base + core * 64, 64), 64)))
        result.append((swapped[k - 1], pl.ds(pl.multiple_of(base + (1 - core) * 64, 64), 64)))
    return [
        pltpu.make_async_copy(part, full.at[:, rows, :], sem.at[i])
        for i, (part, rows) in enumerate(result)
    ]


def demodulate(full, square_row, demod):
    chunk = 32

    @pl.loop(0, full.shape[1] // chunk)
    def _(i):
        rows = pl.ds(pl.multiple_of(i * chunk, chunk), chunk)
        total = None
        for t in range(9):
            value = full[t, rows, :].astype(F32)
            total = value * value if total is None else total + value * value
        total = jnp.sum(total * square_row, axis=1, keepdims=True)
        demod[rows, :] = jnp.broadcast_to(lax.rsqrt(total + epsilon), (chunk, 128))


def up_kernel(ids, gains, x0, x1, x2, x3, own, g1, g2, g3, s1, s2, s3, cols, rows_ref, noise,
              raised, scaled_two, full, scaled_one, demod, copies, sem):
    j = pl.program_id(0)
    me, core = ids[0], ids[1]

    @pl.when(j == 0)
    def _():
        moves = weight_copies(me, core, own, (g1, g2, g3), (s1, s2, s3), full, sem)
        for item in moves:
            item.start()
        for k, part in enumerate((x0, x1, x2, x3)):
            base = jnp.bitwise_xor(me, k) * 128

            @pl.loop(0, 128 // 32)
            def _(i):
                rows = pl.ds(pl.multiple_of(base + i * 32, 32), 32)
                here = pl.ds(pl.multiple_of(i * 32, 32), 32)
                style = jnp.concatenate([cols[0, rows, :]] * 8, axis=1)
                value = (part[here, :].astype(F32) * style).astype(BF)
                scaled_one[rows, :] = value
                for r in (0, 1):
                    for q in (0, 1):
                        copies[2 * r + q, rows, :] = move(value, r, q)

        for item in moves:
            item.wait()
        demodulate(full, rows_ref[0:1, :], demod)

    here = pl.ds(pl.multiple_of(j * TILE, TILE), TILE)
    for phase, (row_phase, col_phase) in enumerate(phase_pairs):
        total = None
        for k, r in phase_taps[row_phase]:
            for l, q in phase_taps[col_phase]:
                term = dot(full[3 * k + l], copies[2 * r + q, :, here])
                total = term if total is None else total + term
        raised[phase] = total
        noise_row = gains[0] * noise[phase : phase + 1, here]

        @pl.loop(0, raised.shape[1] // ROWS)
        def _(i):
            rows = pl.ds(pl.multiple_of(i * ROWS, ROWS), ROWS)
            pre = raised[phase, rows, :] * wide(demod[rows, :]) + noise_row + wide(cols[3, rows, :])
            act = leaky_silu(pre)
            scaled_two[phase, rows, :] = (act * wide(cols[1, rows, :])).astype(BF)


def conv_kernel(ids, gains, scaled_two, own, g1, g2, g3, s1, s2, s3, cols, rows_ref, noise, order, rgb_rows,
                convolved, f0, f1, f2, f3, color, full, demod, copies, ordered, for_rgb, sem):
    j = pl.program_id(0)
    me, core = ids[0], ids[1]

    @pl.when(j == 0)
    def _():
        moves = weight_copies(me, core, own, (g1, g2, g3), (s1, s2, s3), full, sem)
        for item in moves:
            item.start()
        make_copies(scaled_two, copies)
        for item in moves:
            item.wait()
        demodulate(full, rows_ref[1:2, :], demod)

    here = pl.ds(pl.multiple_of(j * TILE, TILE), TILE)
    live = gains[2]
    for phase in range(4):
        total = None
        for t in range(9):
            term = dot(full[t], copies[copy_index(phase, t // 3 - 1, t % 3 - 1), :, here])
            total = term if total is None else total + term
        convolved[phase] = total
        noise_row = gains[1] * noise[phase : phase + 1, here]

        @pl.loop(0, convolved.shape[1] // ROWS)
        def _(i):
            rows = pl.ds(pl.multiple_of(i * ROWS, ROWS), ROWS)
            pre = convolved[phase, rows, :] * wide(demod[rows, :]) + noise_row + wide(cols[4, rows, :])
            act = leaky_silu(pre)
            out = (act * live).astype(BF)
            for half in range(TILE // 128):
                ordered[half, rows, phase * 128 : (phase + 1) * 128] = out[:, half * 128 : (half + 1) * 128]
            for_rgb[rows, :] = (act * wide(cols[2, rows, :])).astype(BF)

        color[phase] = dot(rgb_rows[...], for_rgb[...])
    for half in range(TILE // 128):
        for k, out in enumerate((f0, f1, f2, f3)):
            rows = pl.ds(pl.multiple_of(jnp.bitwise_xor(me, k) * 128, 128), 128)
            out[:, half * 512 : (half + 1) * 512] = dot(ordered[half, rows, :], order[...]).astype(BF)


def cot_kernel(ids, gains, convolved, d0, d1, d2, d3, cols, demod, noise, order, color_cot, rgb_cols,
               cot_two, sums, rgb_grad, inner, fields, for_rgb):
    j = pl.program_id(0)
    me = ids[0]
    live = gains[2]

    @pl.when(j == 0)
    def _():
        sums[...] = jnp.zeros_like(sums)
        rgb_grad[...] = jnp.zeros_like(rgb_grad)

    for half in range(TILE // 128):
        for k, part in enumerate((d0, d1, d2, d3)):
            rows = pl.ds(pl.multiple_of(jnp.bitwise_xor(me, k) * 128, 128), 128)
            value = dot(part[:, half * 512 : (half + 1) * 512], order[...])
            for phase in range(4):
                fields[phase, rows, half * 128 : (half + 1) * 128] = value[:, phase * 128 : (phase + 1) * 128]

    here = pl.ds(pl.multiple_of(j * TILE, TILE), TILE)
    for phase in range(4):
        noise_plain = noise[phase : phase + 1, here]
        noise_row = gains[1] * noise_plain
        cot_here = color_cot[phase, :, here]

        @pl.loop(0, convolved.shape[1] // ROWS)
        def _(i):
            rows = pl.ds(pl.multiple_of(i * ROWS, ROWS), ROWS)
            conv = convolved[phase, rows, :]
            scale = wide(demod[rows, :])
            style = wide(cols[2, rows, :])
            pre = conv * scale + noise_row + wide(cols[4, rows, :])
            sigma = jax.nn.sigmoid(pre)
            act = root_two * (0.2 * pre + 0.8 * (pre * sigma))
            slope = root_two * (0.2 + 0.8 * sigma * (1.0 + pre * (1.0 - sigma)))
            back = dot(rgb_cols[rows, :], cot_here)
            grad = (fields[phase, rows, :] * live + back * style) * slope
            cot_two[phase, rows, :] = (grad * scale).astype(BF)
            for_rgb[rows, :] = (act * style).astype(BF)
            for n, value in enumerate((grad * conv, grad, grad * noise_plain, back * act)):
                sums[n, rows, :] += value[:, :128] + value[:, 128:]

        rgb_grad[...] += dot_nt(cot_here, for_rgb[...])

    @pl.when(j == pl.num_programs(0) - 1)
    def _():
        scale = demod[...]
        total = jnp.sum(sums[0], axis=1, keepdims=True)
        inner[...] = -0.5 * scale * scale * scale * total


def second_grad_kernel(ids, cot_two, scaled_two, full, inner, rows_ref, keep, send, copies, total):
    t = pl.program_id(0)
    me, core = ids[0], ids[1]

    @pl.when(t == 0)
    def _():
        make_copies(cot_two, copies)

    row_step, col_step = 1 - t // 3, 1 - t % 3
    summed = None
    for phase in range(4):
        a, b = phase // 2, phase % 2
        far_row = jnp.where(row_step == 2 * a - 1, 1, 0)
        far_col = jnp.where(col_step == 2 * b - 1, 1, 0)
        other_row = (a + row_step + 2) % 2
        other_col = (b + col_step + 2) % 2
        index = ((other_row * 2 + other_col) * 2 + far_row) * 2 + far_col
        term = dot_nt(copies[index], scaled_two[phase])
        summed = term if summed is None else summed + term
    total[...] = summed
    split_grad(me, core, total, full, t, inner, rows_ref[1:2, :], keep, send)


def split_grad(me, core, total, full, t, inner, square_row, keep, send):
    for k in range(4):
        base = jnp.bitwise_xor(me, k) * 128
        for out, part in ((keep, core), (send, 1 - core)):
            rows = pl.ds(pl.multiple_of(base + part * 64, 64), 64)
            column = jnp.concatenate([inner[rows, :]] * 4, axis=1)
            weight = full[t, rows, :].astype(F32)
            out[k, 0] = (total[rows, :] + (2.0 * weight) * (column * square_row)).astype(BF)


def second_back_kernel(ids, gains, cot_two, full, raised, cols, demod, noise,
                       cot_one, sums, inner, copies, turned, back):
    j = pl.program_id(0)

    @pl.when(j == 0)
    def _():
        sums[...] = jnp.zeros_like(sums)
        make_copies(cot_two, copies)

        @pl.loop(0, 9)
        def _(t):
            turned[t] = full[t].T

    here = pl.ds(pl.multiple_of(j * TILE, TILE), TILE)
    for phase in range(4):
        total = None
        for t in range(9):
            term = dot(turned[t], copies[copy_index(phase, 1 - t // 3, 1 - t % 3), :, here])
            total = term if total is None else total + term
        back[...] = total
        noise_plain = noise[phase : phase + 1, here]
        noise_row = gains[0] * noise_plain

        @pl.loop(0, back.shape[0] // ROWS)
        def _(i):
            rows = pl.ds(pl.multiple_of(i * ROWS, ROWS), ROWS)
            conv = raised[phase, rows, :]
            scale = wide(demod[rows, :])
            pre = conv * scale + noise_row + wide(cols[3, rows, :])
            sigma = jax.nn.sigmoid(pre)
            act = root_two * (0.2 * pre + 0.8 * (pre * sigma))
            slope = root_two * (0.2 + 0.8 * sigma * (1.0 + pre * (1.0 - sigma)))
            value = back[rows, :]
            grad = value * wide(cols[1, rows, :]) * slope
            cot_one[phase, rows, :] = (grad * scale).astype(BF)
            for n, item in enumerate((grad * conv, grad, grad * noise_plain, value * act)):
                sums[n, rows, :] += item[:, :128] + item[:, 128:]

    @pl.when(j == pl.num_programs(0) - 1)
    def _():
        scale = demod[...]
        total = jnp.sum(sums[0], axis=1, keepdims=True)
        inner[...] = -0.5 * scale * scale * scale * total


def first_kernel(ids, cot_one, scaled_one, full, inner, cols, rows_ref, x0, x1, x2, x3,
                 keep, send, b0, b1, b2, b3, sums, copies, total, back):
    t = pl.program_id(0)
    me, core = ids[0], ids[1]

    @pl.when(t == 0)
    def _():
        back[...] = jnp.zeros_like(back)

        @pl.loop(0, cot_one.shape[1] // 32)
        def _(i):
            rows = pl.ds(pl.multiple_of(i * 32, 32), 32)
            for phase, (row_phase, col_phase) in enumerate(phase_pairs):
                field = cot_one[phase, rows, :]
                for k, r in phase_taps[row_phase]:
                    for l, q in phase_taps[col_phase]:
                        copies[3 * k + l, rows, :] = move(field, -r, -q)

    total[...] = dot_nt(copies[t], scaled_one[...])
    split_grad(me, core, total, full, t, inner, rows_ref[0:1, :], keep, send)
    turned = full[t].T
    for n in range(back.shape[1] // TILE):
        here = slice(n * TILE, (n + 1) * TILE)
        back[:, here] += dot(turned, copies[t, :, here])

    @pl.when(t == pl.num_programs(0) - 1)
    def _():
        for k, (out, part) in enumerate(((b0, x0), (b1, x1), (b2, x2), (b3, x3))):
            base = jnp.bitwise_xor(me, k) * 128

            @pl.loop(0, 128 // 32)
            def _(i):
                rows = pl.ds(pl.multiple_of(base + i * 32, 32), 32)
                here = pl.ds(pl.multiple_of(i * 32, 32), 32)
                value = back[rows, :]
                style = jnp.concatenate([cols[0, rows, :]] * 8, axis=1)
                out[here, :] = (value * style).astype(out.dtype)
                sums[rows, :] = jnp.broadcast_to(
                    jnp.sum(value * part[here, :].astype(F32), axis=1, keepdims=True), (32, 128)
                )


def call(kernel, grid, ins, outs, scratch, args):
    return pl.pallas_call(
        kernel,
        grid=(grid,),
        in_specs=ins,
        out_specs=[spec for _, _, spec in outs],
        out_shape=[jax.ShapeDtypeStruct(shape, dtype) for shape, dtype, _ in outs],
        scratch_shapes=scratch,
        compiler_params=pltpu.CompilerParams(vmem_limit_bytes=LIMIT),
    )(*args)


def quad(value, k):
    return lax.ppermute(value, "chan", [(i, i ^ k) for i in range(4)])


def pair(value):
    return lax.ppermute(value, "dp", [(i, i ^ 1) for i in range(8)])


def after(value, *others):
    return lax.optimization_barrier((value,) + others)[0]


def natural(parts, me):
    stacked = jnp.stack(parts)
    stacked = stacked.reshape((2, 2) + stacked.shape[1:])
    stacked = jnp.where(me % 2 == 1, stacked[:, ::-1], stacked)
    stacked = jnp.where(me // 2 == 1, stacked[::-1], stacked)
    return stacked.reshape((4,) + stacked.shape[2:])


def pick(value, index, axis):
    return lax.dynamic_index_in_dim(value, index, axis, keepdims=False)


def to_phases(field):
    lead = field.shape[:-1]
    blocked = field.reshape(lead + (HALF, 2, HALF, 2))
    n = len(lead)
    return blocked.transpose((n + 1, n + 3) + tuple(range(n)) + (n, n + 2)).reshape((4,) + lead + (HALF * HALF,))


def phase_order():
    place = jnp.arange(512)
    row, col = place // SIDE, place % SIDE
    grouped = ((row % 2) * 2 + col % 2) * 128 + (row // 2) * HALF + col // 2
    return (jnp.arange(512)[:, None] == grouped[None, :]).astype(BF)


def image_body(
    feat_in,
    rgb_in,
    latent,
    noise_first,
    noise_second,
    live_count,
    conv_first,
    conv_second,
    style_weight,
    style_bias,
    rgb_weight,
    conv_bias,
    rgb_bias,
    noise_gain,
    feat_grad,
    rgb_grad,
):
    local_ch, images, half_pix = feat_in.shape
    channels = 4 * local_ch
    pixels = feat_grad.shape[2]
    me = lax.axis_index("chan")
    row = lax.axis_index("dp")
    core = row % 2
    depth = row // 2
    to = [jnp.bitwise_xor(me, k) for k in range(4)]
    live_mask = (jnp.arange(images) < live_count[0]).astype(F32)
    live = (me < live_count[0]).astype(F32)
    ids = jnp.stack([me, core]).astype(jnp.int32)
    gains = jnp.concatenate([noise_gain, live[None]])

    styles = jnp.einsum("bw,jwc->bjc", latent, style_weight, precision=precise) + style_bias[None]
    shared = jnp.concatenate([conv_bias, rgb_weight.astype(F32)])
    packs = [jnp.concatenate([pick(styles, to[k], 0), shared]) for k in range(4)]
    packs = [packs[0]] + [quad(packs[k], k) for k in (1, 2, 3)]
    vectors = natural(packs, me).transpose(1, 0, 2).reshape(8, channels)
    style_mine, bias_all, rgb_all = vectors[:3], vectors[3:5], vectors[5:8]
    cols = jnp.broadcast_to(vectors[:5, :, None], (5, channels, 128))
    squares = jnp.pad(style_mine[:2] * style_mine[:2], ((0, 6), (0, 0)))

    x = [pick(feat_in, to[k], 1) for k in range(4)]
    x = [x[0]] + [quad(x[k], k) for k in (1, 2, 3)]

    half_one = lax.dynamic_slice_in_dim(conv_first, core * 64, 64, 1)
    half_two = lax.dynamic_slice_in_dim(conv_second, core * 64, 64, 1)
    one_others = [quad(half_one, k) for k in (1, 2, 3)]
    one_swapped = [pair(part) for part in one_others]
    half_two = after(half_two, one_others[2])
    two_others = [quad(half_two, k) for k in (1, 2, 3)]
    two_swapped = [pair(part) for part in two_others]
    d = [pick(feat_grad, to[k], 1) for k in range(4)]
    d = [d[0]] + [quad(after(d[k], two_others[2]), k) for k in (1, 2, 3)]

    noise_one = to_phases(pick(noise_first, me, 0))
    noise_two = to_phases(pick(noise_second, me, 0))
    order = phase_order()
    cot_mine = (pick(rgb_grad, me, 0) * live).astype(BF)
    color_cot = jnp.pad(to_phases(cot_mine), ((0, 0), (0, 13), (0, 0)))
    rgb_rows = jnp.pad(rgb_all.astype(BF), ((0, 13), (0, 0)))
    rgb_cols = rgb_rows.T

    tiles = half_pix // TILE
    vec = ((channels, 128), F32, whole((channels, 128)))
    cols_spec, row_spec, noise_spec = whole(cols.shape), whole(squares.shape), whole(noise_one.shape)
    full_spec = whole((9, channels, channels))
    tile_spec = pl.BlockSpec((4, channels, TILE), lambda j: (0, 0, j))
    field_spec = whole((4, channels, half_pix))
    image_spec = pl.BlockSpec((local_ch, 4 * TILE), lambda j: (0, j))
    x_spec = whole((local_ch, half_pix))

    raised, scaled_two, full_one, scaled_one, demod_one = call(
        up_kernel,
        tiles,
        [SMEM, SMEM] + [x_spec] * 4 + [ANY] * 7 + [cols_spec, row_spec, noise_spec],
        [
            ((4, channels, half_pix), F32, tile_spec),
            ((4, channels, half_pix), BF, tile_spec),
            ((9, channels, channels), BF, full_spec),
            ((channels, half_pix), BF, whole((channels, half_pix))),
            vec,
        ],
        [pltpu.VMEM((4, channels, half_pix), BF), pltpu.SemaphoreType.DMA((7,))],
        (ids, gains, *x, conv_first, *one_others, *one_swapped, cols, squares, noise_one),
    )

    convolved, f0, f1, f2, f3, color, full_two, demod_two = call(
        conv_kernel,
        tiles,
        [SMEM, SMEM, field_spec] + [ANY] * 7
        + [cols_spec, row_spec, noise_spec, whole((512, 512)), whole((16, channels))],
        [((4, channels, half_pix), F32, tile_spec)]
        + [((local_ch, pixels), BF, image_spec)] * 4
        + [
            ((4, 16, half_pix), F32, pl.BlockSpec((4, 16, TILE), lambda j: (0, 0, j))),
            ((9, channels, channels), BF, full_spec),
            vec,
        ],
        [
            pltpu.VMEM((16, channels, half_pix), BF),
            pltpu.VMEM((TILE // 128, channels, 512), BF),
            pltpu.VMEM((channels, TILE), BF),
            pltpu.SemaphoreType.DMA((7,)),
        ],
        (ids, gains, scaled_two, conv_second, *two_others, *two_swapped, cols, squares, noise_two, order, rgb_rows),
    )

    cot_two, sums_two, rgb_part, inner_two = call(
        cot_kernel,
        tiles,
        [SMEM, SMEM, tile_spec] + [image_spec] * 4
        + [cols_spec, whole((channels, 128)), noise_spec, whole((512, 512)), whole((4, 16, half_pix)),
           whole((channels, 16))],
        [
            ((4, channels, half_pix), BF, tile_spec),
            ((4, channels, 128), F32, whole((4, channels, 128))),
            ((16, channels), F32, whole((16, channels))),
            vec,
        ],
        [pltpu.VMEM((4, channels, TILE), F32), pltpu.VMEM((channels, TILE), BF)],
        (ids, gains, convolved, *d, cols, demod_two, noise_two, order.T, color_cot, rgb_cols),
    )

    grad_spec = pl.BlockSpec((4, 1, 64, channels), lambda t: (0, t, 0, 0))
    grad_shape = ((4, 9, 64, channels), BF, grad_spec)
    keep_two, send_two = call(
        second_grad_kernel,
        9,
        [SMEM, field_spec, field_spec, full_spec, whole((channels, 128)), row_spec],
        [grad_shape, grad_shape],
        [pltpu.VMEM((16, channels, half_pix), BF), pltpu.VMEM((channels, channels), F32)],
        (ids, cot_two, scaled_two, full_two, inner_two, squares),
    )
    grad_two = reduce_grad(keep_two, send_two, me, depth)

    cot_one, sums_one, inner_one = call(
        second_back_kernel,
        tiles,
        [SMEM, SMEM, field_spec, full_spec, tile_spec, cols_spec, whole((channels, 128)), noise_spec],
        [
            ((4, channels, half_pix), BF, tile_spec),
            ((4, channels, 128), F32, whole((4, channels, 128))),
            vec,
        ],
        [
            pltpu.VMEM((16, channels, half_pix), BF),
            pltpu.VMEM((9, channels, channels), BF),
            pltpu.VMEM((channels, TILE), F32),
        ],
        (ids, gains, cot_two, full_two, raised, cols, demod_one, noise_one),
    )

    keep_one, send_one, b0, b1, b2, b3, sums_zero = call(
        first_kernel,
        9,
        [SMEM, field_spec, whole((channels, half_pix)), full_spec, whole((channels, 128)), cols_spec, row_spec]
        + [x_spec] * 4,
        [grad_shape, grad_shape] + [((local_ch, half_pix), BF, x_spec)] * 4 + [vec],
        [
            pltpu.VMEM((9, channels, half_pix), BF),
            pltpu.VMEM((channels, channels), F32),
            pltpu.VMEM((channels, half_pix), F32),
        ],
        (ids, cot_one, scaled_one, full_one, inner_one, cols, squares, *x),
    )
    grad_one = reduce_grad(keep_one, send_one, me, depth)

    feat_out = [f0] + [quad(after(part, d[3]), k + 1) for k, part in enumerate((f1, f2, f3))]
    feat_out = natural(feat_out, me).transpose(1, 0, 2)
    back = [b0] + [quad(part, k + 1) for k, part in enumerate((b1, b2, b3))]
    feat_in_grad = natural(back, me).transpose(1, 0, 2).astype(F32)

    lift_matrix = upsample_matrix(HALF)
    color = color[:, :3].reshape(2, 2, 3, HALF, HALF).transpose(2, 3, 0, 4, 1).reshape(3, pixels)
    shard_pix = pixels // 4
    color = color.reshape(3, 4, shard_pix)
    color = [pick(color, to[k], 1) for k in range(4)]
    color = natural([color[0]] + [quad(color[k], k) for k in (1, 2, 3)], me)
    skip_up = jnp.einsum(
        "up,bkpq,vq->bkuv",
        lift_matrix,
        rgb_in.reshape(images, 3, HALF, HALF),
        lift_matrix,
        precision=precise,
    ).reshape(images, 3, pixels)
    skip_mine = lax.dynamic_slice_in_dim(skip_up, me * shard_pix, shard_pix, 2)
    rgb_out = (color + rgb_bias[None, :, None] + skip_mine) * live_mask[:, None, None]
    rgb_cot = rgb_grad * live_mask[:, None, None]
    rgb_in_grad = jnp.einsum(
        "up,bkuv,vq->bkpq",
        lift_matrix,
        rgb_cot.reshape(images, 3, SIDE, SIDE),
        lift_matrix,
        precision=precise,
    ).reshape(images, 3, half_pix)
    rgb_bias_part = jnp.sum(rgb_cot, axis=(0, 2))

    sums_two = jnp.sum(sums_two, axis=2)
    sums_one = jnp.sum(sums_one, axis=2)
    inner_two, inner_one = inner_two[:, 0], inner_one[:, 0]
    style_two_demod = 2.0 * style_mine[1] * square_back(inner_two, full_two)
    style_one_demod = 2.0 * style_mine[0] * square_back(inner_one, full_one)
    rows_out = jnp.stack(
        [
            sums_zero[:, 0] + style_one_demod,
            sums_one[3] + style_two_demod,
            sums_two[3],
            sums_one[1],
            sums_two[1],
            sums_one[2],
            sums_two[2],
        ]
    )
    rows_out = jnp.concatenate([rows_out, rgb_part[:3]]).reshape(10, 4, local_ch)
    rows_out = [pick(rows_out, to[k], 1) for k in range(4)]
    rows_in = natural([rows_out[0]] + [quad(rows_out[k], k) for k in (1, 2, 3)], me)
    style_grads = rows_in[:, :3]
    latent_part = jnp.einsum("bjc,jwc->bw", style_grads, style_weight, precision=precise)
    latent_grad = latent_part + quad(latent_part, 1) + quad(latent_part, 2) + quad(latent_part, 3)
    extra = jnp.pad(rgb_bias_part[None], ((0, 0), (0, local_ch - 3)))
    gathered = jnp.concatenate([rows_in.reshape(40, local_ch), extra, latent.reshape(16, 128)])
    gathered = lax.all_gather(gathered, "dp")
    every_row = gathered[:, :40].reshape(8, 4, 10, local_ch)
    every_latent = gathered[:, 41:].reshape(8, 4, 512)
    style_weight_grad = jnp.einsum("gbw,gbjc->jwc", every_latent, every_row[:, :, :3], precision=precise)
    summed = jnp.sum(every_row, axis=(0, 1))
    gain_part = jnp.sum(summed[5:7], axis=1)
    gain_grad = lax.psum(gain_part, "chan")
    rgb_bias_grad = jnp.sum(gathered[:, 40, :3], axis=0)
    return (
        feat_out,
        rgb_out,
        feat_in_grad,
        rgb_in_grad,
        latent_grad,
        grad_one,
        grad_two,
        style_weight_grad,
        summed[:3],
        summed[7:10],
        summed[3:5],
        rgb_bias_grad,
        gain_grad,
    )


def square_back(inner, full):
    total = jnp.zeros(full.shape[1:], F32)
    for t in range(9):
        value = full[t].astype(F32)
        total = total + value * value
    return jnp.sum(inner[:, None] * total, axis=0)


def reduce_grad(keep, send, me, depth):
    part = (keep.astype(F32) + pair(send).astype(F32)).astype(BF)
    total = part[0].astype(F32)
    for k in (1, 2, 3):
        total = total + quad(part[k], k).astype(F32)
    block = total.astype(BF).reshape(9, 4, 16, 512)

    def along(value, k):
        return lax.ppermute(value, "dp", [(i, i ^ (2 * k)) for i in range(8)])

    summed = pick(block, depth, 1).astype(F32)
    for k in (1, 2, 3):
        summed = summed + along(pick(block, jnp.bitwise_xor(depth, k), 1), k).astype(F32)
    summed = summed.astype(BF)
    spread = natural([summed] + [along(summed, k) for k in (1, 2, 3)], depth)
    mine = spread.transpose(1, 0, 2, 3).reshape(9, 64, 512)
    theirs = pair(mine)
    core = lax.axis_index("dp") % 2
    low = jnp.where(core == 0, mine, theirs)
    high = jnp.where(core == 0, theirs, mine)
    return jnp.concatenate([low, high], axis=1).astype(F32)


def solution(mesh):
    alone = mesh.shape["chan"] == 4 and mesh.shape["dp"] == 8
    return jax.shard_map(
        image_body if alone else body,
        mesh=mesh,
        in_specs=(
            P("chan", "dp", None),
            P("dp", None, None),
            P("dp", None),
            P("dp", None),
            P("dp", None),
            P("dp"),
            P(None, "chan", None),
            P(None, "chan", None),
            P(None, None, "chan"),
            P(None, "chan"),
            P(None, "chan"),
            P(None, "chan"),
            P(),
            P(),
            P("chan", "dp", None),
            P("dp", None, None),
        ),
        out_specs=(
            P("chan", "dp", None),
            P("dp", None, "chan"),
            P("chan", "dp", None),
            P("dp", None, None),
            P("dp", None),
            P(None, "chan", None),
            P(None, "chan", None),
            P(None, None, "chan"),
            P(None, "chan"),
            P(None, "chan"),
            P(None, "chan"),
            P(),
            P(),
        ),
        check_vma=False,
    )
```

```python
import functools

import jax
import jax.numpy as jnp
from jax import lax
from jax.experimental import pallas as pl
from jax.experimental.pallas import tpu as pltpu
from jax.sharding import PartitionSpec as P

SIDE = 64
HALF = 32


precise = lax.Precision.HIGHEST
epsilon = 1e-08
root_two = 1.4142135623730951
phase_taps = (((1, 0),), ((2, 0), (0, 1)))
phase_pairs = ((0, 0), (0, 1), (1, 0), (1, 1))


def leaky_silu(value):
    return root_two * (0.2 * value + 0.8 * jax.nn.silu(value))


def leaky_slope(value):
    sigma = jax.nn.sigmoid(value)
    return root_two * (0.2 + 0.8 * sigma * (1.0 + value * (1.0 - sigma)))


def shifted(field, row_shift, col_shift, width):
    cells = field.shape[-1]
    offset = row_shift * width + col_shift
    if offset > 0:
        result = jnp.concatenate(
            [field[..., offset:], jnp.zeros(field.shape[:-1] + (offset,), field.dtype)], axis=-1
        )
    elif offset < 0:
        result = jnp.concatenate(
            [jnp.zeros(field.shape[:-1] + (-offset,), field.dtype), field[..., : cells + offset]],
            axis=-1,
        )
    else:
        result = field
    if col_shift != 0:
        column = jnp.arange(cells) % width
        inside = (column + col_shift >= 0) & (column + col_shift < width)
        result = jnp.where(inside, result, jnp.zeros((), field.dtype))
    return result


def upsample_matrix(half_side):
    rows_out = jnp.arange(2 * half_side)[:, None]
    cols_in = jnp.arange(half_side)[None, :]
    centre = rows_out // 2
    beside = centre - 1 + 2 * (rows_out % 2)
    return (
        jnp.where(cols_in == centre, 0.75, 0.0) + jnp.where(cols_in == beside, 0.25, 0.0)
    ).astype(jnp.float32)


def alternate(phases, half_side):
    stacked = jnp.stack(phases)
    out_rows, batch_count = (stacked.shape[1], stacked.shape[2])
    blocked = stacked.reshape(2, 2, out_rows, batch_count, half_side, half_side)
    return blocked.transpose(2, 3, 4, 0, 5, 1).reshape(
        out_rows, batch_count, 4 * half_side * half_side
    )


def split_phases(field, half_side):
    out_rows, batch_count = (field.shape[0], field.shape[1])
    blocked = field.reshape(out_rows, batch_count, half_side, 2, half_side, 2)
    return [
        blocked[:, :, :, row_phase, :, col_phase].reshape(
            out_rows, batch_count, half_side * half_side
        )
        for row_phase, col_phase in phase_pairs
    ]


def up_conv(inputs, weight, half_side):
    shifted_inputs = {}
    for row_shift in (0, 1):
        for col_shift in (0, 1):
            shifted_inputs[row_shift, col_shift] = shifted(inputs, row_shift, col_shift, half_side)
    phases = []
    for row_phase, col_phase in phase_pairs:
        summed = None
        for row_tap, row_shift in phase_taps[row_phase]:
            for col_tap, col_shift in phase_taps[col_phase]:
                product = jnp.einsum(
                    "oc,cbp->obp",
                    weight[row_tap * 3 + col_tap],
                    shifted_inputs[row_shift, col_shift],
                    preferred_element_type=jnp.float32,
                )
                summed = product if summed is None else summed + product
        phases.append(summed)
    return alternate(phases, half_side)


def phase_grads(grad_field, half_side):
    grad_phases = split_phases(grad_field, half_side)
    shifted_grads = [None] * 9
    for phase_index in range(4):
        row_phase, col_phase = phase_pairs[phase_index]
        for row_tap, row_shift in phase_taps[row_phase]:
            for col_tap, col_shift in phase_taps[col_phase]:
                shifted_grads[row_tap * 3 + col_tap] = shifted(
                    grad_phases[phase_index], -row_shift, -col_shift, half_side
                )
    return shifted_grads


def flat_conv(inputs, weight, width):
    summed = None
    for tap_index in range(9):
        product = jnp.einsum(
            "oc,cbp->obp", weight[tap_index], inputs, preferred_element_type=jnp.float32
        )
        product = shifted(product, tap_index // 3 - 1, tap_index % 3 - 1, width)
        summed = product if summed is None else summed + product
    return summed


def body(
    feat_in,
    rgb_in,
    latent,
    noise_first,
    noise_second,
    live_count,
    conv_first,
    conv_second,
    style_weight,
    style_bias,
    rgb_weight,
    conv_bias,
    rgb_bias,
    noise_gain,
    feat_grad,
    rgb_grad,
):
    local_ch, images, half_pix = feat_in.shape
    pixels = feat_grad.shape[2]
    half_side = HALF
    full_side = SIDE
    chan_rank = lax.axis_index("chan")
    live_mask = (jnp.arange(images) < live_count[0]).astype(jnp.float32)
    styles = (
        jnp.einsum("bw,jwc->jbc", latent, style_weight, precision=precise) + style_bias[:, None, :]
    )
    first_all, second_all = (
        lax.all_gather(styles[0], "chan", axis=1, tiled=True),
        lax.all_gather(styles[1], "chan", axis=1, tiled=True),
    )
    weight_one = conv_first.astype(jnp.float32)
    weight_two = conv_second.astype(jnp.float32)
    squares_one = jnp.sum(weight_one * weight_one, axis=0)
    squares_two = jnp.sum(weight_two * weight_two, axis=0)
    demod_one = lax.rsqrt(
        jnp.dot(first_all * first_all, squares_one.T, precision=precise) + epsilon
    )
    demod_two = lax.rsqrt(
        jnp.dot(second_all * second_all, squares_two.T, precision=precise) + epsilon
    )
    scaled_one = (feat_in.astype(jnp.float32) * styles[0].T[:, :, None]).astype(jnp.bfloat16)
    gathered_one = lax.all_gather(scaled_one, "chan", axis=0, tiled=True)
    raised = up_conv(gathered_one, conv_first, half_side)
    pre_one = (
        raised * demod_one.T[:, :, None]
        + noise_gain[0] * noise_first[None, :, :]
        + conv_bias[0][:, None, None]
    )
    act_one = leaky_silu(pre_one)
    scaled_two = (act_one * styles[1].T[:, :, None]).astype(jnp.bfloat16)
    gathered_two = lax.all_gather(scaled_two, "chan", axis=0, tiled=True)
    convolved = flat_conv(gathered_two, conv_second, full_side)
    pre_two = (
        convolved * demod_two.T[:, :, None]
        + noise_gain[1] * noise_second[None, :, :]
        + conv_bias[1][:, None, None]
    )
    act_two = leaky_silu(pre_two)
    feat_out = (act_two * live_mask[None, :, None]).astype(jnp.bfloat16)
    scaled_rgb = (act_two * styles[2].T[:, :, None]).astype(jnp.bfloat16)
    color_part = jnp.einsum(
        "ko,obp->bkp", rgb_weight, scaled_rgb, preferred_element_type=jnp.float32
    )
    color = lax.psum_scatter(color_part, "chan", scatter_dimension=2, tiled=True)
    shard_pix = color.shape[2]
    lift_matrix = upsample_matrix(half_side)
    skip_up = jnp.einsum(
        "up,bkpq,vq->bkuv",
        lift_matrix,
        rgb_in.reshape(images, 3, half_side, half_side),
        lift_matrix,
        precision=precise,
    ).reshape(images, 3, pixels)
    skip_mine = lax.dynamic_slice_in_dim(skip_up, chan_rank * shard_pix, shard_pix, 2)
    rgb_out = (color + rgb_bias[None, :, None] + skip_mine) * live_mask[:, None, None]
    rgb_cot = rgb_grad * live_mask[:, None, None]
    color_cot = rgb_cot.astype(jnp.bfloat16)
    rgb_in_grad = jnp.einsum(
        "up,bkuv,vq->bkpq",
        lift_matrix,
        rgb_cot.reshape(images, 3, full_side, full_side),
        lift_matrix,
        precision=precise,
    ).reshape(images, 3, half_pix)
    rgb_bias_part = jnp.sum(rgb_cot, axis=(0, 2))
    rgb_weight_part = jnp.einsum(
        "bkp,obp->ko", color_cot, scaled_rgb, preferred_element_type=jnp.float32
    )
    back_rgb = jnp.einsum("ko,bkp->obp", rgb_weight, color_cot, preferred_element_type=jnp.float32)
    style_rgb_grad = jnp.sum(back_rgb * act_two, axis=2).T
    grad_pre_two = (
        feat_grad.astype(jnp.float32) * live_mask[None, :, None]
        + back_rgb * styles[2].T[:, :, None]
    ) * leaky_slope(pre_two)
    cot_two = (grad_pre_two * demod_two.T[:, :, None]).astype(jnp.bfloat16)
    inner_two = (
        -0.5 * demod_two * demod_two * demod_two * jnp.sum(grad_pre_two * convolved, axis=2).T
    )
    taps_two = jnp.stack(
        [
            shifted(cot_two, 1 - tap_index // 3, 1 - tap_index % 3, full_side)
            for tap_index in range(9)
        ]
    )
    squares_two_grad = jnp.dot(inner_two.T, second_all * second_all, precision=precise)
    conv_two_grad = (
        jnp.einsum("tobp,cbp->toc", taps_two, gathered_two, preferred_element_type=jnp.float32)
        + 2.0 * weight_two * squares_two_grad[None]
    )
    style_two_demod = 2.0 * second_all * jnp.dot(inner_two, squares_two, precision=precise)
    columns = conv_second
    back_two = lax.psum_scatter(
        jnp.einsum("toc,tobp->cbp", columns, taps_two, preferred_element_type=jnp.float32),
        "chan",
        scatter_dimension=0,
        tiled=True,
    )
    style_two_conv = jnp.sum(back_two * act_one, axis=2).T
    grad_pre_one = back_two * styles[1].T[:, :, None] * leaky_slope(pre_one)
    cot_one = (grad_pre_one * demod_one.T[:, :, None]).astype(jnp.bfloat16)
    inner_one = -0.5 * demod_one * demod_one * demod_one * jnp.sum(grad_pre_one * raised, axis=2).T
    taps_one = jnp.stack(phase_grads(cot_one, half_side))
    squares_one_grad = jnp.dot(inner_one.T, first_all * first_all, precision=precise)
    conv_one_grad = (
        jnp.einsum("tobp,cbp->toc", taps_one, gathered_one, preferred_element_type=jnp.float32)
        + 2.0 * weight_one * squares_one_grad[None]
    )
    style_one_demod = 2.0 * first_all * jnp.dot(inner_one, squares_one, precision=precise)
    columns = conv_first
    back_one = lax.psum_scatter(
        jnp.einsum("toc,tobp->cbp", columns, taps_one, preferred_element_type=jnp.float32),
        "chan",
        scatter_dimension=0,
        tiled=True,
    )
    feat_in_grad = back_one * styles[0].T[:, :, None]
    style_one_conv = jnp.sum(back_one * feat_in.astype(jnp.float32), axis=2).T
    demod_one_sum, demod_two_sum = (
        lax.psum_scatter(style_one_demod, "chan", scatter_dimension=1, tiled=True),
        lax.psum_scatter(style_two_demod, "chan", scatter_dimension=1, tiled=True),
    )
    style_grads = jnp.stack(
        [style_one_conv + demod_one_sum, style_two_conv + demod_two_sum, style_rgb_grad]
    )
    latent_part = jnp.einsum("jbc,jwc->bw", style_grads, style_weight, precision=precise)
    gain_part = jnp.stack(
        [
            jnp.sum(grad_pre_one * noise_first[None, :, :]),
            jnp.sum(grad_pre_two * noise_second[None, :, :]),
        ]
    )
    latent_grad, gain_chan = lax.psum((latent_part, gain_part), "chan")
    style_weight_part = jnp.einsum("bw,jbc->jwc", latent, style_grads, precision=precise)
    style_bias_part = jnp.sum(style_grads, axis=1)
    conv_bias_part = jnp.stack(
        [jnp.sum(grad_pre_one, axis=(1, 2)), jnp.sum(grad_pre_two, axis=(1, 2))]
    )
    totals = lax.psum(
        (
            conv_one_grad,
            conv_two_grad,
            style_weight_part,
            style_bias_part,
            rgb_weight_part,
            conv_bias_part,
            rgb_bias_part,
            gain_chan,
        ),
        "dp",
    )
    return (feat_out, rgb_out, feat_in_grad, rgb_in_grad, latent_grad) + tuple(totals)


BF = jnp.bfloat16
F32 = jnp.float32
TILE = 256
ROWS = 16
ANY = pl.BlockSpec(memory_space=pl.ANY)
SMEM = pl.BlockSpec(memory_space=pltpu.SMEM)
LIMIT = 56 * 1024 * 1024


def whole(shape):
    return pl.BlockSpec(shape, lambda j: (0,) * len(shape))


def dot(a, b):
    return jnp.dot(a, b, preferred_element_type=F32)


def dot_nt(a, b):
    return lax.dot_general(a, b, (((1,), (1,)), ((), ())), preferred_element_type=F32)


def wide(column):
    return jnp.concatenate([column] * (TILE // 128), axis=1)


def move(field, row_shift, col_shift):
    offset = row_shift * HALF + col_shift
    if offset == 0:
        return field
    cells = field.shape[1]
    lane = lax.broadcasted_iota(jnp.int32, field.shape, 1)
    row, col = lane // HALF, lane % HALF
    inside = (row + row_shift >= 0) & (row + row_shift < HALF)
    inside = inside & (col + col_shift >= 0) & (col + col_shift < HALF)
    rolled = pltpu.roll(field.astype(F32), (-offset) % cells, 1)
    return jnp.where(inside, rolled, 0.0).astype(field.dtype)


def near(parity, step):
    other = (parity + step) % 2
    return other, (parity + step - other) // 2


def copy_index(phase, row_step, col_step):
    a, r = near(phase // 2, row_step)
    b, q = near(phase % 2, col_step)
    return ((a * 2 + b) * 2 + abs(r)) * 2 + abs(q)


def make_copies(source, copies):
    chunk = 32

    @pl.loop(0, source.shape[1] // chunk)
    def _(i):
        rows = pl.ds(pl.multiple_of(i * chunk, chunk), chunk)
        for phase in range(4):
            field = source[phase, rows, :]
            row_sign = 1 if phase // 2 == 0 else -1
            col_sign = 1 if phase % 2 == 0 else -1
            for r in (0, 1):
                for q in (0, 1):
                    copies[(phase * 2 + r) * 2 + q, rows, :] = move(
                        field, row_sign * r, col_sign * q
                    )


def demodulate(full, square_row, demod):
    chunk = 32

    @pl.loop(0, full.shape[1] // chunk)
    def _(i):
        rows = pl.ds(pl.multiple_of(i * chunk, chunk), chunk)
        total = None
        for t in range(9):
            value = full[t, rows, :].astype(F32)
            total = value * value if total is None else total + value * value
        total = jnp.sum(total * square_row, axis=1, keepdims=True)
        demod[rows, :] = jnp.broadcast_to(lax.rsqrt(total + epsilon), (chunk, 128))


def chan_peer(me, k):
    if k == 1:
        return me + 1 - 2 * (me % 2)
    return (me + 2) % 4 if k == 2 else 3 - me


def rows_of(base, size):
    return pl.ds(pl.multiple_of(base, size), size)


def forward_kernel(gains, x0, x1, x2, x3, own1, g1, g2, g3, s1, s2, s3, own2, feat_grad,
                   cols, rows_ref, noise1, noise2, order, rgb_rows,
                   raised_out, scaled_out, conv_out, feat_out, full1_out, full2_out, grad_out,
                   scaled_one, demod1, demod2, color,
                   raised, scaled, full1, full2, copies, conv_tile, feat_tile, ordered,
                   load_sem, store_sem, tile_sem, send_sem, recv_sem, swap_send, swap_recv, grad_send, grad_recv):
    me = lax.axis_index("chan")
    row = lax.axis_index("dp")
    core = row % 2
    twin = row + 1 - 2 * core
    barrier = pltpu.get_barrier_semaphore()
    for k in (1, 2, 3):
        pl.semaphore_signal(barrier, inc=1, device_id={"chan": chan_peer(me, k)}, device_id_type=pl.DeviceIdType.MESH)
    pl.semaphore_signal(barrier, inc=1, device_id={"dp": twin}, device_id_type=pl.DeviceIdType.MESH)
    pl.semaphore_wait(barrier, 4)

    mine = rows_of(me * 128 + core * 64, 64)
    weight_moves = [
        pltpu.make_async_remote_copy(
            own2.at[:, rows_of(core * 64, 64), :], full2.at[:, mine, :], send_sem.at[k - 1], recv_sem.at[k - 1],
            device_id={"chan": chan_peer(me, k)}, device_id_type=pl.DeviceIdType.MESH,
        )
        for k in (1, 2, 3)
    ]
    for item in weight_moves:
        item.start()
    swap_moves = []
    for k in (1, 2, 3):
        part = rows_of(chan_peer(me, k) * 128 + core * 64, 64)
        swap_moves.append(
            pltpu.make_async_remote_copy(
                full2.at[:, part, :], full2.at[:, part, :], swap_send.at[k - 1], swap_recv.at[k - 1],
                device_id={"dp": twin}, device_id_type=pl.DeviceIdType.MESH,
            )
        )
    local2 = pltpu.make_async_copy(own2, full2.at[:, rows_of(me * 128, 128), :], load_sem.at[7])
    local2.start()
    loads = [pltpu.make_async_copy(own1, full1.at[:, rows_of(me * 128, 128), :], load_sem.at[0])]
    for k, (same, other) in enumerate(((g1, s1), (g2, s2), (g3, s3))):
        base = chan_peer(me, k + 1) * 128
        loads.append(pltpu.make_async_copy(same, full1.at[:, rows_of(base + core * 64, 64), :], load_sem.at[1 + k]))
        loads.append(pltpu.make_async_copy(other, full1.at[:, rows_of(base + 64 - core * 64, 64), :], load_sem.at[4 + k]))
    for item in loads:
        item.start()

    for k, part in enumerate((x0, x1, x2, x3)):
        base = me * 128 if k == 0 else chan_peer(me, k) * 128

        @pl.loop(0, 128 // 32)
        def _(i):
            rows = rows_of(base + i * 32, 32)
            style = jnp.concatenate([cols[0, rows, :]] * 8, axis=1)
            value = (part[rows_of(i * 32, 32), :].astype(F32) * style).astype(BF)
            scaled_one[rows, :] = value
            for r in (0, 1):
                for q in (0, 1):
                    copies[2 * r + q, rows, :] = move(value, r, q)

    for item in loads:
        item.wait()
    store1 = pltpu.make_async_copy(full1, full1_out, store_sem.at[0])
    store1.start()
    demodulate(full1, rows_ref[0:1, :], demod1)

    @pl.loop(0, raised.shape[2] // TILE)
    def _(j):
        here = rows_of(j * TILE, TILE)
        for phase, (row_phase, col_phase) in enumerate(phase_pairs):
            total = None
            for k, r in phase_taps[row_phase]:
                for l, q in phase_taps[col_phase]:
                    term = dot(full1[3 * k + l], copies[2 * r + q, :, here])
                    total = term if total is None else total + term
            raised[phase, :, here] = total
            noise_row = gains[0] * noise1[phase : phase + 1, here]
            for i in range(raised.shape[1] // ROWS):
                rows = slice(i * ROWS, (i + 1) * ROWS)
                pre = raised[phase, rows, here] * wide(demod1[rows, :]) + noise_row + wide(cols[3, rows, :])
                act = pre * (0.6 * root_two + 0.4 * root_two * jnp.tanh(0.5 * pre))
                scaled[phase, rows, here] = (act * wide(cols[1, rows, :])).astype(BF)

    stores = [
        pltpu.make_async_copy(raised, raised_out, store_sem.at[1]),
        pltpu.make_async_copy(scaled, scaled_out, store_sem.at[2]),
    ]
    for item in stores:
        item.start()
    make_copies(scaled, copies)
    for item, swap in zip(weight_moves, swap_moves):
        item.wait_recv()
        swap.start()
    grad_moves = [
        pltpu.make_async_remote_copy(
            feat_grad.at[chan_peer(me, k)], grad_out.at[rows_of(me * 128, 128), :], grad_send.at[k - 1], grad_recv.at[k - 1],
            device_id={"chan": chan_peer(me, k)}, device_id_type=pl.DeviceIdType.MESH,
        )
        for k in (1, 2, 3)
    ]
    for item in grad_moves:
        item.start()
    local3 = pltpu.make_async_copy(feat_grad.at[me], grad_out.at[rows_of(me * 128, 128), :], store_sem.at[4])
    local3.start()
    local2.wait()
    for swap in swap_moves:
        swap.wait_recv()
    store2 = pltpu.make_async_copy(full2, full2_out, store_sem.at[3])
    store2.start()
    demodulate(full2, rows_ref[1:2, :], demod2)
    live = gains[2]

    def tile_stores(j, slot):
        return (
            pltpu.make_async_copy(conv_tile.at[slot], conv_out.at[:, :, rows_of(j * TILE, TILE)], tile_sem.at[0, slot]),
            pltpu.make_async_copy(feat_tile.at[slot], feat_out.at[:, rows_of(j * 4 * TILE, 4 * TILE)], tile_sem.at[1, slot]),
        )

    @pl.loop(0, raised.shape[2] // TILE)
    def _(j):
        here = rows_of(j * TILE, TILE)
        slot = j % 2

        @pl.when(j >= 2)
        def _():
            for item in tile_stores(j - 2, slot):
                item.wait()

        for phase in range(4):
            total = None
            for t in range(9):
                term = dot(full2[t], copies[copy_index(phase, t // 3 - 1, t % 3 - 1), :, here])
                total = term if total is None else total + term
            conv_tile[slot, phase] = total
            noise_row = gains[1] * noise2[phase : phase + 1, here]
            for i in range(raised.shape[1] // ROWS):
                rows = slice(i * ROWS, (i + 1) * ROWS)
                pre = conv_tile[slot, phase, rows, :] * wide(demod2[rows, :]) + noise_row + wide(cols[4, rows, :])
                act = pre * (0.6 * root_two + 0.4 * root_two * jnp.tanh(0.5 * pre))
                out = (act * live).astype(BF)
                for half in range(TILE // 128):
                    ordered[half, rows, phase * 128 : (phase + 1) * 128] = out[:, half * 128 : (half + 1) * 128]
        for half in range(TILE // 128):
            image = dot(ordered[half], order[...]).astype(BF)
            feat_tile[slot, :, half * 512 : (half + 1) * 512] = image
            color[:, rows_of(j * 4 * TILE + half * 512, 512)] = dot(rgb_rows[...], image)
        for item in tile_stores(j, slot):
            item.start()

    for j in (2, 3):
        for item in tile_stores(j, j % 2):
            item.wait()
    for item in [store1, store2, local3] + stores:
        item.wait()
    for item in weight_moves + swap_moves:
        item.wait_send()
    for item in grad_moves:
        item.wait()


def cot_kernel(gains, convolved, arrived, cols, demod, noise, order, color_cot, rgb_cols,
               cot_two, sums, rgb_grad, inner, fields, for_rgb):
    j = pl.program_id(0)
    live = gains[2]

    @pl.when(j == 0)
    def _():
        sums[...] = jnp.zeros_like(sums)
        rgb_grad[...] = jnp.zeros_like(rgb_grad)

    for half in range(TILE // 128):
        value = dot(arrived[:, half * 512 : (half + 1) * 512], order[...])
        for phase in range(4):
            fields[phase, :, half * 128 : (half + 1) * 128] = value[:, phase * 128 : (phase + 1) * 128]

    here = pl.ds(pl.multiple_of(j * TILE, TILE), TILE)
    for phase in range(4):
        noise_plain = noise[phase : phase + 1, here]
        noise_row = gains[1] * noise_plain
        cot_here = color_cot[phase, :, here]

        for i in range(convolved.shape[1] // ROWS):
            rows = slice(i * ROWS, (i + 1) * ROWS)
            conv = convolved[phase, rows, :]
            scale = wide(demod[rows, :])
            style = wide(cols[2, rows, :])
            pre = conv * scale + noise_row + wide(cols[4, rows, :])
            sigma = 0.5 + 0.5 * jnp.tanh(0.5 * pre)
            act = root_two * (0.2 * pre + 0.8 * (pre * sigma))
            slope = root_two * (0.2 + 0.8 * sigma * (1.0 + pre * (1.0 - sigma)))
            back = dot(rgb_cols[rows, :], cot_here)
            grad = (fields[phase, rows, :] * live + back * style) * slope
            cot_two[phase, rows, :] = (grad * scale).astype(BF)
            for_rgb[rows, :] = (act * style).astype(BF)
            for n, value in enumerate((grad * conv, grad, grad * noise_plain, back * act)):
                sums[n, rows, :] += value[:, :128] + value[:, 128:]

        rgb_grad[...] += dot_nt(cot_here, for_rgb[...])

    @pl.when(j == pl.num_programs(0) - 1)
    def _():
        scale = demod[...]
        total = jnp.sum(sums[0], axis=1, keepdims=True)
        inner[...] = -0.5 * scale * scale * scale * total


def second_grad_kernel(ids, cot_two, scaled_two, full, inner, rows_ref, keep, send, copies, total):
    t = pl.program_id(0)
    me, core = ids[0], ids[1]

    @pl.when(t == 0)
    def _():
        make_copies(cot_two, copies)

    row_step, col_step = 1 - t // 3, 1 - t % 3
    summed = None
    for phase in range(4):
        a, b = phase // 2, phase % 2
        far_row = jnp.where(row_step == 2 * a - 1, 1, 0)
        far_col = jnp.where(col_step == 2 * b - 1, 1, 0)
        other_row = (a + row_step + 2) % 2
        other_col = (b + col_step + 2) % 2
        index = ((other_row * 2 + other_col) * 2 + far_row) * 2 + far_col
        term = dot_nt(copies[index], scaled_two[phase])
        summed = term if summed is None else summed + term
    total[...] = summed
    split_grad(me, core, total, full, t, inner, rows_ref[1:2, :], keep, send)


def split_grad(me, core, total, full, t, inner, square_row, keep, send):
    for k in range(4):
        base = jnp.bitwise_xor(me, k) * 128
        for out, part in ((keep, core), (send, 1 - core)):
            rows = pl.ds(pl.multiple_of(base + part * 64, 64), 64)
            column = jnp.concatenate([inner[rows, :]] * 4, axis=1)
            weight = full[t, rows, :].astype(F32)
            out[k, 0] = (total[rows, :] + (2.0 * weight) * (column * square_row)).astype(BF)


def second_back_kernel(ids, gains, cot_two, full, raised, cols, demod, noise,
                       cot_one, sums, inner, copies, turned, back):
    j = pl.program_id(0)

    @pl.when(j == 0)
    def _():
        sums[...] = jnp.zeros_like(sums)
        make_copies(cot_two, copies)

        @pl.loop(0, 9)
        def _(t):
            turned[t] = full[t].T

    here = pl.ds(pl.multiple_of(j * TILE, TILE), TILE)
    for phase in range(4):
        total = None
        for t in range(9):
            term = dot(turned[t], copies[copy_index(phase, 1 - t // 3, 1 - t % 3), :, here])
            total = term if total is None else total + term
        back[...] = total
        noise_plain = noise[phase : phase + 1, here]
        noise_row = gains[0] * noise_plain

        for i in range(back.shape[0] // ROWS):
            rows = slice(i * ROWS, (i + 1) * ROWS)
            conv = raised[phase, rows, :]
            scale = wide(demod[rows, :])
            pre = conv * scale + noise_row + wide(cols[3, rows, :])
            sigma = 0.5 + 0.5 * jnp.tanh(0.5 * pre)
            act = root_two * (0.2 * pre + 0.8 * (pre * sigma))
            slope = root_two * (0.2 + 0.8 * sigma * (1.0 + pre * (1.0 - sigma)))
            value = back[rows, :]
            grad = value * wide(cols[1, rows, :]) * slope
            cot_one[phase, rows, :] = (grad * scale).astype(BF)
            for n, item in enumerate((grad * conv, grad, grad * noise_plain, value * act)):
                sums[n, rows, :] += item[:, :128] + item[:, 128:]

    @pl.when(j == pl.num_programs(0) - 1)
    def _():
        scale = demod[...]
        total = jnp.sum(sums[0], axis=1, keepdims=True)
        inner[...] = -0.5 * scale * scale * scale * total


def first_kernel(ids, cot_one, scaled_one, full, inner, cols, rows_ref, x0, x1, x2, x3,
                 keep, send, b0, b1, b2, b3, sums, copies, total, back):
    t = pl.program_id(0)
    me, core = ids[0], ids[1]

    @pl.when(t == 0)
    def _():
        back[...] = jnp.zeros_like(back)

        @pl.loop(0, cot_one.shape[1] // 32)
        def _(i):
            rows = pl.ds(pl.multiple_of(i * 32, 32), 32)
            for phase, (row_phase, col_phase) in enumerate(phase_pairs):
                field = cot_one[phase, rows, :]
                for k, r in phase_taps[row_phase]:
                    for l, q in phase_taps[col_phase]:
                        copies[3 * k + l, rows, :] = move(field, -r, -q)

    total[...] = dot_nt(copies[t], scaled_one[...])
    split_grad(me, core, total, full, t, inner, rows_ref[0:1, :], keep, send)
    turned = full[t].T
    for n in range(back.shape[1] // TILE):
        here = slice(n * TILE, (n + 1) * TILE)
        back[:, here] += dot(turned, copies[t, :, here])

    @pl.when(t == pl.num_programs(0) - 1)
    def _():
        for k, (out, part) in enumerate(((b0, x0), (b1, x1), (b2, x2), (b3, x3))):
            base = jnp.bitwise_xor(me, k) * 128

            @pl.loop(0, 128 // 32)
            def _(i):
                rows = pl.ds(pl.multiple_of(base + i * 32, 32), 32)
                here = pl.ds(pl.multiple_of(i * 32, 32), 32)
                value = back[rows, :]
                style = jnp.concatenate([cols[0, rows, :]] * 8, axis=1)
                out[here, :] = (value * style).astype(out.dtype)
                sums[rows, :] = jnp.broadcast_to(
                    jnp.sum(value * part[here, :].astype(F32), axis=1, keepdims=True), (32, 128)
                )


def call(kernel, grid, flops, ins, outs, scratch, args):
    return pl.pallas_call(
        kernel,
        grid=(grid,),
        in_specs=ins,
        out_specs=[spec for _, _, spec in outs],
        out_shape=[jax.ShapeDtypeStruct(shape, dtype) for shape, dtype, _ in outs],
        scratch_shapes=scratch,
        compiler_params=pltpu.CompilerParams(vmem_limit_bytes=LIMIT),
        cost_estimate=pl.CostEstimate(flops=flops, bytes_accessed=12 << 20, transcendentals=0),
    )(*args)


def quad(value, k):
    return lax.ppermute(value, "chan", [(i, i ^ k) for i in range(4)])


def pair(value):
    return lax.ppermute(value, "dp", [(i, i ^ 1) for i in range(8)])


def after(value, *others):
    return lax.optimization_barrier((value,) + others)[0]


def natural(parts, me):
    stacked = jnp.stack(parts)
    stacked = stacked.reshape((2, 2) + stacked.shape[1:])
    stacked = jnp.where(me % 2 == 1, stacked[:, ::-1], stacked)
    stacked = jnp.where(me // 2 == 1, stacked[::-1], stacked)
    return stacked.reshape((4,) + stacked.shape[2:])


def pick(value, index, axis):
    return lax.dynamic_index_in_dim(value, index, axis, keepdims=False)


def to_phases(field):
    lead = field.shape[:-1]
    blocked = field.reshape(lead + (HALF, 2, HALF, 2))
    n = len(lead)
    return blocked.transpose((n + 1, n + 3) + tuple(range(n)) + (n, n + 2)).reshape((4,) + lead + (HALF * HALF,))


def phase_order():
    place = jnp.arange(512)
    row, col = place // SIDE, place % SIDE
    grouped = ((row % 2) * 2 + col % 2) * 128 + (row // 2) * HALF + col // 2
    return (jnp.arange(512)[:, None] == grouped[None, :]).astype(BF)


def image_body(
    feat_in,
    rgb_in,
    latent,
    noise_first,
    noise_second,
    live_count,
    conv_first,
    conv_second,
    style_weight,
    style_bias,
    rgb_weight,
    conv_bias,
    rgb_bias,
    noise_gain,
    feat_grad,
    rgb_grad,
):
    local_ch, images, half_pix = feat_in.shape
    channels = 4 * local_ch
    pixels = feat_grad.shape[2]
    me = lax.axis_index("chan")
    row = lax.axis_index("dp")
    core = row % 2
    depth = row // 2
    to = [jnp.bitwise_xor(me, k) for k in range(4)]
    live_mask = (jnp.arange(images) < live_count[0]).astype(F32)
    live = (me < live_count[0]).astype(F32)
    ids = jnp.stack([me, core]).astype(jnp.int32)
    gains = jnp.concatenate([noise_gain, live[None]])

    styles = jnp.einsum("bw,jwc->bjc", latent, style_weight, precision=precise) + style_bias[None]
    shared = jnp.concatenate([conv_bias, rgb_weight.astype(F32)])
    packs = [jnp.concatenate([pick(styles, to[k], 0), shared]) for k in range(4)]
    packs = [packs[0]] + [quad(packs[k], k) for k in (1, 2, 3)]
    vectors = natural(packs, me).transpose(1, 0, 2).reshape(8, channels)
    style_mine, bias_all, rgb_all = vectors[:3], vectors[3:5], vectors[5:8]
    cols = jnp.broadcast_to(vectors[:5, :, None], (5, channels, 128))
    squares = jnp.pad(style_mine[:2] * style_mine[:2], ((0, 6), (0, 0)))

    x = [pick(feat_in, to[k], 1) for k in range(4)]
    x = [x[0]] + [quad(x[k], k) for k in (1, 2, 3)]

    half_one = lax.dynamic_slice_in_dim(conv_first, core * 64, 64, 1)
    one_others = [quad(half_one, k) for k in (1, 2, 3)]
    one_swapped = [pair(part) for part in one_others]
    grad_by_image = feat_grad.transpose(1, 0, 2)

    noise_one = to_phases(pick(noise_first, me, 0))
    noise_two = to_phases(pick(noise_second, me, 0))
    order = phase_order()
    cot_mine = (pick(rgb_grad, me, 0) * live).astype(BF)
    color_cot = jnp.pad(to_phases(cot_mine), ((0, 0), (0, 13), (0, 0)))
    rgb_rows = jnp.pad((rgb_all * style_mine[2:3]).astype(BF), ((0, 13), (0, 0)))
    rgb_cols = jnp.pad(rgb_all.astype(BF), ((0, 13), (0, 0))).T

    tiles = half_pix // TILE
    vec = ((channels, 128), F32, whole((channels, 128)))
    cols_spec, row_spec, noise_spec = whole(cols.shape), whole(squares.shape), whole(noise_one.shape)
    full_spec = whole((9, channels, channels))
    tile_spec = pl.BlockSpec((4, channels, TILE), lambda j: (0, 0, j))
    field_spec = whole((4, channels, half_pix))
    image_spec = pl.BlockSpec((local_ch, 4 * TILE), lambda j: (0, j))
    x_spec = whole((local_ch, half_pix))

    vmem = pl.BlockSpec(memory_space=pltpu.VMEM)
    field, wide_weight = (4, channels, half_pix), (9, channels, channels)
    (raised, scaled_two, convolved, feat_natural, full_one, full_two, grad_arrived,
     scaled_one, demod_one, demod_two, color) = pl.pallas_call(
        forward_kernel,
        in_specs=[SMEM] + [vmem] * 4 + [ANY] * 9 + [vmem] * 6,
        out_specs=[ANY] * 7 + [vmem] * 4,
        out_shape=[
            jax.ShapeDtypeStruct(shape, dtype)
            for shape, dtype in (
                (field, F32), (field, BF), (field, F32), ((channels, pixels), BF), (wide_weight, BF),
                (wide_weight, BF), ((channels, pixels), BF), ((channels, half_pix), BF), ((channels, 128), F32),
                ((channels, 128), F32), ((16, pixels), F32),
            )
        ],
        scratch_shapes=[
            pltpu.VMEM(field, F32),
            pltpu.VMEM(field, BF),
            pltpu.VMEM(wide_weight, BF),
            pltpu.VMEM(wide_weight, BF),
            pltpu.VMEM((16, channels, half_pix), BF),
            pltpu.VMEM((2, 4, channels, TILE), F32),
            pltpu.VMEM((2, channels, 4 * TILE), BF),
            pltpu.VMEM((TILE // 128, channels, 512), BF),
            pltpu.SemaphoreType.DMA((8,)),
            pltpu.SemaphoreType.DMA((5,)),
            pltpu.SemaphoreType.DMA((2, 2)),
        ]
        + [pltpu.SemaphoreType.DMA((3,))] * 6,
        compiler_params=pltpu.CompilerParams(vmem_limit_bytes=LIMIT, collective_id=0, has_side_effects=True),
        cost_estimate=pl.CostEstimate(flops=int(50e9), bytes_accessed=12 << 20, transcendentals=0),
    )(gains, *x, conv_first, *one_others, *one_swapped, conv_second, grad_by_image, cols, squares,
      noise_one, noise_two, order, rgb_rows)

    cot_two, sums_two, rgb_part, inner_two = call(
        cot_kernel,
        tiles,
        int(12e9),
        [SMEM, tile_spec, pl.BlockSpec((channels, 4 * TILE), lambda j: (0, j))]
        + [cols_spec, whole((channels, 128)), noise_spec, whole((512, 512)), whole((4, 16, half_pix)),
           whole((channels, 16))],
        [
            ((4, channels, half_pix), BF, tile_spec),
            ((4, channels, 128), F32, whole((4, channels, 128))),
            ((16, channels), F32, whole((16, channels))),
            vec,
        ],
        [pltpu.VMEM((4, channels, TILE), F32), pltpu.VMEM((channels, TILE), BF)],
        (gains, convolved, grad_arrived, cols, demod_two, noise_two, order.T, color_cot, rgb_cols),
    )

    grad_spec = pl.BlockSpec((4, 1, 64, channels), lambda t: (0, t, 0, 0))
    grad_shape = ((4, 9, 64, channels), BF, grad_spec)
    keep_two, send_two = call(
        second_grad_kernel,
        9,
        int(22e9),
        [SMEM, field_spec, field_spec, full_spec, whole((channels, 128)), row_spec],
        [grad_shape, grad_shape],
        [pltpu.VMEM((16, channels, half_pix), BF), pltpu.VMEM((channels, channels), F32)],
        (ids, cot_two, scaled_two, full_two, inner_two, squares),
    )
    grad_two = reduce_grad(keep_two, send_two, me, depth)

    cot_one, sums_one, inner_one = call(
        second_back_kernel,
        tiles,
        int(35e9),
        [SMEM, SMEM, field_spec, full_spec, tile_spec, cols_spec, whole((channels, 128)), noise_spec],
        [
            ((4, channels, half_pix), BF, tile_spec),
            ((4, channels, 128), F32, whole((4, channels, 128))),
            vec,
        ],
        [
            pltpu.VMEM((16, channels, half_pix), BF),
            pltpu.VMEM((9, channels, channels), BF),
            pltpu.VMEM((channels, TILE), F32),
        ],
        (ids, gains, cot_two, full_two, raised, cols, demod_one, noise_one),
    )

    keep_one, send_one, b0, b1, b2, b3, sums_zero = call(
        first_kernel,
        9,
        int(15e9),
        [SMEM, field_spec, whole((channels, half_pix)), full_spec, whole((channels, 128)), cols_spec, row_spec]
        + [x_spec] * 4,
        [grad_shape, grad_shape] + [((local_ch, half_pix), BF, x_spec)] * 4 + [vec],
        [
            pltpu.VMEM((9, channels, half_pix), BF),
            pltpu.VMEM((channels, channels), F32),
            pltpu.VMEM((channels, half_pix), F32),
        ],
        (ids, cot_one, scaled_one, full_one, inner_one, cols, squares, *x),
    )
    grad_one = reduce_grad(keep_one, send_one, me, depth)

    feat_out = [lax.dynamic_slice_in_dim(feat_natural, to[k] * local_ch, local_ch, 0) for k in range(4)]
    feat_out = [feat_out[0]] + [quad(feat_out[k], k) for k in (1, 2, 3)]
    feat_out = natural(feat_out, me).transpose(1, 0, 2)
    back = [b0] + [quad(part, k + 1) for k, part in enumerate((b1, b2, b3))]
    feat_in_grad = natural(back, me).transpose(1, 0, 2).astype(F32)

    lift_matrix = upsample_matrix(HALF)
    color = color[:3]
    shard_pix = pixels // 4
    color = color.reshape(3, 4, shard_pix)
    color = [pick(color, to[k], 1) for k in range(4)]
    color = natural([color[0]] + [quad(color[k], k) for k in (1, 2, 3)], me)
    skip_up = jnp.einsum(
        "up,bkpq,vq->bkuv",
        lift_matrix,
        rgb_in.reshape(images, 3, HALF, HALF),
        lift_matrix,
        precision=precise,
    ).reshape(images, 3, pixels)
    skip_mine = lax.dynamic_slice_in_dim(skip_up, me * shard_pix, shard_pix, 2)
    rgb_out = (color + rgb_bias[None, :, None] + skip_mine) * live_mask[:, None, None]
    rgb_cot = rgb_grad * live_mask[:, None, None]
    rgb_in_grad = jnp.einsum(
        "up,bkuv,vq->bkpq",
        lift_matrix,
        rgb_cot.reshape(images, 3, SIDE, SIDE),
        lift_matrix,
        precision=precise,
    ).reshape(images, 3, half_pix)
    rgb_bias_part = jnp.sum(rgb_cot, axis=(0, 2))

    sums_two = jnp.sum(sums_two, axis=2)
    sums_one = jnp.sum(sums_one, axis=2)
    inner_two, inner_one = inner_two[:, 0], inner_one[:, 0]
    style_two_demod = 2.0 * style_mine[1] * square_back(inner_two, full_two)
    style_one_demod = 2.0 * style_mine[0] * square_back(inner_one, full_one)
    rows_out = jnp.stack(
        [
            sums_zero[:, 0] + style_one_demod,
            sums_one[3] + style_two_demod,
            sums_two[3],
            sums_one[1],
            sums_two[1],
            sums_one[2],
            sums_two[2],
        ]
    )
    rows_out = jnp.concatenate([rows_out, rgb_part[:3]]).reshape(10, 4, local_ch)
    rows_out = [pick(rows_out, to[k], 1) for k in range(4)]
    rows_in = natural([rows_out[0]] + [quad(rows_out[k], k) for k in (1, 2, 3)], me)
    style_grads = rows_in[:, :3]
    latent_part = jnp.einsum("bjc,jwc->bw", style_grads, style_weight, precision=precise)
    latent_grad = latent_part + quad(latent_part, 1) + quad(latent_part, 2) + quad(latent_part, 3)
    extra = jnp.pad(rgb_bias_part[None], ((0, 0), (0, local_ch - 3)))
    gathered = jnp.concatenate([rows_in.reshape(40, local_ch), extra, latent.reshape(16, 128)])
    gathered = lax.all_gather(gathered, "dp")
    every_row = gathered[:, :40].reshape(8, 4, 10, local_ch)
    every_latent = gathered[:, 41:].reshape(8, 4, 512)
    style_weight_grad = jnp.einsum("gbw,gbjc->jwc", every_latent, every_row[:, :, :3], precision=precise)
    summed = jnp.sum(every_row, axis=(0, 1))
    gain_part = jnp.sum(summed[5:7], axis=1)
    gain_grad = lax.psum(gain_part, "chan")
    rgb_bias_grad = jnp.sum(gathered[:, 40, :3], axis=0)
    return (
        feat_out,
        rgb_out,
        feat_in_grad,
        rgb_in_grad,
        latent_grad,
        grad_one,
        grad_two,
        style_weight_grad,
        summed[:3],
        summed[7:10],
        summed[3:5],
        rgb_bias_grad,
        gain_grad,
    )


def square_back(inner, full):
    total = jnp.zeros(full.shape[1:], F32)
    for t in range(9):
        value = full[t].astype(F32)
        total = total + value * value
    return jnp.sum(inner[:, None] * total, axis=0)


def reduce_grad(keep, send, me, depth):
    part = (keep.astype(F32) + pair(send).astype(F32)).astype(BF)
    total = part[0].astype(F32)
    for k in (1, 2, 3):
        total = total + quad(part[k], k).astype(F32)
    block = total.astype(BF).reshape(9, 4, 16, 512)

    def along(value, k):
        return lax.ppermute(value, "dp", [(i, i ^ (2 * k)) for i in range(8)])

    summed = pick(block, depth, 1).astype(F32)
    for k in (1, 2, 3):
        summed = summed + along(pick(block, jnp.bitwise_xor(depth, k), 1), k).astype(F32)
    summed = summed.astype(BF)
    spread = natural([summed] + [along(summed, k) for k in (1, 2, 3)], depth)
    mine = spread.transpose(1, 0, 2, 3).reshape(9, 64, 512)
    theirs = pair(mine)
    core = lax.axis_index("dp") % 2
    low = jnp.where(core == 0, mine, theirs)
    high = jnp.where(core == 0, theirs, mine)
    return jnp.concatenate([low, high], axis=1).astype(F32)


def solution(mesh):
    alone = mesh.shape["chan"] == 4 and mesh.shape["dp"] == 8
    return jax.shard_map(
        image_body if alone else body,
        mesh=mesh,
        in_specs=(
            P("chan", "dp", None),
            P("dp", None, None),
            P("dp", None),
            P("dp", None),
            P("dp", None),
            P("dp"),
            P(None, "chan", None),
            P(None, "chan", None),
            P(None, None, "chan"),
            P(None, "chan"),
            P(None, "chan"),
            P(None, "chan"),
            P(),
            P(),
            P("chan", "dp", None),
            P("dp", None, None),
        ),
        out_specs=(
            P("chan", "dp", None),
            P("dp", None, "chan"),
            P("chan", "dp", None),
            P("dp", None, None),
            P("dp", None),
            P(None, "chan", None),
            P(None, "chan", None),
            P(None, None, "chan"),
            P(None, "chan"),
            P(None, "chan"),
            P(None, "chan"),
            P(),
            P(),
        ),
        check_vma=False,
    )
```

```python
import functools

import jax
import jax.numpy as jnp
from jax import lax
from jax.experimental import pallas as pl
from jax.experimental.pallas import tpu as pltpu
from jax.sharding import PartitionSpec as P

SIDE = 64
HALF = 32


precise = lax.Precision.HIGHEST
epsilon = 1e-08
root_two = 1.4142135623730951
phase_taps = (((1, 0),), ((2, 0), (0, 1)))
phase_pairs = ((0, 0), (0, 1), (1, 0), (1, 1))


def leaky_silu(value):
    return root_two * (0.2 * value + 0.8 * jax.nn.silu(value))


def leaky_slope(value):
    sigma = jax.nn.sigmoid(value)
    return root_two * (0.2 + 0.8 * sigma * (1.0 + value * (1.0 - sigma)))


def shifted(field, row_shift, col_shift, width):
    cells = field.shape[-1]
    offset = row_shift * width + col_shift
    if offset > 0:
        result = jnp.concatenate(
            [field[..., offset:], jnp.zeros(field.shape[:-1] + (offset,), field.dtype)], axis=-1
        )
    elif offset < 0:
        result = jnp.concatenate(
            [jnp.zeros(field.shape[:-1] + (-offset,), field.dtype), field[..., : cells + offset]],
            axis=-1,
        )
    else:
        result = field
    if col_shift != 0:
        column = jnp.arange(cells) % width
        inside = (column + col_shift >= 0) & (column + col_shift < width)
        result = jnp.where(inside, result, jnp.zeros((), field.dtype))
    return result


def upsample_matrix(half_side):
    rows_out = jnp.arange(2 * half_side)[:, None]
    cols_in = jnp.arange(half_side)[None, :]
    centre = rows_out // 2
    beside = centre - 1 + 2 * (rows_out % 2)
    return (
        jnp.where(cols_in == centre, 0.75, 0.0) + jnp.where(cols_in == beside, 0.25, 0.0)
    ).astype(jnp.float32)


def alternate(phases, half_side):
    stacked = jnp.stack(phases)
    out_rows, batch_count = (stacked.shape[1], stacked.shape[2])
    blocked = stacked.reshape(2, 2, out_rows, batch_count, half_side, half_side)
    return blocked.transpose(2, 3, 4, 0, 5, 1).reshape(
        out_rows, batch_count, 4 * half_side * half_side
    )


def split_phases(field, half_side):
    out_rows, batch_count = (field.shape[0], field.shape[1])
    blocked = field.reshape(out_rows, batch_count, half_side, 2, half_side, 2)
    return [
        blocked[:, :, :, row_phase, :, col_phase].reshape(
            out_rows, batch_count, half_side * half_side
        )
        for row_phase, col_phase in phase_pairs
    ]


def up_conv(inputs, weight, half_side):
    shifted_inputs = {}
    for row_shift in (0, 1):
        for col_shift in (0, 1):
            shifted_inputs[row_shift, col_shift] = shifted(inputs, row_shift, col_shift, half_side)
    phases = []
    for row_phase, col_phase in phase_pairs:
        summed = None
        for row_tap, row_shift in phase_taps[row_phase]:
            for col_tap, col_shift in phase_taps[col_phase]:
                product = jnp.einsum(
                    "oc,cbp->obp",
                    weight[row_tap * 3 + col_tap],
                    shifted_inputs[row_shift, col_shift],
                    preferred_element_type=jnp.float32,
                )
                summed = product if summed is None else summed + product
        phases.append(summed)
    return alternate(phases, half_side)


def phase_grads(grad_field, half_side):
    grad_phases = split_phases(grad_field, half_side)
    shifted_grads = [None] * 9
    for phase_index in range(4):
        row_phase, col_phase = phase_pairs[phase_index]
        for row_tap, row_shift in phase_taps[row_phase]:
            for col_tap, col_shift in phase_taps[col_phase]:
                shifted_grads[row_tap * 3 + col_tap] = shifted(
                    grad_phases[phase_index], -row_shift, -col_shift, half_side
                )
    return shifted_grads


def flat_conv(inputs, weight, width):
    summed = None
    for tap_index in range(9):
        product = jnp.einsum(
            "oc,cbp->obp", weight[tap_index], inputs, preferred_element_type=jnp.float32
        )
        product = shifted(product, tap_index // 3 - 1, tap_index % 3 - 1, width)
        summed = product if summed is None else summed + product
    return summed


def body(
    feat_in,
    rgb_in,
    latent,
    noise_first,
    noise_second,
    live_count,
    conv_first,
    conv_second,
    style_weight,
    style_bias,
    rgb_weight,
    conv_bias,
    rgb_bias,
    noise_gain,
    feat_grad,
    rgb_grad,
):
    local_ch, images, half_pix = feat_in.shape
    pixels = feat_grad.shape[2]
    half_side = HALF
    full_side = SIDE
    chan_rank = lax.axis_index("chan")
    live_mask = (jnp.arange(images) < live_count[0]).astype(jnp.float32)
    styles = (
        jnp.einsum("bw,jwc->jbc", latent, style_weight, precision=precise) + style_bias[:, None, :]
    )
    first_all, second_all = (
        lax.all_gather(styles[0], "chan", axis=1, tiled=True),
        lax.all_gather(styles[1], "chan", axis=1, tiled=True),
    )
    weight_one = conv_first.astype(jnp.float32)
    weight_two = conv_second.astype(jnp.float32)
    squares_one = jnp.sum(weight_one * weight_one, axis=0)
    squares_two = jnp.sum(weight_two * weight_two, axis=0)
    demod_one = lax.rsqrt(
        jnp.dot(first_all * first_all, squares_one.T, precision=precise) + epsilon
    )
    demod_two = lax.rsqrt(
        jnp.dot(second_all * second_all, squares_two.T, precision=precise) + epsilon
    )
    scaled_one = (feat_in.astype(jnp.float32) * styles[0].T[:, :, None]).astype(jnp.bfloat16)
    gathered_one = lax.all_gather(scaled_one, "chan", axis=0, tiled=True)
    raised = up_conv(gathered_one, conv_first, half_side)
    pre_one = (
        raised * demod_one.T[:, :, None]
        + noise_gain[0] * noise_first[None, :, :]
        + conv_bias[0][:, None, None]
    )
    act_one = leaky_silu(pre_one)
    scaled_two = (act_one * styles[1].T[:, :, None]).astype(jnp.bfloat16)
    gathered_two = lax.all_gather(scaled_two, "chan", axis=0, tiled=True)
    convolved = flat_conv(gathered_two, conv_second, full_side)
    pre_two = (
        convolved * demod_two.T[:, :, None]
        + noise_gain[1] * noise_second[None, :, :]
        + conv_bias[1][:, None, None]
    )
    act_two = leaky_silu(pre_two)
    feat_out = (act_two * live_mask[None, :, None]).astype(jnp.bfloat16)
    scaled_rgb = (act_two * styles[2].T[:, :, None]).astype(jnp.bfloat16)
    color_part = jnp.einsum(
        "ko,obp->bkp", rgb_weight, scaled_rgb, preferred_element_type=jnp.float32
    )
    color = lax.psum_scatter(color_part, "chan", scatter_dimension=2, tiled=True)
    shard_pix = color.shape[2]
    lift_matrix = upsample_matrix(half_side)
    skip_up = jnp.einsum(
        "up,bkpq,vq->bkuv",
        lift_matrix,
        rgb_in.reshape(images, 3, half_side, half_side),
        lift_matrix,
        precision=precise,
    ).reshape(images, 3, pixels)
    skip_mine = lax.dynamic_slice_in_dim(skip_up, chan_rank * shard_pix, shard_pix, 2)
    rgb_out = (color + rgb_bias[None, :, None] + skip_mine) * live_mask[:, None, None]
    rgb_cot = rgb_grad * live_mask[:, None, None]
    color_cot = rgb_cot.astype(jnp.bfloat16)
    rgb_in_grad = jnp.einsum(
        "up,bkuv,vq->bkpq",
        lift_matrix,
        rgb_cot.reshape(images, 3, full_side, full_side),
        lift_matrix,
        precision=precise,
    ).reshape(images, 3, half_pix)
    rgb_bias_part = jnp.sum(rgb_cot, axis=(0, 2))
    rgb_weight_part = jnp.einsum(
        "bkp,obp->ko", color_cot, scaled_rgb, preferred_element_type=jnp.float32
    )
    back_rgb = jnp.einsum("ko,bkp->obp", rgb_weight, color_cot, preferred_element_type=jnp.float32)
    style_rgb_grad = jnp.sum(back_rgb * act_two, axis=2).T
    grad_pre_two = (
        feat_grad.astype(jnp.float32) * live_mask[None, :, None]
        + back_rgb * styles[2].T[:, :, None]
    ) * leaky_slope(pre_two)
    cot_two = (grad_pre_two * demod_two.T[:, :, None]).astype(jnp.bfloat16)
    inner_two = (
        -0.5 * demod_two * demod_two * demod_two * jnp.sum(grad_pre_two * convolved, axis=2).T
    )
    taps_two = jnp.stack(
        [
            shifted(cot_two, 1 - tap_index // 3, 1 - tap_index % 3, full_side)
            for tap_index in range(9)
        ]
    )
    squares_two_grad = jnp.dot(inner_two.T, second_all * second_all, precision=precise)
    conv_two_grad = (
        jnp.einsum("tobp,cbp->toc", taps_two, gathered_two, preferred_element_type=jnp.float32)
        + 2.0 * weight_two * squares_two_grad[None]
    )
    style_two_demod = 2.0 * second_all * jnp.dot(inner_two, squares_two, precision=precise)
    columns = conv_second
    back_two = lax.psum_scatter(
        jnp.einsum("toc,tobp->cbp", columns, taps_two, preferred_element_type=jnp.float32),
        "chan",
        scatter_dimension=0,
        tiled=True,
    )
    style_two_conv = jnp.sum(back_two * act_one, axis=2).T
    grad_pre_one = back_two * styles[1].T[:, :, None] * leaky_slope(pre_one)
    cot_one = (grad_pre_one * demod_one.T[:, :, None]).astype(jnp.bfloat16)
    inner_one = -0.5 * demod_one * demod_one * demod_one * jnp.sum(grad_pre_one * raised, axis=2).T
    taps_one = jnp.stack(phase_grads(cot_one, half_side))
    squares_one_grad = jnp.dot(inner_one.T, first_all * first_all, precision=precise)
    conv_one_grad = (
        jnp.einsum("tobp,cbp->toc", taps_one, gathered_one, preferred_element_type=jnp.float32)
        + 2.0 * weight_one * squares_one_grad[None]
    )
    style_one_demod = 2.0 * first_all * jnp.dot(inner_one, squares_one, precision=precise)
    columns = conv_first
    back_one = lax.psum_scatter(
        jnp.einsum("toc,tobp->cbp", columns, taps_one, preferred_element_type=jnp.float32),
        "chan",
        scatter_dimension=0,
        tiled=True,
    )
    feat_in_grad = back_one * styles[0].T[:, :, None]
    style_one_conv = jnp.sum(back_one * feat_in.astype(jnp.float32), axis=2).T
    demod_one_sum, demod_two_sum = (
        lax.psum_scatter(style_one_demod, "chan", scatter_dimension=1, tiled=True),
        lax.psum_scatter(style_two_demod, "chan", scatter_dimension=1, tiled=True),
    )
    style_grads = jnp.stack(
        [style_one_conv + demod_one_sum, style_two_conv + demod_two_sum, style_rgb_grad]
    )
    latent_part = jnp.einsum("jbc,jwc->bw", style_grads, style_weight, precision=precise)
    gain_part = jnp.stack(
        [
            jnp.sum(grad_pre_one * noise_first[None, :, :]),
            jnp.sum(grad_pre_two * noise_second[None, :, :]),
        ]
    )
    latent_grad, gain_chan = lax.psum((latent_part, gain_part), "chan")
    style_weight_part = jnp.einsum("bw,jbc->jwc", latent, style_grads, precision=precise)
    style_bias_part = jnp.sum(style_grads, axis=1)
    conv_bias_part = jnp.stack(
        [jnp.sum(grad_pre_one, axis=(1, 2)), jnp.sum(grad_pre_two, axis=(1, 2))]
    )
    totals = lax.psum(
        (
            conv_one_grad,
            conv_two_grad,
            style_weight_part,
            style_bias_part,
            rgb_weight_part,
            conv_bias_part,
            rgb_bias_part,
            gain_chan,
        ),
        "dp",
    )
    return (feat_out, rgb_out, feat_in_grad, rgb_in_grad, latent_grad) + tuple(totals)


BF = jnp.bfloat16
F32 = jnp.float32
TILE = 256
ROWS = 16
ANY = pl.BlockSpec(memory_space=pl.ANY)
SMEM = pl.BlockSpec(memory_space=pltpu.SMEM)
LIMIT = 60 * 1024 * 1024


def whole(shape):
    return pl.BlockSpec(shape, lambda j: (0,) * len(shape))


def dot(a, b):
    return jnp.dot(a, b, preferred_element_type=F32)


def dot_nt(a, b):
    return lax.dot_general(a, b, (((1,), (1,)), ((), ())), preferred_element_type=F32)


def wide(column):
    return jnp.concatenate([column] * (TILE // 128), axis=1)


def move(field, row_shift, col_shift):
    offset = row_shift * HALF + col_shift
    if offset == 0:
        return field
    cells = field.shape[1]
    lane = lax.broadcasted_iota(jnp.int32, field.shape, 1)
    row, col = lane // HALF, lane % HALF
    inside = (row + row_shift >= 0) & (row + row_shift < HALF)
    inside = inside & (col + col_shift >= 0) & (col + col_shift < HALF)
    rolled = pltpu.roll(field.astype(F32), (-offset) % cells, 1)
    return jnp.where(inside, rolled, 0.0).astype(field.dtype)


def near(parity, step):
    other = (parity + step) % 2
    return other, (parity + step - other) // 2


def copy_index(phase, row_step, col_step):
    a, r = near(phase // 2, row_step)
    b, q = near(phase % 2, col_step)
    return ((a * 2 + b) * 2 + abs(r)) * 2 + abs(q)


def make_copies(source, copies):
    chunk = 32

    @pl.loop(0, source.shape[1] // chunk)
    def _(i):
        rows = pl.ds(pl.multiple_of(i * chunk, chunk), chunk)
        for phase in range(4):
            field = source[phase, rows, :]
            row_sign = 1 if phase // 2 == 0 else -1
            col_sign = 1 if phase % 2 == 0 else -1
            for r in (0, 1):
                for q in (0, 1):
                    copies[(phase * 2 + r) * 2 + q, rows, :] = move(
                        field, row_sign * r, col_sign * q
                    )


def demodulate(full, square_row, demod):
    chunk = 32

    @pl.loop(0, full.shape[1] // chunk)
    def _(i):
        rows = pl.ds(pl.multiple_of(i * chunk, chunk), chunk)
        total = None
        for t in range(9):
            value = full[t, rows, :].astype(F32)
            total = value * value if total is None else total + value * value
        total = jnp.sum(total * square_row, axis=1, keepdims=True)
        demod[rows, :] = jnp.broadcast_to(lax.rsqrt(total + epsilon), (chunk, 128))


def chan_peer(me, k):
    if k == 1:
        return me + 1 - 2 * (me % 2)
    return (me + 2) % 4 if k == 2 else 3 - me


def rows_of(base, size):
    return pl.ds(pl.multiple_of(base, size), size)


def forward_kernel(gains, x0, x1, x2, x3, own1, g1, g2, g3, s1, s2, s3, own2, feat_grad,
                   cols, rows_ref, noise1, noise2, order, rgb_rows, color_cot,
                   raised_out, scaled_out, conv_out, feat_out, full1_out, full2_out, grad_out,
                   scaled_one, demod1, demod2, color, rgb_grad,
                   raised, scaled, full1, full2, copies, conv_tile, feat_tile, ordered,
                   load_sem, store_sem, tile_sem, send_sem, recv_sem, swap_send, swap_recv, grad_send, grad_recv):
    me = lax.axis_index("chan")
    row = lax.axis_index("dp")
    core = row % 2
    twin = row + 1 - 2 * core
    barrier = pltpu.get_barrier_semaphore()
    for k in (1, 2, 3):
        pl.semaphore_signal(barrier, inc=1, device_id={"chan": chan_peer(me, k)}, device_id_type=pl.DeviceIdType.MESH)
    pl.semaphore_signal(barrier, inc=1, device_id={"dp": twin}, device_id_type=pl.DeviceIdType.MESH)
    pl.semaphore_wait(barrier, 4)

    mine = rows_of(me * 128 + core * 64, 64)
    weight_moves = [
        pltpu.make_async_remote_copy(
            own2.at[:, rows_of(core * 64, 64), :], full2.at[:, mine, :], send_sem.at[k - 1], recv_sem.at[k - 1],
            device_id={"chan": chan_peer(me, k)}, device_id_type=pl.DeviceIdType.MESH,
        )
        for k in (1, 2, 3)
    ]
    for item in weight_moves:
        item.start()
    swap_moves = []
    for k in (1, 2, 3):
        part = rows_of(chan_peer(me, k) * 128 + core * 64, 64)
        swap_moves.append(
            pltpu.make_async_remote_copy(
                full2.at[:, part, :], full2.at[:, part, :], swap_send.at[k - 1], swap_recv.at[k - 1],
                device_id={"dp": twin}, device_id_type=pl.DeviceIdType.MESH,
            )
        )
    local2 = pltpu.make_async_copy(own2, full2.at[:, rows_of(me * 128, 128), :], load_sem.at[7])
    local2.start()
    loads = [pltpu.make_async_copy(own1, full1.at[:, rows_of(me * 128, 128), :], load_sem.at[0])]
    for k, (same, other) in enumerate(((g1, s1), (g2, s2), (g3, s3))):
        base = chan_peer(me, k + 1) * 128
        loads.append(pltpu.make_async_copy(same, full1.at[:, rows_of(base + core * 64, 64), :], load_sem.at[1 + k]))
        loads.append(pltpu.make_async_copy(other, full1.at[:, rows_of(base + 64 - core * 64, 64), :], load_sem.at[4 + k]))
    for item in loads:
        item.start()

    for k, part in enumerate((x0, x1, x2, x3)):
        base = me * 128 if k == 0 else chan_peer(me, k) * 128

        @pl.loop(0, 128 // 32)
        def _(i):
            rows = rows_of(base + i * 32, 32)
            style = jnp.concatenate([cols[0, rows, :]] * 8, axis=1)
            value = (part[rows_of(i * 32, 32), :].astype(F32) * style).astype(BF)
            scaled_one[rows, :] = value
            for r in (0, 1):
                for q in (0, 1):
                    copies[2 * r + q, rows, :] = move(value, r, q)

    for item in loads:
        item.wait()
    store1 = pltpu.make_async_copy(full1, full1_out, store_sem.at[0])
    store1.start()
    demodulate(full1, rows_ref[0:1, :], demod1)

    @pl.loop(0, raised.shape[2] // TILE)
    def _(j):
        here = rows_of(j * TILE, TILE)
        for phase, (row_phase, col_phase) in enumerate(phase_pairs):
            total = None
            for k, r in phase_taps[row_phase]:
                for l, q in phase_taps[col_phase]:
                    term = dot(full1[3 * k + l], copies[2 * r + q, :, here])
                    total = term if total is None else total + term
            raised[phase, :, here] = total
            noise_row = gains[0] * noise1[phase : phase + 1, here]
            for i in range(raised.shape[1] // ROWS):
                rows = slice(i * ROWS, (i + 1) * ROWS)
                pre = raised[phase, rows, here] * wide(demod1[rows, :]) + noise_row + wide(cols[3, rows, :])
                act = pre * (0.6 * root_two + 0.4 * root_two * jnp.tanh(0.5 * pre))
                scaled[phase, rows, here] = (act * wide(cols[1, rows, :])).astype(BF)

    stores = [
        pltpu.make_async_copy(raised, raised_out, store_sem.at[1]),
        pltpu.make_async_copy(scaled, scaled_out, store_sem.at[2]),
    ]
    for item in stores:
        item.start()
    make_copies(scaled, copies)
    for item, swap in zip(weight_moves, swap_moves):
        item.wait_recv()
        swap.start()
    grad_moves = [
        pltpu.make_async_remote_copy(
            feat_grad.at[chan_peer(me, k)], grad_out.at[rows_of(me * 128, 128), :], grad_send.at[k - 1], grad_recv.at[k - 1],
            device_id={"chan": chan_peer(me, k)}, device_id_type=pl.DeviceIdType.MESH,
        )
        for k in (1, 2, 3)
    ]
    for item in grad_moves:
        item.start()
    local3 = pltpu.make_async_copy(feat_grad.at[me], grad_out.at[rows_of(me * 128, 128), :], store_sem.at[4])
    local3.start()
    local2.wait()
    for swap in swap_moves:
        swap.wait_recv()
    store2 = pltpu.make_async_copy(full2, full2_out, store_sem.at[3])
    store2.start()
    demodulate(full2, rows_ref[1:2, :], demod2)
    live = gains[2]
    rgb_grad[...] = jnp.zeros_like(rgb_grad)

    def tile_stores(j, slot):
        return (
            pltpu.make_async_copy(conv_tile.at[slot], conv_out.at[:, :, rows_of(j * TILE, TILE)], tile_sem.at[0, slot]),
            pltpu.make_async_copy(feat_tile.at[slot], feat_out.at[:, rows_of(j * 4 * TILE, 4 * TILE)], tile_sem.at[1, slot]),
        )

    @pl.loop(0, raised.shape[2] // TILE)
    def _(j):
        here = rows_of(j * TILE, TILE)
        slot = j % 2

        @pl.when(j >= 2)
        def _():
            for item in tile_stores(j - 2, slot):
                item.wait()

        for phase in range(4):
            total = None
            for t in range(9):
                term = dot(full2[t], copies[copy_index(phase, t // 3 - 1, t % 3 - 1), :, here])
                total = term if total is None else total + term
            conv_tile[slot, phase] = total
            noise_row = gains[1] * noise2[phase : phase + 1, here]
            for i in range(raised.shape[1] // ROWS):
                rows = slice(i * ROWS, (i + 1) * ROWS)
                pre = conv_tile[slot, phase, rows, :] * wide(demod2[rows, :]) + noise_row + wide(cols[4, rows, :])
                act = pre * (0.6 * root_two + 0.4 * root_two * jnp.tanh(0.5 * pre))
                out = (act * live).astype(BF)
                for half in range(TILE // 128):
                    ordered[half, rows, phase * 128 : (phase + 1) * 128] = out[:, half * 128 : (half + 1) * 128]
        for half in range(TILE // 128):
            image = dot(ordered[half], order[...]).astype(BF)
            feat_tile[slot, :, half * 512 : (half + 1) * 512] = image
            pixels = rows_of(j * 4 * TILE + half * 512, 512)
            color[:, pixels] = dot(rgb_rows[...], image)
            rgb_grad[...] += dot_nt(color_cot[:, pixels], image)
        for item in tile_stores(j, slot):
            item.start()

    for j in (2, 3):
        for item in tile_stores(j, j % 2):
            item.wait()
    for item in [store1, store2, local3] + stores:
        item.wait()
    for item in weight_moves + swap_moves:
        item.wait_send()
    for item in grad_moves:
        item.wait()


def backward_kernel(gains, arrived, convolved, raised, scaled_two, full1, full2, feat_natural,
                    scaled_one, x0, x1, x2, x3, cols, rows_ref, demod1, demod2, noise1, noise2, order, color_cot, rgb_cols,
                    feat_all, back_all, grad1_out, grad2_out,
                    sums2, sums1, sums0, inner2, inner1,
                    tile, grad_tile, copies, field, weight, total, back,
                    keep, send, core1, core2, quad1, quad2, zsum1, zsum2, zin1, zin2, out1, out2,
                    load_sem, tile_sem, feat_send, feat_recv, back_send, back_recv, core_send, core_recv,
                    quad_send, quad_recv, z_send, z_recv, all_send, all_recv, twin_send, twin_recv):
    me = lax.axis_index("chan")
    row = lax.axis_index("dp")
    core = row % 2
    depth = row // 2
    twin = row + 1 - 2 * core
    mesh_id = pl.DeviceIdType.MESH
    chans = [me] + [chan_peer(me, k) for k in (1, 2, 3)]
    depths = [depth] + [chan_peer(depth, k) for k in (1, 2, 3)]
    barrier = pltpu.get_barrier_semaphore()
    for k in (1, 2, 3):
        pl.semaphore_signal(barrier, inc=1, device_id={"chan": chans[k]}, device_id_type=mesh_id)
        pl.semaphore_signal(barrier, inc=1, device_id={"dp": depths[k] * 2 + core}, device_id_type=mesh_id)
    pl.semaphore_signal(barrier, inc=1, device_id={"dp": twin}, device_id_type=mesh_id)
    pl.semaphore_wait(barrier, 7)

    def remote(source, target, sent, received, where):
        return pltpu.make_async_remote_copy(source, target, sent, received, device_id=where, device_id_type=mesh_id)

    feat_moves = [
        remote(feat_natural.at[rows_of(chans[k] * 128, 128), :], feat_all.at[me],
               feat_send.at[k - 1], feat_recv.at[k - 1], {"chan": chans[k]})
        for k in (1, 2, 3)
    ]
    for item in feat_moves:
        item.start()
    feat_own = pltpu.make_async_copy(feat_natural.at[rows_of(me * 128, 128), :], feat_all.at[me], load_sem.at[0])
    feat_own.start()
    load2 = pltpu.make_async_copy(full2, weight, load_sem.at[1])
    load2.start()
    load_field = pltpu.make_async_copy(scaled_two, field, load_sem.at[2])
    load_field.start()

    def tiles_in(source, j, slot):
        return pltpu.make_async_copy(source.at[:, :, rows_of(j * TILE, TILE)], tile.at[slot], tile_sem.at[0, slot])

    def grads_in(j, slot):
        return pltpu.make_async_copy(
            arrived.at[:, rows_of(j * 4 * TILE, 4 * TILE)], grad_tile.at[slot], tile_sem.at[1, slot]
        )

    tiles_in(convolved, 0, 0).start()
    grads_in(0, 0).start()
    live = gains[2]
    channels = cols.shape[1]
    tiles = copies.shape[2] // TILE
    sums2[...] = jnp.zeros_like(sums2)
    sums1[...] = jnp.zeros_like(sums1)

    def add_sums(sums, rows, values):
        for n, value in enumerate(values):
            sums[n, rows, :] += value[:, :128] + value[:, 128:]

    @pl.loop(0, tiles)
    def _(j):
        slot = j % 2

        @pl.when(j + 1 < tiles)
        def _():
            tiles_in(convolved, j + 1, 1 - slot).start()
            grads_in(j + 1, 1 - slot).start()

        tiles_in(convolved, j, slot).wait()
        grads_in(j, slot).wait()
        here = rows_of(j * TILE, TILE)
        for half in range(TILE // 128):
            total[half] = dot(grad_tile[slot, :, half * 512 : (half + 1) * 512], order[...])
        for phase in range(4):
            noise_plain = noise2[phase : phase + 1, here]
            noise_row = gains[1] * noise_plain
            back[phase % 2] = dot(rgb_cols[...], color_cot[phase, :, here])
            for i in range(channels // ROWS):
                rows = slice(i * ROWS, (i + 1) * ROWS)
                conv = tile[slot, phase, rows, :]
                scale = wide(demod2[rows, :])
                pre = conv * scale + noise_row + wide(cols[4, rows, :])
                sigma = 0.5 + 0.5 * jnp.tanh(0.5 * pre)
                slope = root_two * (0.2 + 0.8 * sigma * (1.0 + pre * (1.0 - sigma)))
                grad_feat = jnp.concatenate(
                    [total[half, rows, phase * 128 : (phase + 1) * 128] for half in range(TILE // 128)], axis=1
                )
                grad = (grad_feat * live + back[phase % 2, rows, :] * wide(cols[2, rows, :])) * slope
                copies[4 * phase, rows, here] = (grad * scale).astype(BF)
                add_sums(sums2, rows, (grad * conv, grad, grad * noise_plain))

    tiles_in(raised, 0, 0).start()

    def inner_of(sums, demod, inner):
        scale = demod[...]
        inner[...] = -0.5 * scale * scale * scale * jnp.sum(sums[0], axis=1, keepdims=True)

    inner_of(sums2, demod2, inner2)

    def spread_copies():
        chunk = 32

        @pl.loop(0, channels // chunk)
        def _(i):
            rows = rows_of(i * chunk, chunk)
            for phase in range(4):
                value = copies[4 * phase, rows, :]
                row_sign = 1 if phase // 2 == 0 else -1
                col_sign = 1 if phase % 2 == 0 else -1
                for r, q in ((0, 1), (1, 0), (1, 1)):
                    copies[4 * phase + 2 * r + q, rows, :] = move(value, row_sign * r, col_sign * q)

    spread_copies()
    load2.wait()
    load_field.wait()

    def split(slot, t, inner, square_row):
        for k in range(4):
            base = chans[k] * 128
            for out, start in ((keep, base + core * 64), (send, base + 64 - core * 64)):
                rows = rows_of(start, 64)
                column = jnp.concatenate([inner[rows, :]] * 4, axis=1)
                value = total[slot, rows, :] + (2.0 * weight[t, rows, :].astype(F32)) * (column * square_row)
                out[t, k] = value.astype(BF)

    cores, quads, zsums, zins, outs = (core1, core2), (quad1, quad2), (zsum1, zsum2), (zin1, zin2), (out1, out2)

    def taps(g):
        return pl.ds(3 * g, 3)

    def core_move(c, g):
        return remote(send.at[taps(g)], cores[c].at[taps(g)], core_send.at[c, g], core_recv.at[c, g], {"dp": twin})

    def quad_move(c, g, k):
        return remote(keep.at[taps(g), k], quads[c].at[taps(g), k - 1], quad_send.at[c, g, k - 1],
                      quad_recv.at[c, g, k - 1], {"chan": chans[k]})

    def z_move(c, g, k):
        return remote(zsums[c].at[taps(g), rows_of(depths[k] * 16, 16), :], zins[c].at[taps(g), k - 1],
                      z_send.at[c, g, k - 1], z_recv.at[c, g, k - 1], {"dp": depths[k] * 2 + core})

    def all_move(c, g, k):
        part = outs[c].at[taps(g), rows_of(core * 64 + depth * 16, 16), :]
        return remote(part, part, all_send.at[c, g, k - 1], all_recv.at[c, g, k - 1], {"dp": depths[k] * 2 + core})

    def twin_move(c, g):
        part = outs[c].at[taps(g), rows_of(core * 64, 64), :]
        return remote(part, part, twin_send.at[c, g], twin_recv.at[c, g], {"dp": twin})

    def join_cores(c, g):
        core_move(c, g).wait_recv()
        for i in range(3):
            t = 3 * g + i
            for k in range(4):
                keep[t, k] = (keep[t, k].astype(F32) + cores[c][t, k].astype(F32)).astype(BF)
        for k in (1, 2, 3):
            quad_move(c, g, k).start()

    def join_quad(c, g):
        for k in (1, 2, 3):
            quad_move(c, g, k).wait_recv()
        for i in range(3):
            t = 3 * g + i
            value = keep[t, 0].astype(F32)
            for k in range(3):
                value = value + quads[c][t, k].astype(F32)
            zsums[c][t] = value.astype(BF)
        for k in (1, 2, 3):
            z_move(c, g, k).start()

    def join_depth(c, g):
        for k in (1, 2, 3):
            z_move(c, g, k).wait_recv()
        for i in range(3):
            t = 3 * g + i
            value = zsums[c][t, rows_of(depth * 16, 16), :].astype(F32)
            for k in range(3):
                value = value + zins[c][t, k].astype(F32)
            outs[c][t, rows_of(core * 64 + depth * 16, 16), :] = value.astype(BF)
        for k in (1, 2, 3):
            all_move(c, g, k).start()

    def join_all(c, g):
        for k in (1, 2, 3):
            all_move(c, g, k).wait_recv()
        twin_move(c, g).start()

    def weight_grad(c, product, inner, square_row):
        @pl.loop(0, 3)
        def _(g):
            t = 3 * g
            total[0] = product(t)
            total[1] = product(t + 1)
            split(0, t, inner, square_row)
            total[0] = product(t + 2)
            split(1, t + 1, inner, square_row)
            split(0, t + 2, inner, square_row)
            core_move(c, g).start()

            @pl.when(g >= 1)
            def _():
                join_cores(c, g - 1)

        join_cores(c, 2)
        for g in range(3):
            core_move(c, g).wait_send()

    def second_product(t):
        row_step, col_step = 1 - t // 3, 1 - t % 3
        summed = None
        for phase in range(4):
            a, b = phase // 2, phase % 2
            far_row = (row_step * (2 * a - 1) + 1) // 2 * (row_step * row_step)
            far_col = (col_step * (2 * b - 1) + 1) // 2 * (col_step * col_step)
            index = (((a + row_step + 2) % 2 * 2 + (b + col_step + 2) % 2) * 2 + far_row) * 2 + far_col
            term = dot_nt(copies[index], field[phase])
            summed = term if summed is None else summed + term
        return summed

    weight_grad(1, second_product, inner2, rows_ref[1:2, :])

    def turn():
        @pl.loop(0, 9)
        def _(t):
            weight[t] = weight[t].T

    turn()

    @pl.loop(0, tiles)
    def _(j):
        slot = j % 2

        @pl.when(j + 1 < tiles)
        def _():
            tiles_in(raised, j + 1, 1 - slot).start()

        tiles_in(raised, j, slot).wait()
        here = rows_of(j * TILE, TILE)
        for phase in range(4):
            summed = None
            for t in range(9):
                term = dot(weight[t], copies[copy_index(phase, 1 - t // 3, 1 - t % 3), :, here])
                summed = term if summed is None else summed + term
            back[phase % 2] = summed
            noise_plain = noise1[phase : phase + 1, here]
            noise_row = gains[0] * noise_plain
            for i in range(channels // ROWS):
                rows = slice(i * ROWS, (i + 1) * ROWS)
                conv = tile[slot, phase, rows, :]
                scale = wide(demod1[rows, :])
                pre = conv * scale + noise_row + wide(cols[3, rows, :])
                sigma = 0.5 + 0.5 * jnp.tanh(0.5 * pre)
                act = root_two * (pre * (0.2 + 0.8 * sigma))
                slope = root_two * (0.2 + 0.8 * sigma * (1.0 + pre * (1.0 - sigma)))
                value = back[phase % 2, rows, :]
                grad = value * wide(cols[1, rows, :]) * slope
                field[phase, rows, here] = (grad * scale).astype(BF)
                add_sums(sums1, rows, (grad * conv, grad, grad * noise_plain, value * act))

    inner_of(sums1, demod1, inner1)
    load1 = pltpu.make_async_copy(full1, weight, load_sem.at[1])
    load1.start()

    @pl.loop(0, channels // 32)
    def _(i):
        rows = rows_of(i * 32, 32)
        for phase, (row_phase, col_phase) in enumerate(phase_pairs):
            value = field[phase, rows, :]
            for k, r in phase_taps[row_phase]:
                for l, q in phase_taps[col_phase]:
                    copies[3 * k + l, rows, :] = move(value, -r, -q)

    for g in range(3):
        join_quad(1, g)
    for g in range(3):
        for k in (1, 2, 3):
            quad_move(1, g, k).wait_send()
    load1.wait()
    weight_grad(0, lambda t: dot_nt(copies[t], scaled_one[...]), inner1, rows_ref[0:1, :])
    for g in range(3):
        join_depth(1, g)
    turn()

    parts = (x0, x1, x2, x3)
    for n in range(tiles):
        here = slice(n * TILE, (n + 1) * TILE)
        summed = None
        for t in range(9):
            term = dot(weight[t], copies[t, :, here])
            summed = term if summed is None else summed + term
        back[n % 2] = summed
        for k in range(4):
            for i in range(128 // ROWS):
                rows = rows_of(chans[k] * 128 + i * ROWS, ROWS)
                value = back[n % 2, rows, :]
                copies[9, rows, here] = (value * wide(cols[0, rows, :])).astype(BF)
                item = value * parts[k][i * ROWS : (i + 1) * ROWS, here].astype(F32)
                item = item[:, :128] + item[:, 128:]
                sums0[rows, :] = item if n == 0 else sums0[rows, :] + item
    back_moves = [
        remote(copies.at[9, rows_of(chans[k] * 128, 128), :], back_all.at[me],
               back_send.at[k - 1], back_recv.at[k - 1], {"chan": chans[k]})
        for k in (1, 2, 3)
    ]
    for item in back_moves:
        item.start()
    back_own = pltpu.make_async_copy(copies.at[9, rows_of(me * 128, 128), :], back_all.at[me], load_sem.at[2])
    back_own.start()

    for g in range(3):
        join_all(1, g)
    for g in range(3):
        join_quad(0, g)
    for g in range(3):
        join_depth(0, g)
    for g in range(3):
        twin_move(1, g).wait()
    store2 = pltpu.make_async_copy(out2, grad2_out, load_sem.at[1])
    store2.start()
    for g in range(3):
        join_all(0, g)
    for g in range(3):
        twin_move(0, g).wait()
    store1 = pltpu.make_async_copy(out1, grad1_out, load_sem.at[3])
    store1.start()
    for c in (0, 1):
        for g in range(3):
            for k in (1, 2, 3):
                if c == 0:
                    quad_move(c, g, k).wait_send()
                z_move(c, g, k).wait_send()
                all_move(c, g, k).wait_send()
    for item in feat_moves + back_moves:
        item.wait()
    for item in (feat_own, back_own, store2, store1):
        item.wait()


def quad(value, k):
    return lax.ppermute(value, "chan", [(i, i ^ k) for i in range(4)])


def pair(value):
    return lax.ppermute(value, "dp", [(i, i ^ 1) for i in range(8)])


def after(value, *others):
    return lax.optimization_barrier((value,) + others)[0]


def natural(parts, me):
    stacked = jnp.stack(parts)
    stacked = stacked.reshape((2, 2) + stacked.shape[1:])
    stacked = jnp.where(me % 2 == 1, stacked[:, ::-1], stacked)
    stacked = jnp.where(me // 2 == 1, stacked[::-1], stacked)
    return stacked.reshape((4,) + stacked.shape[2:])


def pick(value, index, axis):
    return lax.dynamic_index_in_dim(value, index, axis, keepdims=False)


def to_phases(field):
    lead = field.shape[:-1]
    blocked = field.reshape(lead + (HALF, 2, HALF, 2))
    n = len(lead)
    return blocked.transpose((n + 1, n + 3) + tuple(range(n)) + (n, n + 2)).reshape((4,) + lead + (HALF * HALF,))


def phase_order():
    place = jnp.arange(512)
    row, col = place // SIDE, place % SIDE
    grouped = ((row % 2) * 2 + col % 2) * 128 + (row // 2) * HALF + col // 2
    return (jnp.arange(512)[:, None] == grouped[None, :]).astype(BF)


def image_body(
    feat_in,
    rgb_in,
    latent,
    noise_first,
    noise_second,
    live_count,
    conv_first,
    conv_second,
    style_weight,
    style_bias,
    rgb_weight,
    conv_bias,
    rgb_bias,
    noise_gain,
    feat_grad,
    rgb_grad,
):
    local_ch, images, half_pix = feat_in.shape
    channels = 4 * local_ch
    pixels = feat_grad.shape[2]
    me = lax.axis_index("chan")
    row = lax.axis_index("dp")
    core = row % 2
    depth = row // 2
    to = [jnp.bitwise_xor(me, k) for k in range(4)]
    live_mask = (jnp.arange(images) < live_count[0]).astype(F32)
    live = (me < live_count[0]).astype(F32)
    ids = jnp.stack([me, core]).astype(jnp.int32)
    gains = jnp.concatenate([noise_gain, live[None]])

    styles = jnp.einsum("bw,jwc->bjc", latent, style_weight, precision=precise) + style_bias[None]
    shared = jnp.concatenate([conv_bias, rgb_weight.astype(F32)])
    packs = [jnp.concatenate([pick(styles, to[k], 0), shared]) for k in range(4)]
    packs = [packs[0]] + [quad(packs[k], k) for k in (1, 2, 3)]
    vectors = natural(packs, me).transpose(1, 0, 2).reshape(8, channels)
    style_mine, bias_all, rgb_all = vectors[:3], vectors[3:5], vectors[5:8]
    cols = jnp.broadcast_to(vectors[:5, :, None], (5, channels, 128))
    squares = jnp.pad(style_mine[:2] * style_mine[:2], ((0, 6), (0, 0)))

    x = [pick(feat_in, to[k], 1) for k in range(4)]
    x = [x[0]] + [quad(x[k], k) for k in (1, 2, 3)]

    half_one = lax.dynamic_slice_in_dim(conv_first, core * 64, 64, 1)
    one_others = [quad(half_one, k) for k in (1, 2, 3)]
    one_swapped = [pair(part) for part in one_others]
    grad_by_image = feat_grad.transpose(1, 0, 2)

    noise_one = to_phases(pick(noise_first, me, 0))
    noise_two = to_phases(pick(noise_second, me, 0))
    order = phase_order()
    cot_mine = (pick(rgb_grad, me, 0) * live).astype(BF)
    color_cot = jnp.pad(cot_mine, ((0, 13), (0, 0)))
    color_phases = to_phases(color_cot)
    rgb_rows = jnp.pad((rgb_all * style_mine[2:3]).astype(BF), ((0, 13), (0, 0)))
    rgb_cols = jnp.pad(rgb_all.astype(BF), ((0, 13), (0, 0))).T

    tiles = half_pix // TILE
    vec = ((channels, 128), F32, whole((channels, 128)))
    cols_spec, row_spec, noise_spec = whole(cols.shape), whole(squares.shape), whole(noise_one.shape)
    full_spec = whole((9, channels, channels))
    tile_spec = pl.BlockSpec((4, channels, TILE), lambda j: (0, 0, j))
    field_spec = whole((4, channels, half_pix))
    image_spec = pl.BlockSpec((local_ch, 4 * TILE), lambda j: (0, j))
    x_spec = whole((local_ch, half_pix))

    vmem = pl.BlockSpec(memory_space=pltpu.VMEM)
    field, wide_weight = (4, channels, half_pix), (9, channels, channels)
    (raised, scaled_two, convolved, feat_natural, full_one, full_two, grad_arrived,
     scaled_one, demod_one, demod_two, color, rgb_part) = pl.pallas_call(
        forward_kernel,
        in_specs=[SMEM] + [vmem] * 4 + [ANY] * 9 + [vmem] * 7,
        out_specs=[ANY] * 7 + [vmem] * 5,
        out_shape=[
            jax.ShapeDtypeStruct(shape, dtype)
            for shape, dtype in (
                (field, F32), (field, BF), (field, F32), ((channels, pixels), BF), (wide_weight, BF),
                (wide_weight, BF), ((channels, pixels), BF), ((channels, half_pix), BF), ((channels, 128), F32),
                ((channels, 128), F32), ((16, pixels), F32), ((16, channels), F32),
            )
        ],
        scratch_shapes=[
            pltpu.VMEM(field, F32),
            pltpu.VMEM(field, BF),
            pltpu.VMEM(wide_weight, BF),
            pltpu.VMEM(wide_weight, BF),
            pltpu.VMEM((16, channels, half_pix), BF),
            pltpu.VMEM((2, 4, channels, TILE), F32),
            pltpu.VMEM((2, channels, 4 * TILE), BF),
            pltpu.VMEM((TILE // 128, channels, 512), BF),
            pltpu.SemaphoreType.DMA((8,)),
            pltpu.SemaphoreType.DMA((5,)),
            pltpu.SemaphoreType.DMA((2, 2)),
        ]
        + [pltpu.SemaphoreType.DMA((3,))] * 6,
        compiler_params=pltpu.CompilerParams(vmem_limit_bytes=LIMIT, collective_id=0, has_side_effects=True),
        cost_estimate=pl.CostEstimate(flops=int(50e9), bytes_accessed=12 << 20, transcendentals=0),
    )(gains, *x, conv_first, *one_others, *one_swapped, conv_second, grad_by_image, cols, squares,
      noise_one, noise_two, order, rgb_rows, color_cot)

    feat_all, back_all, grad_one, grad_two, sums_two, sums_one, sums_zero, inner_two, inner_one = pl.pallas_call(
        backward_kernel,
        in_specs=[SMEM] + [ANY] * 7 + [vmem] * 14,
        out_specs=[ANY] * 4 + [vmem] * 5,
        out_shape=[
            jax.ShapeDtypeStruct(shape, dtype)
            for shape, dtype in (
                ((4, local_ch, pixels), BF), ((4, local_ch, half_pix), BF), ((9, local_ch, channels), BF),
                ((9, local_ch, channels), BF), ((3, channels, 128), F32), ((4, channels, 128), F32),
                ((channels, 128), F32), ((channels, 128), F32), ((channels, 128), F32),
            )
        ],
        scratch_shapes=[
            pltpu.VMEM((2, 4, channels, TILE), F32),
            pltpu.VMEM((2, channels, 4 * TILE), BF),
            pltpu.VMEM((16, channels, half_pix), BF),
            pltpu.VMEM(field, BF),
            pltpu.VMEM(wide_weight, BF),
            pltpu.VMEM((2, channels, channels), F32),
            pltpu.VMEM((2, channels, TILE), F32),
        ]
        + [pltpu.VMEM((9, 4, 64, channels), BF)] * 4
        + [pltpu.VMEM((9, 3, 64, channels), BF)] * 2
        + [pltpu.VMEM((9, 64, channels), BF)] * 2
        + [pltpu.VMEM((9, 3, 16, channels), BF)] * 2
        + [pltpu.VMEM((9, local_ch, channels), BF)] * 2
        + [pltpu.SemaphoreType.DMA((4,)), pltpu.SemaphoreType.DMA((2, 2))]
        + [pltpu.SemaphoreType.DMA((3,))] * 4
        + [pltpu.SemaphoreType.DMA((2, 3))] * 2
        + [pltpu.SemaphoreType.DMA((2, 3, 3))] * 6
        + [pltpu.SemaphoreType.DMA((2, 3))] * 2,
        compiler_params=pltpu.CompilerParams(vmem_limit_bytes=LIMIT, collective_id=1, has_side_effects=True),
        cost_estimate=pl.CostEstimate(flops=int(100e9), bytes_accessed=12 << 20, transcendentals=0),
    )(gains, grad_arrived, convolved, raised, scaled_two, full_one, full_two, feat_natural, scaled_one, *x,
      cols, squares, demod_one, demod_two, noise_one, noise_two, order.T, color_phases, rgb_cols)
    feat_out = feat_all.transpose(1, 0, 2)
    feat_in_grad = back_all.transpose(1, 0, 2).astype(F32)
    grad_one, grad_two = grad_one.astype(F32), grad_two.astype(F32)

    lift_matrix = upsample_matrix(HALF)
    color = color[:3]
    shard_pix = pixels // 4
    color = color.reshape(3, 4, shard_pix)
    color = [pick(color, to[k], 1) for k in range(4)]
    color = natural([color[0]] + [quad(color[k], k) for k in (1, 2, 3)], me)
    skip_up = jnp.einsum(
        "up,bkpq,vq->bkuv",
        lift_matrix,
        rgb_in.reshape(images, 3, HALF, HALF),
        lift_matrix,
        precision=precise,
    ).reshape(images, 3, pixels)
    skip_mine = lax.dynamic_slice_in_dim(skip_up, me * shard_pix, shard_pix, 2)
    rgb_out = (color + rgb_bias[None, :, None] + skip_mine) * live_mask[:, None, None]
    rgb_cot = rgb_grad * live_mask[:, None, None]
    rgb_in_grad = jnp.einsum(
        "up,bkuv,vq->bkpq",
        lift_matrix,
        rgb_cot.reshape(images, 3, SIDE, SIDE),
        lift_matrix,
        precision=precise,
    ).reshape(images, 3, half_pix)
    rgb_bias_part = jnp.sum(rgb_cot, axis=(0, 2))

    sums_two = jnp.sum(sums_two, axis=2)
    sums_one = jnp.sum(sums_one, axis=2)
    sums_zero = jnp.sum(sums_zero, axis=1)
    inner_two, inner_one = inner_two[:, 0], inner_one[:, 0]
    style_two_demod = 2.0 * style_mine[1] * square_back(inner_two, full_two)
    style_one_demod = 2.0 * style_mine[0] * square_back(inner_one, full_one)
    rows_out = jnp.stack(
        [
            sums_zero + style_one_demod,
            sums_one[3] + style_two_demod,
            jnp.sum(rgb_all * rgb_part[:3], axis=0),
            sums_one[1],
            sums_two[1],
            sums_one[2],
            sums_two[2],
        ]
    )
    rows_out = jnp.concatenate([rows_out, rgb_part[:3] * style_mine[2:3]]).reshape(10, 4, local_ch)
    rows_out = [pick(rows_out, to[k], 1) for k in range(4)]
    rows_in = natural([rows_out[0]] + [quad(rows_out[k], k) for k in (1, 2, 3)], me)
    style_grads = rows_in[:, :3]
    latent_part = jnp.einsum("bjc,jwc->bw", style_grads, style_weight, precision=precise)
    latent_grad = latent_part + quad(latent_part, 1) + quad(latent_part, 2) + quad(latent_part, 3)
    extra = jnp.pad(rgb_bias_part[None], ((0, 0), (0, local_ch - 3)))
    gathered = jnp.concatenate([rows_in.reshape(40, local_ch), extra, latent.reshape(16, 128)])
    gathered = lax.all_gather(gathered, "dp")
    every_row = gathered[:, :40].reshape(8, 4, 10, local_ch)
    every_latent = gathered[:, 41:].reshape(8, 4, 512)
    style_weight_grad = jnp.einsum("gbw,gbjc->jwc", every_latent, every_row[:, :, :3], precision=precise)
    summed = jnp.sum(every_row, axis=(0, 1))
    gain_part = jnp.sum(summed[5:7], axis=1)
    gain_grad = lax.psum(gain_part, "chan")
    rgb_bias_grad = jnp.sum(gathered[:, 40, :3], axis=0)
    return (
        feat_out,
        rgb_out,
        feat_in_grad,
        rgb_in_grad,
        latent_grad,
        grad_one,
        grad_two,
        style_weight_grad,
        summed[:3],
        summed[7:10],
        summed[3:5],
        rgb_bias_grad,
        gain_grad,
    )


def square_back(inner, full):
    total = jnp.zeros(full.shape[1:], F32)
    for t in range(9):
        value = full[t].astype(F32)
        total = total + value * value
    return jnp.sum(inner[:, None] * total, axis=0)


def solution(mesh):
    alone = mesh.shape["chan"] == 4 and mesh.shape["dp"] == 8
    return jax.shard_map(
        image_body if alone else body,
        mesh=mesh,
        in_specs=(
            P("chan", "dp", None),
            P("dp", None, None),
            P("dp", None),
            P("dp", None),
            P("dp", None),
            P("dp"),
            P(None, "chan", None),
            P(None, "chan", None),
            P(None, None, "chan"),
            P(None, "chan"),
            P(None, "chan"),
            P(None, "chan"),
            P(),
            P(),
            P("chan", "dp", None),
            P("dp", None, None),
        ),
        out_specs=(
            P("chan", "dp", None),
            P("dp", None, "chan"),
            P("chan", "dp", None),
            P("dp", None, None),
            P("dp", None),
            P(None, "chan", None),
            P(None, "chan", None),
            P(None, None, "chan"),
            P(None, "chan"),
            P(None, "chan"),
            P(None, "chan"),
            P(),
            P(),
        ),
        check_vma=False,
    )
```

```python
import functools

import jax
import jax.numpy as jnp
from jax import lax
from jax.experimental import pallas as pl
from jax.experimental.pallas import tpu as pltpu
from jax.sharding import PartitionSpec as P

SIDE = 64
HALF = 32


precise = lax.Precision.HIGHEST
epsilon = 1e-08
root_two = 1.4142135623730951
phase_taps = (((1, 0),), ((2, 0), (0, 1)))
phase_pairs = ((0, 0), (0, 1), (1, 0), (1, 1))


def leaky_silu(value):
    return root_two * (0.2 * value + 0.8 * jax.nn.silu(value))


def leaky_slope(value):
    sigma = jax.nn.sigmoid(value)
    return root_two * (0.2 + 0.8 * sigma * (1.0 + value * (1.0 - sigma)))


def shifted(field, row_shift, col_shift, width):
    cells = field.shape[-1]
    offset = row_shift * width + col_shift
    if offset > 0:
        result = jnp.concatenate(
            [field[..., offset:], jnp.zeros(field.shape[:-1] + (offset,), field.dtype)], axis=-1
        )
    elif offset < 0:
        result = jnp.concatenate(
            [jnp.zeros(field.shape[:-1] + (-offset,), field.dtype), field[..., : cells + offset]],
            axis=-1,
        )
    else:
        result = field
    if col_shift != 0:
        column = jnp.arange(cells) % width
        inside = (column + col_shift >= 0) & (column + col_shift < width)
        result = jnp.where(inside, result, jnp.zeros((), field.dtype))
    return result


def upsample_matrix(half_side):
    rows_out = jnp.arange(2 * half_side)[:, None]
    cols_in = jnp.arange(half_side)[None, :]
    centre = rows_out // 2
    beside = centre - 1 + 2 * (rows_out % 2)
    return (
        jnp.where(cols_in == centre, 0.75, 0.0) + jnp.where(cols_in == beside, 0.25, 0.0)
    ).astype(jnp.float32)


def alternate(phases, half_side):
    stacked = jnp.stack(phases)
    out_rows, batch_count = (stacked.shape[1], stacked.shape[2])
    blocked = stacked.reshape(2, 2, out_rows, batch_count, half_side, half_side)
    return blocked.transpose(2, 3, 4, 0, 5, 1).reshape(
        out_rows, batch_count, 4 * half_side * half_side
    )


def split_phases(field, half_side):
    out_rows, batch_count = (field.shape[0], field.shape[1])
    blocked = field.reshape(out_rows, batch_count, half_side, 2, half_side, 2)
    return [
        blocked[:, :, :, row_phase, :, col_phase].reshape(
            out_rows, batch_count, half_side * half_side
        )
        for row_phase, col_phase in phase_pairs
    ]


def up_conv(inputs, weight, half_side):
    shifted_inputs = {}
    for row_shift in (0, 1):
        for col_shift in (0, 1):
            shifted_inputs[row_shift, col_shift] = shifted(inputs, row_shift, col_shift, half_side)
    phases = []
    for row_phase, col_phase in phase_pairs:
        summed = None
        for row_tap, row_shift in phase_taps[row_phase]:
            for col_tap, col_shift in phase_taps[col_phase]:
                product = jnp.einsum(
                    "oc,cbp->obp",
                    weight[row_tap * 3 + col_tap],
                    shifted_inputs[row_shift, col_shift],
                    preferred_element_type=jnp.float32,
                )
                summed = product if summed is None else summed + product
        phases.append(summed)
    return alternate(phases, half_side)


def phase_grads(grad_field, half_side):
    grad_phases = split_phases(grad_field, half_side)
    shifted_grads = [None] * 9
    for phase_index in range(4):
        row_phase, col_phase = phase_pairs[phase_index]
        for row_tap, row_shift in phase_taps[row_phase]:
            for col_tap, col_shift in phase_taps[col_phase]:
                shifted_grads[row_tap * 3 + col_tap] = shifted(
                    grad_phases[phase_index], -row_shift, -col_shift, half_side
                )
    return shifted_grads


def flat_conv(inputs, weight, width):
    summed = None
    for tap_index in range(9):
        product = jnp.einsum(
            "oc,cbp->obp", weight[tap_index], inputs, preferred_element_type=jnp.float32
        )
        product = shifted(product, tap_index // 3 - 1, tap_index % 3 - 1, width)
        summed = product if summed is None else summed + product
    return summed


def body(
    feat_in,
    rgb_in,
    latent,
    noise_first,
    noise_second,
    live_count,
    conv_first,
    conv_second,
    style_weight,
    style_bias,
    rgb_weight,
    conv_bias,
    rgb_bias,
    noise_gain,
    feat_grad,
    rgb_grad,
):
    local_ch, images, half_pix = feat_in.shape
    pixels = feat_grad.shape[2]
    half_side = HALF
    full_side = SIDE
    chan_rank = lax.axis_index("chan")
    live_mask = (jnp.arange(images) < live_count[0]).astype(jnp.float32)
    styles = (
        jnp.einsum("bw,jwc->jbc", latent, style_weight, precision=precise) + style_bias[:, None, :]
    )
    first_all, second_all = (
        lax.all_gather(styles[0], "chan", axis=1, tiled=True),
        lax.all_gather(styles[1], "chan", axis=1, tiled=True),
    )
    weight_one = conv_first.astype(jnp.float32)
    weight_two = conv_second.astype(jnp.float32)
    squares_one = jnp.sum(weight_one * weight_one, axis=0)
    squares_two = jnp.sum(weight_two * weight_two, axis=0)
    demod_one = lax.rsqrt(
        jnp.dot(first_all * first_all, squares_one.T, precision=precise) + epsilon
    )
    demod_two = lax.rsqrt(
        jnp.dot(second_all * second_all, squares_two.T, precision=precise) + epsilon
    )
    scaled_one = (feat_in.astype(jnp.float32) * styles[0].T[:, :, None]).astype(jnp.bfloat16)
    gathered_one = lax.all_gather(scaled_one, "chan", axis=0, tiled=True)
    raised = up_conv(gathered_one, conv_first, half_side)
    pre_one = (
        raised * demod_one.T[:, :, None]
        + noise_gain[0] * noise_first[None, :, :]
        + conv_bias[0][:, None, None]
    )
    act_one = leaky_silu(pre_one)
    scaled_two = (act_one * styles[1].T[:, :, None]).astype(jnp.bfloat16)
    gathered_two = lax.all_gather(scaled_two, "chan", axis=0, tiled=True)
    convolved = flat_conv(gathered_two, conv_second, full_side)
    pre_two = (
        convolved * demod_two.T[:, :, None]
        + noise_gain[1] * noise_second[None, :, :]
        + conv_bias[1][:, None, None]
    )
    act_two = leaky_silu(pre_two)
    feat_out = (act_two * live_mask[None, :, None]).astype(jnp.bfloat16)
    scaled_rgb = (act_two * styles[2].T[:, :, None]).astype(jnp.bfloat16)
    color_part = jnp.einsum(
        "ko,obp->bkp", rgb_weight, scaled_rgb, preferred_element_type=jnp.float32
    )
    color = lax.psum_scatter(color_part, "chan", scatter_dimension=2, tiled=True)
    shard_pix = color.shape[2]
    lift_matrix = upsample_matrix(half_side)
    skip_up = jnp.einsum(
        "up,bkpq,vq->bkuv",
        lift_matrix,
        rgb_in.reshape(images, 3, half_side, half_side),
        lift_matrix,
        precision=precise,
    ).reshape(images, 3, pixels)
    skip_mine = lax.dynamic_slice_in_dim(skip_up, chan_rank * shard_pix, shard_pix, 2)
    rgb_out = (color + rgb_bias[None, :, None] + skip_mine) * live_mask[:, None, None]
    rgb_cot = rgb_grad * live_mask[:, None, None]
    color_cot = rgb_cot.astype(jnp.bfloat16)
    rgb_in_grad = jnp.einsum(
        "up,bkuv,vq->bkpq",
        lift_matrix,
        rgb_cot.reshape(images, 3, full_side, full_side),
        lift_matrix,
        precision=precise,
    ).reshape(images, 3, half_pix)
    rgb_bias_part = jnp.sum(rgb_cot, axis=(0, 2))
    rgb_weight_part = jnp.einsum(
        "bkp,obp->ko", color_cot, scaled_rgb, preferred_element_type=jnp.float32
    )
    back_rgb = jnp.einsum("ko,bkp->obp", rgb_weight, color_cot, preferred_element_type=jnp.float32)
    style_rgb_grad = jnp.sum(back_rgb * act_two, axis=2).T
    grad_pre_two = (
        feat_grad.astype(jnp.float32) * live_mask[None, :, None]
        + back_rgb * styles[2].T[:, :, None]
    ) * leaky_slope(pre_two)
    cot_two = (grad_pre_two * demod_two.T[:, :, None]).astype(jnp.bfloat16)
    inner_two = (
        -0.5 * demod_two * demod_two * demod_two * jnp.sum(grad_pre_two * convolved, axis=2).T
    )
    taps_two = jnp.stack(
        [
            shifted(cot_two, 1 - tap_index // 3, 1 - tap_index % 3, full_side)
            for tap_index in range(9)
        ]
    )
    squares_two_grad = jnp.dot(inner_two.T, second_all * second_all, precision=precise)
    conv_two_grad = (
        jnp.einsum("tobp,cbp->toc", taps_two, gathered_two, preferred_element_type=jnp.float32)
        + 2.0 * weight_two * squares_two_grad[None]
    )
    style_two_demod = 2.0 * second_all * jnp.dot(inner_two, squares_two, precision=precise)
    columns = conv_second
    back_two = lax.psum_scatter(
        jnp.einsum("toc,tobp->cbp", columns, taps_two, preferred_element_type=jnp.float32),
        "chan",
        scatter_dimension=0,
        tiled=True,
    )
    style_two_conv = jnp.sum(back_two * act_one, axis=2).T
    grad_pre_one = back_two * styles[1].T[:, :, None] * leaky_slope(pre_one)
    cot_one = (grad_pre_one * demod_one.T[:, :, None]).astype(jnp.bfloat16)
    inner_one = -0.5 * demod_one * demod_one * demod_one * jnp.sum(grad_pre_one * raised, axis=2).T
    taps_one = jnp.stack(phase_grads(cot_one, half_side))
    squares_one_grad = jnp.dot(inner_one.T, first_all * first_all, precision=precise)
    conv_one_grad = (
        jnp.einsum("tobp,cbp->toc", taps_one, gathered_one, preferred_element_type=jnp.float32)
        + 2.0 * weight_one * squares_one_grad[None]
    )
    style_one_demod = 2.0 * first_all * jnp.dot(inner_one, squares_one, precision=precise)
    columns = conv_first
    back_one = lax.psum_scatter(
        jnp.einsum("toc,tobp->cbp", columns, taps_one, preferred_element_type=jnp.float32),
        "chan",
        scatter_dimension=0,
        tiled=True,
    )
    feat_in_grad = back_one * styles[0].T[:, :, None]
    style_one_conv = jnp.sum(back_one * feat_in.astype(jnp.float32), axis=2).T
    demod_one_sum, demod_two_sum = (
        lax.psum_scatter(style_one_demod, "chan", scatter_dimension=1, tiled=True),
        lax.psum_scatter(style_two_demod, "chan", scatter_dimension=1, tiled=True),
    )
    style_grads = jnp.stack(
        [style_one_conv + demod_one_sum, style_two_conv + demod_two_sum, style_rgb_grad]
    )
    latent_part = jnp.einsum("jbc,jwc->bw", style_grads, style_weight, precision=precise)
    gain_part = jnp.stack(
        [
            jnp.sum(grad_pre_one * noise_first[None, :, :]),
            jnp.sum(grad_pre_two * noise_second[None, :, :]),
        ]
    )
    latent_grad, gain_chan = lax.psum((latent_part, gain_part), "chan")
    style_weight_part = jnp.einsum("bw,jbc->jwc", latent, style_grads, precision=precise)
    style_bias_part = jnp.sum(style_grads, axis=1)
    conv_bias_part = jnp.stack(
        [jnp.sum(grad_pre_one, axis=(1, 2)), jnp.sum(grad_pre_two, axis=(1, 2))]
    )
    totals = lax.psum(
        (
            conv_one_grad,
            conv_two_grad,
            style_weight_part,
            style_bias_part,
            rgb_weight_part,
            conv_bias_part,
            rgb_bias_part,
            gain_chan,
        ),
        "dp",
    )
    return (feat_out, rgb_out, feat_in_grad, rgb_in_grad, latent_grad) + tuple(totals)


BF = jnp.bfloat16
F32 = jnp.float32
TILE = 256
ROWS = 16
ANY = pl.BlockSpec(memory_space=pl.ANY)
SMEM = pl.BlockSpec(memory_space=pltpu.SMEM)
LIMIT = 60 * 1024 * 1024


def whole(shape):
    return pl.BlockSpec(shape, lambda j: (0,) * len(shape))


def dot(a, b):
    return jnp.dot(a, b, preferred_element_type=F32)


def dot_nt(a, b):
    return lax.dot_general(a, b, (((1,), (1,)), ((), ())), preferred_element_type=F32)


def wide(column):
    return jnp.concatenate([column] * (TILE // 128), axis=1)


def move(field, row_shift, col_shift):
    offset = row_shift * HALF + col_shift
    if offset == 0:
        return field
    cells = field.shape[1]
    lane = lax.broadcasted_iota(jnp.int32, field.shape, 1)
    row, col = lane // HALF, lane % HALF
    inside = (row + row_shift >= 0) & (row + row_shift < HALF)
    inside = inside & (col + col_shift >= 0) & (col + col_shift < HALF)
    rolled = pltpu.roll(field.astype(F32), (-offset) % cells, 1)
    return jnp.where(inside, rolled, 0.0).astype(field.dtype)


def near(parity, step):
    other = (parity + step) % 2
    return other, (parity + step - other) // 2


def copy_index(phase, row_step, col_step):
    a, r = near(phase // 2, row_step)
    b, q = near(phase % 2, col_step)
    return ((a * 2 + b) * 2 + abs(r)) * 2 + abs(q)


def make_copies(source, copies):
    chunk = 32

    @pl.loop(0, source.shape[1] // chunk)
    def _(i):
        rows = pl.ds(pl.multiple_of(i * chunk, chunk), chunk)
        for phase in range(4):
            field = source[phase, rows, :]
            row_sign = 1 if phase // 2 == 0 else -1
            col_sign = 1 if phase % 2 == 0 else -1
            for r in (0, 1):
                for q in (0, 1):
                    copies[(phase * 2 + r) * 2 + q, rows, :] = move(
                        field, row_sign * r, col_sign * q
                    )


def demodulate(full, square_row, demod):
    chunk = 32

    @pl.loop(0, full.shape[1] // chunk)
    def _(i):
        rows = pl.ds(pl.multiple_of(i * chunk, chunk), chunk)
        total = None
        for t in range(9):
            value = full[t, rows, :].astype(F32)
            total = value * value if total is None else total + value * value
        total = jnp.sum(total * square_row, axis=1, keepdims=True)
        demod[rows, :] = jnp.broadcast_to(lax.rsqrt(total + epsilon), (chunk, 128))


def chan_peer(me, k):
    if k == 1:
        return me + 1 - 2 * (me % 2)
    return (me + 2) % 4 if k == 2 else 3 - me


def rows_of(base, size):
    return pl.ds(pl.multiple_of(base, size), size)


def take_rows(packs, rows_ref, cols):
    for d in range(4):
        here = slice(d * 128, (d + 1) * 128)
        pack = packs[d]
        rows_ref[:, here] = pack
        for j in range(3, 8):
            cols[j - 3, here, :] = jnp.broadcast_to(pack[j : j + 1, :], (128, 128)).T


def take_phases(plain, order, stacked, noise, color_phases):
    lanes = 512
    for n in range(plain.shape[1] // lanes):
        here = slice(n * lanes, (n + 1) * lanes)
        value = plain[:, here]
        first = value.astype(BF)
        rest = value - first.astype(F32)
        second = rest.astype(BF)
        third = rest - second.astype(F32)
        part = jnp.concatenate([first.astype(F32), second.astype(F32)], axis=0).astype(BF)
        stacked[:, here] = part
        high = dot(part, order[...])
        low = dot(jnp.concatenate([third, third], axis=0).astype(BF), order[...])
        for phase in range(4):
            grouped = slice(phase * 128, (phase + 1) * 128)
            out = slice(n * 128, (n + 1) * 128)
            color_phases[phase, :, out] = high[:, grouped].astype(BF)
            for i in (0, 1):
                noise[4 * i + phase : 4 * i + phase + 1, out] = (
                    high[3 + i : 4 + i, grouped] + high[11 + i : 12 + i, grouped] + low[3 + i : 4 + i, grouped]
                )


def forward_kernel(gains, pack, x_in, own1, own2, feat_grad, plain, order_back, order,
                   raised_out, scaled_out, conv_out, feat_out, full1_out, full2_out, grad_out,
                   x_all, scaled_one, demod1, demod2, color, rgb_grad, cols, rows_ref, noise, color_phases,
                   raised, scaled, full1, full2, copies, conv_tile, feat_tile, ordered, packs, stacked,
                   load_sem, store_sem, tile_sem, pack_send, pack_recv, x_send, x_recv,
                   w_send, w_recv, swap_send, swap_recv, grad_send, grad_recv):
    me = lax.axis_index("chan")
    row = lax.axis_index("dp")
    core = row % 2
    twin = row + 1 - 2 * core
    mesh_id = pl.DeviceIdType.MESH
    chans = [me] + [chan_peer(me, k) for k in (1, 2, 3)]
    barrier = pltpu.get_barrier_semaphore()
    for k in (1, 2, 3):
        pl.semaphore_signal(barrier, inc=1, device_id={"chan": chans[k]}, device_id_type=mesh_id)
    pl.semaphore_signal(barrier, inc=1, device_id={"dp": twin}, device_id_type=mesh_id)
    pl.semaphore_wait(barrier, 4)

    def remote(source, target, sent, received, where):
        return pltpu.make_async_remote_copy(source, target, sent, received, device_id=where, device_id_type=mesh_id)

    pack_moves = [
        remote(pack.at[chans[k]], packs.at[me], pack_send.at[k - 1], pack_recv.at[k - 1], {"chan": chans[k]})
        for k in (1, 2, 3)
    ]
    x_moves = [
        remote(x_in.at[chans[k]], x_all.at[rows_of(me * 128, 128), :], x_send.at[k - 1], x_recv.at[k - 1],
               {"chan": chans[k]})
        for k in (1, 2, 3)
    ]
    for item in pack_moves + x_moves:
        item.start()

    def half_rows(k):
        return rows_of(chans[k] * 128 + core * 64, 64)

    fulls, owns = (full1, full2), (own1, own2)
    cut = 5

    def near_move(c, k):
        return remote(owns[c].at[:, rows_of(core * 64, 64), :], fulls[c].at[:, half_rows(0), :],
                      w_send.at[c, k - 1], w_recv.at[c, k - 1], {"chan": chans[k]})

    def relay_move(c, k):
        part = fulls[c].at[pl.ds(0, cut) if k == 1 else pl.ds(cut, 9 - cut), half_rows(k), :]
        return remote(part, part, w_send.at[c, 1 + k], w_recv.at[c, 1 + k], {"chan": chans[3 - k]})

    def swap_move(c, k):
        part = fulls[c].at[:, half_rows(k), :]
        return remote(part, part, swap_send.at[c, k - 1], swap_recv.at[c, k - 1], {"dp": twin})

    near = [[near_move(c, k) for k in (1, 2)] for c in (0, 1)]
    relay = [[relay_move(c, k) for k in (1, 2)] for c in (0, 1)]
    swap = [[swap_move(c, k) for k in (1, 2, 3)] for c in (0, 1)]

    for item in near[0]:
        item.start()
    loads = [
        pltpu.make_async_copy(pack.at[me], packs.at[me], load_sem.at[0]),
        pltpu.make_async_copy(x_in.at[me], x_all.at[rows_of(me * 128, 128), :], load_sem.at[1]),
        pltpu.make_async_copy(own1, full1.at[:, rows_of(me * 128, 128), :], load_sem.at[2]),
        pltpu.make_async_copy(own2, full2.at[:, rows_of(me * 128, 128), :], load_sem.at[3]),
    ]
    for item in loads:
        item.start()
    take_phases(plain, order_back, stacked, noise, color_phases)
    loads[0].wait()
    for item in pack_moves:
        item.wait_recv()
    take_rows(packs, rows_ref, cols)
    loads[1].wait()
    for item in x_moves:
        item.wait_recv()

    @pl.loop(0, x_all.shape[0] // 32)
    def _(i):
        rows = rows_of(i * 32, 32)
        style = jnp.concatenate([cols[0, rows, :]] * 8, axis=1)
        value = (x_all[rows, :].astype(F32) * style).astype(BF)
        scaled_one[rows, :] = value
        for r in (0, 1):
            for q in (0, 1):
                copies[2 * r + q, rows, :] = move(value, r, q)

    for k in (0, 1):
        near[0][k].wait_recv()
        relay[0][k].start()
        swap[0][k].start()
    for item in near[1]:
        item.start()
    for item in relay[0]:
        item.wait_recv()
    swap[0][2].start()
    loads[2].wait()
    for item in swap[0]:
        item.wait_recv()
    store1 = pltpu.make_async_copy(full1, full1_out, store_sem.at[0])
    store1.start()
    demodulate(full1, rows_ref[3:4, :] * rows_ref[3:4, :], demod1)

    grad_moves = [
        remote(feat_grad.at[chans[k]], grad_out.at[rows_of(me * 128, 128), :], grad_send.at[k - 1], grad_recv.at[k - 1],
               {"chan": chans[k]})
        for k in (1, 2, 3)
    ]
    local3 = pltpu.make_async_copy(feat_grad.at[me], grad_out.at[rows_of(me * 128, 128), :], store_sem.at[4])

    @pl.loop(0, raised.shape[2] // TILE)
    def _(j):
        here = rows_of(j * TILE, TILE)
        for phase, (row_phase, col_phase) in enumerate(phase_pairs):
            total = None
            for k, r in phase_taps[row_phase]:
                for l, q in phase_taps[col_phase]:
                    term = dot(full1[3 * k + l], copies[2 * r + q, :, here])
                    total = term if total is None else total + term
            raised[phase, :, here] = total
            noise_row = gains[0] * noise[phase : phase + 1, here]
            for i in range(raised.shape[1] // ROWS):
                rows = slice(i * ROWS, (i + 1) * ROWS)
                pre = raised[phase, rows, here] * wide(demod1[rows, :]) + noise_row + wide(cols[3, rows, :])
                act = pre * (0.6 * root_two + 0.4 * root_two * jnp.tanh(0.5 * pre))
                scaled[phase, rows, here] = (act * wide(cols[1, rows, :])).astype(BF)

        @pl.when(j == 1)
        def _():
            for k in (0, 1):
                near[1][k].wait_recv()
                relay[1][k].start()
                swap[1][k].start()
            for item in grad_moves:
                item.start()
            local3.start()

    stores = [
        pltpu.make_async_copy(raised, raised_out, store_sem.at[1]),
        pltpu.make_async_copy(scaled, scaled_out, store_sem.at[2]),
    ]
    for item in stores:
        item.start()
    make_copies(scaled, copies)
    for item in relay[1]:
        item.wait_recv()
    swap[1][2].start()
    loads[3].wait()
    for item in swap[1]:
        item.wait_recv()
    store2 = pltpu.make_async_copy(full2, full2_out, store_sem.at[3])
    store2.start()
    demodulate(full2, rows_ref[4:5, :] * rows_ref[4:5, :], demod2)
    rgb_rows = jnp.concatenate([rows_ref[...] * rows_ref[5:6, :]] * 2, axis=0).astype(BF)
    live = gains[2]
    rgb_grad[...] = jnp.zeros_like(rgb_grad)

    def tile_stores(j, slot):
        return (
            pltpu.make_async_copy(conv_tile.at[slot], conv_out.at[:, :, rows_of(j * TILE, TILE)], tile_sem.at[0, slot]),
            pltpu.make_async_copy(feat_tile.at[slot], feat_out.at[:, rows_of(j * 4 * TILE, 4 * TILE)], tile_sem.at[1, slot]),
        )

    @pl.loop(0, raised.shape[2] // TILE)
    def _(j):
        here = rows_of(j * TILE, TILE)
        slot = j % 2

        @pl.when(j >= 2)
        def _():
            for item in tile_stores(j - 2, slot):
                item.wait()

        for phase in range(4):
            total = None
            for t in range(9):
                term = dot(full2[t], copies[copy_index(phase, t // 3 - 1, t % 3 - 1), :, here])
                total = term if total is None else total + term
            conv_tile[slot, phase] = total
            noise_row = gains[1] * noise[4 + phase : 5 + phase, here]
            for i in range(raised.shape[1] // ROWS):
                rows = slice(i * ROWS, (i + 1) * ROWS)
                pre = conv_tile[slot, phase, rows, :] * wide(demod2[rows, :]) + noise_row + wide(cols[4, rows, :])
                act = pre * (0.6 * root_two + 0.4 * root_two * jnp.tanh(0.5 * pre))
                out = (act * live).astype(BF)
                for half in range(TILE // 128):
                    ordered[half, rows, phase * 128 : (phase + 1) * 128] = out[:, half * 128 : (half + 1) * 128]
        for half in range(TILE // 128):
            image = dot(ordered[half], order[...]).astype(BF)
            feat_tile[slot, :, half * 512 : (half + 1) * 512] = image
            pixels = rows_of(j * 4 * TILE + half * 512, 512)
            color[:, pixels] = dot(rgb_rows, image)
            rgb_grad[...] += dot_nt(stacked[:, pixels], image)
        for item in tile_stores(j, slot):
            item.start()

    for j in (2, 3):
        for item in tile_stores(j, j % 2):
            item.wait()
    for item in [store1, store2, local3] + stores:
        item.wait()
    for item in pack_moves + x_moves + near[0] + near[1] + relay[0] + relay[1] + swap[0] + swap[1]:
        item.wait_send()
    for item in grad_moves:
        item.wait()


def backward_kernel(gains, arrived, convolved, raised, scaled_two, full1, full2, feat_natural,
                    scaled_one, x_all, cols, rows_ref, demod1, demod2, noise, order, color_phases, rgb_grad,
                    style_weight, shared, color,
                    feat_all, back_all, grad1_out, grad2_out, every, every_shared, latent_grad, color_in,
                    sums2, sums1, sums0, inner2, inner1, style_sums, vectors, owned, latent_in, tile, grad_tile, copies, field, weight, total, back,
                    keep, send, core1, core2, quad1, quad2, zsum1, zsum2, zin1, zin2, out1, out2,
                    load_sem, tile_sem, feat_send, feat_recv, back_send, back_recv, core_send, core_recv,
                    quad_send, quad_recv, z_send, z_recv, all_send, all_recv, twin_send, twin_recv,
                    shared_send, shared_recv, every_send, every_recv, owned_send, owned_recv, latent_send, latent_recv, color_send, color_recv):
    me = lax.axis_index("chan")
    row = lax.axis_index("dp")
    core = row % 2
    depth = row // 2
    twin = row + 1 - 2 * core
    mesh_id = pl.DeviceIdType.MESH
    chans = [me] + [chan_peer(me, k) for k in (1, 2, 3)]
    depths = [depth] + [chan_peer(depth, k) for k in (1, 2, 3)]
    barrier = pltpu.get_barrier_semaphore()
    for k in (1, 2, 3):
        pl.semaphore_signal(barrier, inc=1, device_id={"chan": chans[k]}, device_id_type=mesh_id)
    lines = [depths[k] * 2 + core for k in (1, 2, 3)] + [twin] + [depths[k] * 2 + 1 - core for k in (1, 2, 3)]
    for line in lines:
        pl.semaphore_signal(barrier, inc=1, device_id={"dp": line}, device_id_type=mesh_id)
    pl.semaphore_wait(barrier, 10)

    def remote(source, target, sent, received, where):
        return pltpu.make_async_remote_copy(source, target, sent, received, device_id=where, device_id_type=mesh_id)

    shared_moves = [
        remote(shared, every_shared.at[row], shared_send.at[i], shared_recv.at[i], {"dp": line})
        for i, line in enumerate(lines)
    ]
    for item in shared_moves:
        item.start()
    every_shared[row] = shared[...]

    quarter = color.shape[1] // 4
    color_moves = [
        remote(color.at[0:8, rows_of(chans[k] * quarter, quarter)], color_in.at[me],
               color_send.at[k - 1], color_recv.at[k - 1], {"chan": chans[k]})
        for k in (1, 2, 3)
    ]
    for item in color_moves:
        item.start()
    color_own = pltpu.make_async_copy(color.at[0:8, rows_of(me * quarter, quarter)], color_in.at[me], load_sem.at[9])
    color_own.start()

    feat_moves = [
        remote(feat_natural.at[rows_of(chans[k] * 128, 128), :], feat_all.at[me],
               feat_send.at[k - 1], feat_recv.at[k - 1], {"chan": chans[k]})
        for k in (1, 2, 3)
    ]
    for item in feat_moves:
        item.start()
    feat_own = pltpu.make_async_copy(feat_natural.at[rows_of(me * 128, 128), :], feat_all.at[me], load_sem.at[0])
    feat_own.start()
    load2 = pltpu.make_async_copy(full2, weight, load_sem.at[1])
    load2.start()
    load_field = pltpu.make_async_copy(scaled_two, field, load_sem.at[2])
    load_field.start()

    def tiles_in(source, j, slot):
        return pltpu.make_async_copy(source.at[:, :, rows_of(j * TILE, TILE)], tile.at[slot], tile_sem.at[0, slot])

    def grads_in(j, slot):
        return pltpu.make_async_copy(
            arrived.at[:, rows_of(j * 4 * TILE, 4 * TILE)], grad_tile.at[slot], tile_sem.at[1, slot]
        )

    tiles_in(convolved, 0, 0).start()
    grads_in(0, 0).start()
    live = gains[2]
    channels = cols.shape[1]
    tiles = copies.shape[2] // TILE
    sums2[...] = jnp.zeros_like(sums2)
    sums1[...] = jnp.zeros_like(sums1)
    style_sums[...] = jnp.zeros_like(style_sums)
    is_color = lax.broadcasted_iota(jnp.int32, (16, channels), 0) < 3
    rgb_rows = jnp.where(is_color, jnp.concatenate([rows_ref[...]] * 2, axis=0), 0.0).astype(BF)

    def add_sums(sums, rows, values):
        for n, value in enumerate(values):
            sums[n, rows, :] += value[:, :128] + value[:, 128:]

    @pl.loop(0, tiles)
    def _(j):
        slot = j % 2

        @pl.when(j + 1 < tiles)
        def _():
            tiles_in(convolved, j + 1, 1 - slot).start()
            grads_in(j + 1, 1 - slot).start()

        tiles_in(convolved, j, slot).wait()
        grads_in(j, slot).wait()
        here = rows_of(j * TILE, TILE)
        for half in range(TILE // 128):
            total[half] = dot(grad_tile[slot, :, half * 512 : (half + 1) * 512], order[...])
        for phase in range(4):
            noise_plain = noise[4 + phase : 5 + phase, here]
            noise_row = gains[1] * noise_plain
            back[phase % 2] = lax.dot_general(
                rgb_rows, color_phases[phase, :, here], (((0,), (0,)), ((), ())), preferred_element_type=F32
            )
            for i in range(channels // ROWS):
                rows = slice(i * ROWS, (i + 1) * ROWS)
                conv = tile[slot, phase, rows, :]
                scale = wide(demod2[rows, :])
                pre = conv * scale + noise_row + wide(cols[4, rows, :])
                sigma = 0.5 + 0.5 * jnp.tanh(0.5 * pre)
                slope = root_two * (0.2 + 0.8 * sigma * (1.0 + pre * (1.0 - sigma)))
                grad_feat = jnp.concatenate(
                    [total[half, rows, phase * 128 : (phase + 1) * 128] for half in range(TILE // 128)], axis=1
                )
                grad = (grad_feat * live + back[phase % 2, rows, :] * wide(cols[2, rows, :])) * slope
                copies[4 * phase, rows, here] = (grad * scale).astype(BF)
                add_sums(sums2, rows, (grad * conv, grad, grad * noise_plain))

    tiles_in(raised, 0, 0).start()
    late = [
        pltpu.make_async_copy(scaled_one, grad_tile.at[0], load_sem.at[4]),
        pltpu.make_async_copy(x_all, grad_tile.at[1], load_sem.at[5]),
    ]
    for item in late:
        item.start()

    def inner_of(sums, demod, inner):
        scale = demod[...]
        inner[...] = -0.5 * scale * scale * scale * jnp.sum(sums[0], axis=1, keepdims=True)

    inner_of(sums2, demod2, inner2)

    def spread_copies():
        chunk = 32

        @pl.loop(0, channels // chunk)
        def _(i):
            rows = rows_of(i * chunk, chunk)
            for phase in range(4):
                value = copies[4 * phase, rows, :]
                row_sign = 1 if phase // 2 == 0 else -1
                col_sign = 1 if phase % 2 == 0 else -1
                for r, q in ((0, 1), (1, 0), (1, 1)):
                    copies[4 * phase + 2 * r + q, rows, :] = move(value, row_sign * r, col_sign * q)

    spread_copies()
    load2.wait()
    load_field.wait()

    def split(c, slot, t, inner, square_row):
        for k in range(4):
            base = chans[k] * 128
            for out, start in ((keep, base + core * 64), (send, base + 64 - core * 64)):
                rows = rows_of(start, 64)
                column = jnp.concatenate([inner[rows, :]] * 4, axis=1)
                plain = weight[t, rows, :].astype(F32)
                scaled = plain * column
                out[t, k] = (total[slot, rows, :] + scaled * square_row).astype(BF)
                scaled = plain * scaled
                style_sums[c] += sum(scaled[i * 8 : (i + 1) * 8, :] for i in range(8))

    cores, quads, zsums, zins, outs = (core1, core2), (quad1, quad2), (zsum1, zsum2), (zin1, zin2), (out1, out2)

    def taps(g):
        return pl.ds(3 * g, 3)

    def core_move(c, g):
        return remote(send.at[taps(g)], cores[c].at[taps(g)], core_send.at[c, g], core_recv.at[c, g], {"dp": twin})

    def quad_move(c, g, k):
        return remote(keep.at[taps(g), k], quads[c].at[taps(g), k - 1], quad_send.at[c, g, k - 1],
                      quad_recv.at[c, g, k - 1], {"chan": chans[k]})

    def z_move(c, g, k):
        return remote(zsums[c].at[taps(g), rows_of(depths[k] * 16, 16), :], zins[c].at[taps(g), k - 1],
                      z_send.at[c, g, k - 1], z_recv.at[c, g, k - 1], {"dp": depths[k] * 2 + core})

    def all_move(c, g, k):
        part = outs[c].at[taps(g), rows_of(core * 64 + depth * 16, 16), :]
        return remote(part, part, all_send.at[c, g, k - 1], all_recv.at[c, g, k - 1], {"dp": depths[k] * 2 + core})

    def twin_move(c, g):
        part = outs[c].at[taps(g), rows_of(core * 64, 64), :]
        return remote(part, part, twin_send.at[c, g], twin_recv.at[c, g], {"dp": twin})

    def join_cores(c, g):
        core_move(c, g).wait_recv()
        for i in range(3):
            t = 3 * g + i
            for k in range(4):
                keep[t, k] = (keep[t, k].astype(F32) + cores[c][t, k].astype(F32)).astype(BF)
        for k in (1, 2, 3):
            quad_move(c, g, k).start()

    def join_quad(c, g):
        for k in (1, 2, 3):
            quad_move(c, g, k).wait_recv()
        for i in range(3):
            t = 3 * g + i
            value = keep[t, 0].astype(F32)
            for k in range(3):
                value = value + quads[c][t, k].astype(F32)
            zsums[c][t] = value.astype(BF)
        for k in (1, 2, 3):
            z_move(c, g, k).start()

    def join_depth(c, g):
        for k in (1, 2, 3):
            z_move(c, g, k).wait_recv()
        for i in range(3):
            t = 3 * g + i
            value = zsums[c][t, rows_of(depth * 16, 16), :].astype(F32)
            for k in range(3):
                value = value + zins[c][t, k].astype(F32)
            outs[c][t, rows_of(core * 64 + depth * 16, 16), :] = value.astype(BF)
        for k in (1, 2, 3):
            all_move(c, g, k).start()

    def join_all(c, g):
        for k in (1, 2, 3):
            all_move(c, g, k).wait_recv()
        twin_move(c, g).start()

    def weight_grad(c, product, inner, square_row):
        @pl.loop(0, 3)
        def _(g):
            t = 3 * g
            total[0] = product(t)
            total[1] = product(t + 1)
            split(c, 0, t, inner, square_row)
            total[0] = product(t + 2)
            split(c, 1, t + 1, inner, square_row)
            split(c, 0, t + 2, inner, square_row)
            core_move(c, g).start()

            @pl.when(g >= 1)
            def _():
                join_cores(c, g - 1)

        join_cores(c, 2)
        for g in range(3):
            core_move(c, g).wait_send()

    def second_product(t):
        row_step, col_step = 1 - t // 3, 1 - t % 3
        summed = None
        for phase in range(4):
            a, b = phase // 2, phase % 2
            far_row = (row_step * (2 * a - 1) + 1) // 2 * (row_step * row_step)
            far_col = (col_step * (2 * b - 1) + 1) // 2 * (col_step * col_step)
            index = (((a + row_step + 2) % 2 * 2 + (b + col_step + 2) % 2) * 2 + far_row) * 2 + far_col
            term = dot_nt(copies[index], field[phase])
            summed = term if summed is None else summed + term
        return summed

    weight_grad(1, second_product, inner2, 2.0 * rows_ref[4:5, :] * rows_ref[4:5, :])

    def turn():
        @pl.loop(0, 9)
        def _(t):
            weight[t] = weight[t].T

    turn()

    @pl.loop(0, tiles)
    def _(j):
        slot = j % 2

        @pl.when(j + 1 < tiles)
        def _():
            tiles_in(raised, j + 1, 1 - slot).start()

        tiles_in(raised, j, slot).wait()
        here = rows_of(j * TILE, TILE)
        for phase in range(4):
            summed = None
            for t in range(9):
                term = dot(weight[t], copies[copy_index(phase, 1 - t // 3, 1 - t % 3), :, here])
                summed = term if summed is None else summed + term
            back[phase % 2] = summed
            noise_plain = noise[phase : phase + 1, here]
            noise_row = gains[0] * noise_plain
            for i in range(channels // ROWS):
                rows = slice(i * ROWS, (i + 1) * ROWS)
                conv = tile[slot, phase, rows, :]
                scale = wide(demod1[rows, :])
                pre = conv * scale + noise_row + wide(cols[3, rows, :])
                sigma = 0.5 + 0.5 * jnp.tanh(0.5 * pre)
                act = root_two * (pre * (0.2 + 0.8 * sigma))
                slope = root_two * (0.2 + 0.8 * sigma * (1.0 + pre * (1.0 - sigma)))
                value = back[phase % 2, rows, :]
                grad = value * wide(cols[1, rows, :]) * slope
                field[phase, rows, here] = (grad * scale).astype(BF)
                add_sums(sums1, rows, (grad * conv, grad, grad * noise_plain, value * act))

        @pl.when(j == 2)
        def _():
            join_quad(1, 0)
            join_quad(1, 1)

    inner_of(sums1, demod1, inner1)
    load1 = pltpu.make_async_copy(full1, weight, load_sem.at[1])
    load1.start()

    @pl.loop(0, channels // 32)
    def _(i):
        rows = rows_of(i * 32, 32)
        for phase, (row_phase, col_phase) in enumerate(phase_pairs):
            value = field[phase, rows, :]
            for k, r in phase_taps[row_phase]:
                for l, q in phase_taps[col_phase]:
                    copies[3 * k + l, rows, :] = move(value, -r, -q)

    join_quad(1, 2)
    for g in range(3):
        for k in (1, 2, 3):
            quad_move(1, g, k).wait_send()
    load1.wait()
    for item in late:
        item.wait()
    weight_grad(0, lambda t: dot_nt(copies[t], grad_tile[0]), inner1, 2.0 * rows_ref[3:4, :] * rows_ref[3:4, :])
    style_loads = [
        pltpu.make_async_copy(style_weight.at[j], total.at[0, :, j * 128 : (j + 1) * 128], load_sem.at[6 + j])
        for j in range(3)
    ]
    for item in style_loads:
        item.start()
    for g in range(3):
        join_depth(1, g)
    turn()

    for n in range(tiles):
        here = slice(n * TILE, (n + 1) * TILE)
        summed = None
        for t in range(9):
            term = dot(weight[t], copies[t, :, here])
            summed = term if summed is None else summed + term
        back[n % 2] = summed
        for i in range(channels // ROWS):
            rows = slice(i * ROWS, (i + 1) * ROWS)
            value = back[n % 2, rows, :]
            copies[9, rows, here] = (value * wide(cols[0, rows, :])).astype(BF)
            item = value * grad_tile[1, rows, here].astype(F32)
            item = item[:, :128] + item[:, 128:]
            sums0[rows, :] = item if n == 0 else sums0[rows, :] + item
        if n == 1:
            join_quad(0, 0)
    back_moves = [
        remote(copies.at[9, rows_of(chans[k] * 128, 128), :], back_all.at[me],
               back_send.at[k - 1], back_recv.at[k - 1], {"chan": chans[k]})
        for k in (1, 2, 3)
    ]
    for item in back_moves:
        item.start()
    back_own = pltpu.make_async_copy(copies.at[9, rows_of(me * 128, 128), :], back_all.at[me], load_sem.at[2])
    back_own.start()

    def as_row(sums):
        return jnp.sum(sums[...].T, axis=0, keepdims=True)

    style_two, style_one = as_row(sums1.at[3]), as_row(sums0)
    color_grad = rgb_grad[0:8, :]
    vector_rows = [
        style_one + 2.0 * rows_ref[3:4, :] * jnp.sum(style_sums[0], axis=0, keepdims=True),
        style_two + 2.0 * rows_ref[4:5, :] * jnp.sum(style_sums[1], axis=0, keepdims=True),
        sum(rows_ref[k : k + 1, :] * color_grad[k : k + 1, :] for k in range(3)),
        as_row(sums1.at[1]),
        as_row(sums2.at[1]),
        jnp.broadcast_to(jnp.sum(as_row(sums1.at[2]), axis=1, keepdims=True), (1, channels)),
        jnp.broadcast_to(jnp.sum(as_row(sums2.at[2]), axis=1, keepdims=True), (1, channels)),
        jnp.zeros((1, channels), F32),
    ]
    for i, value in enumerate(vector_rows):
        for d in range(4):
            vectors[d, i : i + 1, :] = value[:, d * 128 : (d + 1) * 128]
    color_grad = color_grad * rows_ref[5:6, :]
    for d in range(4):
        vectors[d, 8:16, :] = color_grad[:, d * 128 : (d + 1) * 128]
    owned_moves = [
        remote(vectors.at[chans[k]], owned.at[me], owned_send.at[k - 1], owned_recv.at[k - 1], {"chan": chans[k]})
        for k in (1, 2, 3)
    ]
    for item in owned_moves:
        item.start()
    owned[me] = vectors[me]

    for g in range(3):
        join_all(1, g)
    join_quad(0, 1)
    join_depth(0, 0)
    for item in owned_moves:
        item.wait_recv()
    for item in style_loads:
        item.wait()
    latent_part = None
    for j in range(3):
        value = jnp.concatenate([owned[d, j : j + 1, :] for d in range(4)] + [jnp.zeros((4, 128), F32)], axis=0)
        term = lax.dot_general(
            value, total[0, :, j * 128 : (j + 1) * 128], (((1,), (1,)), ((), ())), precision=precise, preferred_element_type=F32
        )
        latent_part = term if latent_part is None else latent_part + term
    latent_in[3] = latent_part
    latent_moves = [
        remote(latent_in.at[3], latent_in.at[k - 1], latent_send.at[k - 1], latent_recv.at[k - 1], {"chan": chans[k]})
        for k in (1, 2, 3)
    ]
    every_moves = [
        remote(owned, every.at[row], every_send.at[i], every_recv.at[i], {"dp": line})
        for i, line in enumerate(lines)
    ]
    for item in latent_moves + every_moves:
        item.start()
    every[row] = owned[...]
    join_quad(0, 2)
    join_depth(0, 1)
    join_all(0, 0)
    join_depth(0, 2)
    join_all(0, 1)
    for g in range(3):
        twin_move(1, g).wait()
    store2 = pltpu.make_async_copy(out2, grad2_out, load_sem.at[1])
    store2.start()
    join_all(0, 2)
    for item in latent_moves:
        item.wait_recv()
    latent_grad[...] = latent_in[0] + latent_in[1] + latent_in[2] + latent_in[3]
    for g in range(3):
        twin_move(0, g).wait()
    store1 = pltpu.make_async_copy(out1, grad1_out, load_sem.at[3])
    store1.start()
    for c in (0, 1):
        for g in range(3):
            for k in (1, 2, 3):
                if c == 0:
                    quad_move(c, g, k).wait_send()
                z_move(c, g, k).wait_send()
                all_move(c, g, k).wait_send()
    for item in feat_moves + back_moves + shared_moves + every_moves + color_moves:
        item.wait()
    for item in owned_moves + latent_moves:
        item.wait_send()
    for item in (feat_own, back_own, color_own, store2, store1):
        item.wait()


def pick(value, index, axis):
    return lax.dynamic_index_in_dim(value, index, axis, keepdims=False)


def phase_order():
    place = jnp.arange(512)
    row, col = place // SIDE, place % SIDE
    grouped = ((row % 2) * 2 + col % 2) * 128 + (row // 2) * HALF + col // 2
    return (jnp.arange(512)[:, None] == grouped[None, :]).astype(BF)


def image_body(
    feat_in,
    rgb_in,
    latent,
    noise_first,
    noise_second,
    live_count,
    conv_first,
    conv_second,
    style_weight,
    style_bias,
    rgb_weight,
    conv_bias,
    rgb_bias,
    noise_gain,
    feat_grad,
    rgb_grad,
):
    local_ch, images, half_pix = feat_in.shape
    channels = 4 * local_ch
    pixels = feat_grad.shape[2]
    me = lax.axis_index("chan")
    live_mask = (jnp.arange(images) < live_count[0]).astype(F32)
    live = (me < live_count[0]).astype(F32)
    gains = jnp.concatenate([noise_gain, live[None]])
    styles = jnp.einsum("bw,jwc->bjc", latent, style_weight, precision=precise) + style_bias[None]

    def each_image(value):
        return jnp.broadcast_to(value[None], (images,) + value.shape)

    pack = jnp.concatenate([each_image(rgb_weight.astype(F32)), styles, each_image(conv_bias)], axis=1)
    plain = jnp.concatenate(
        [pick(rgb_grad, me, 0) * live, pick(noise_first, me, 0)[None], pick(noise_second, me, 0)[None],
         jnp.zeros((3, pixels), F32)]
    )
    x_by_image = feat_in.transpose(1, 0, 2)
    grad_by_image = feat_grad.transpose(1, 0, 2)
    order = phase_order()

    vmem = pl.BlockSpec(memory_space=pltpu.VMEM)
    field, wide_weight = (4, channels, half_pix), (9, channels, channels)
    vector = ((channels, 128), F32)
    forward_outs = (
        (field, F32), (field, BF), (field, F32), ((channels, pixels), BF), (wide_weight, BF), (wide_weight, BF),
        ((channels, pixels), BF), ((channels, half_pix), BF), ((channels, half_pix), BF), vector, vector,
        ((16, pixels), F32), ((16, channels), F32), ((5, channels, 128), F32), ((8, channels), F32),
        ((8, half_pix), F32), ((4, 16, half_pix), BF),
    )
    (raised, scaled_two, convolved, feat_natural, full_one, full_two, grad_arrived,
     x_all, scaled_one, demod_one, demod_two, color, rgb_part, cols, row_vectors, noise, color_phases) = pl.pallas_call(
        forward_kernel,
        in_specs=[SMEM, ANY, ANY, ANY, ANY, ANY, vmem, vmem, vmem],
        out_specs=[ANY] * 7 + [vmem] * 10,
        out_shape=[jax.ShapeDtypeStruct(shape, dtype) for shape, dtype in forward_outs],
        scratch_shapes=[
            pltpu.VMEM(field, F32),
            pltpu.VMEM(field, BF),
            pltpu.VMEM(wide_weight, BF),
            pltpu.VMEM(wide_weight, BF),
            pltpu.VMEM((16, channels, half_pix), BF),
            pltpu.VMEM((2, 4, channels, TILE), F32),
            pltpu.VMEM((2, channels, 4 * TILE), BF),
            pltpu.VMEM((TILE // 128, channels, 512), BF),
            pltpu.VMEM((4, 8, 128), F32),
            pltpu.VMEM((16, pixels), BF),
            pltpu.SemaphoreType.DMA((4,)),
            pltpu.SemaphoreType.DMA((5,)),
            pltpu.SemaphoreType.DMA((2, 2)),
        ]
        + [pltpu.SemaphoreType.DMA((3,))] * 4
        + [pltpu.SemaphoreType.DMA((2, 4))] * 2
        + [pltpu.SemaphoreType.DMA((2, 3))] * 2
        + [pltpu.SemaphoreType.DMA((3,))] * 2,
        compiler_params=pltpu.CompilerParams(vmem_limit_bytes=LIMIT, collective_id=0, has_side_effects=True),
        cost_estimate=pl.CostEstimate(flops=int(50e9), bytes_accessed=12 << 20, transcendentals=0),
    )(gains, pack, x_by_image, conv_first, conv_second, grad_by_image, plain, order.T, order)

    rgb_cot = rgb_grad * live_mask[:, None, None]
    rgb_bias_part = jnp.sum(rgb_cot, axis=(0, 2))
    shared = jnp.concatenate([latent, jnp.broadcast_to(jnp.pad(rgb_bias_part, (0, 509))[None], (4, 512))])
    backward_outs = (
        ((4, local_ch, pixels), BF), ((4, local_ch, half_pix), BF), ((9, local_ch, channels), BF),
        ((9, local_ch, channels), BF), ((8, 4, 16, 128), F32), ((8, 8, 512), F32), ((8, 512), F32),
        ((4, 8, pixels // 4), F32),
    )
    feat_all, back_all, grad_one, grad_two, every, every_shared, latent_grad, color_in = pl.pallas_call(
        backward_kernel,
        in_specs=[SMEM] + [ANY] * 9 + [vmem] * 8 + [ANY, vmem, ANY],
        out_specs=[ANY] * 4 + [vmem] * 3 + [ANY],
        out_shape=[jax.ShapeDtypeStruct(shape, dtype) for shape, dtype in backward_outs],
        scratch_shapes=[
            pltpu.VMEM((3, channels, 128), F32),
            pltpu.VMEM((4, channels, 128), F32),
            pltpu.VMEM((channels, 128), F32),
            pltpu.VMEM((channels, 128), F32),
            pltpu.VMEM((channels, 128), F32),
            pltpu.VMEM((2, 8, channels), F32),
            pltpu.VMEM((4, 16, 128), F32),
            pltpu.VMEM((4, 16, 128), F32),
            pltpu.VMEM((4, 8, 512), F32),
            pltpu.VMEM((2, 4, channels, TILE), F32),
            pltpu.VMEM((2, channels, 4 * TILE), BF),
            pltpu.VMEM((16, channels, half_pix), BF),
            pltpu.VMEM(field, BF),
            pltpu.VMEM(wide_weight, BF),
            pltpu.VMEM((2, channels, channels), F32),
            pltpu.VMEM((2, channels, TILE), F32),
        ]
        + [pltpu.VMEM((9, 4, 64, channels), BF)] * 4
        + [pltpu.VMEM((9, 3, 64, channels), BF)] * 2
        + [pltpu.VMEM((9, 64, channels), BF)] * 2
        + [pltpu.VMEM((9, 3, 16, channels), BF)] * 2
        + [pltpu.VMEM((9, local_ch, channels), BF)] * 2
        + [pltpu.SemaphoreType.DMA((10,)), pltpu.SemaphoreType.DMA((2, 2))]
        + [pltpu.SemaphoreType.DMA((3,))] * 4
        + [pltpu.SemaphoreType.DMA((2, 3))] * 2
        + [pltpu.SemaphoreType.DMA((2, 3, 3))] * 6
        + [pltpu.SemaphoreType.DMA((2, 3))] * 2
        + [pltpu.SemaphoreType.DMA((7,))] * 4
        + [pltpu.SemaphoreType.DMA((3,))] * 6,
        compiler_params=pltpu.CompilerParams(vmem_limit_bytes=LIMIT, collective_id=1, has_side_effects=True),
        cost_estimate=pl.CostEstimate(flops=int(100e9), bytes_accessed=12 << 20, transcendentals=0),
    )(gains, grad_arrived, convolved, raised, scaled_two, full_one, full_two, feat_natural, scaled_one, x_all,
      cols, row_vectors, demod_one, demod_two, noise, order.T, color_phases, rgb_part, style_weight, shared, color)
    feat_out = feat_all.transpose(1, 0, 2)
    feat_in_grad = back_all.transpose(1, 0, 2).astype(F32)
    grad_one, grad_two = grad_one.astype(F32), grad_two.astype(F32)

    lift_matrix = upsample_matrix(HALF)
    shard_pix = pixels // 4
    skip_up = jnp.einsum(
        "up,bkpq,vq->bkuv",
        lift_matrix,
        rgb_in.reshape(images, 3, HALF, HALF),
        lift_matrix,
        precision=precise,
    ).reshape(images, 3, pixels)
    skip_mine = lax.dynamic_slice_in_dim(skip_up, me * shard_pix, shard_pix, 2)
    rgb_out = (color_in[:, :3] + rgb_bias[None, :, None] + skip_mine) * live_mask[:, None, None]
    rgb_in_grad = jnp.einsum(
        "up,bkuv,vq->bkpq",
        lift_matrix,
        rgb_cot.reshape(images, 3, SIDE, SIDE),
        lift_matrix,
        precision=precise,
    ).reshape(images, 3, half_pix)

    summed = jnp.sum(every, axis=(0, 1))
    style_weight_grad = jnp.einsum("gbw,gbjc->jwc", every_shared[:, :4], every[:, :, :3], precision=precise)
    return (
        feat_out,
        rgb_out,
        feat_in_grad,
        rgb_in_grad,
        latent_grad[:4],
        grad_one,
        grad_two,
        style_weight_grad,
        summed[:3],
        summed[8:11],
        summed[3:5],
        jnp.sum(every_shared[:, 4, :3], axis=0),
        summed[5:7, 0],
    )


def solution(mesh):
    alone = mesh.shape["chan"] == 4 and mesh.shape["dp"] == 8
    return jax.shard_map(
        image_body if alone else body,
        mesh=mesh,
        in_specs=(
            P("chan", "dp", None),
            P("dp", None, None),
            P("dp", None),
            P("dp", None),
            P("dp", None),
            P("dp"),
            P(None, "chan", None),
            P(None, "chan", None),
            P(None, None, "chan"),
            P(None, "chan"),
            P(None, "chan"),
            P(None, "chan"),
            P(),
            P(),
            P("chan", "dp", None),
            P("dp", None, None),
        ),
        out_specs=(
            P("chan", "dp", None),
            P("dp", None, "chan"),
            P("chan", "dp", None),
            P("dp", None, None),
            P("dp", None),
            P(None, "chan", None),
            P(None, "chan", None),
            P(None, None, "chan"),
            P(None, "chan"),
            P(None, "chan"),
            P(None, "chan"),
            P(),
            P(),
        ),
        check_vma=False,
    )
```

```python
import functools

import jax
import jax.numpy as jnp
from jax import lax
from jax.experimental import pallas as pl
from jax.experimental.pallas import tpu as pltpu
from jax.sharding import PartitionSpec as P

SIDE = 64
HALF = 32


precise = lax.Precision.HIGHEST
epsilon = 1e-08
root_two = 1.4142135623730951
phase_taps = (((1, 0),), ((2, 0), (0, 1)))
phase_pairs = ((0, 0), (0, 1), (1, 0), (1, 1))


def leaky_silu(value):
    return root_two * (0.2 * value + 0.8 * jax.nn.silu(value))


def leaky_slope(value):
    sigma = jax.nn.sigmoid(value)
    return root_two * (0.2 + 0.8 * sigma * (1.0 + value * (1.0 - sigma)))


def shifted(field, row_shift, col_shift, width):
    cells = field.shape[-1]
    offset = row_shift * width + col_shift
    if offset > 0:
        result = jnp.concatenate(
            [field[..., offset:], jnp.zeros(field.shape[:-1] + (offset,), field.dtype)], axis=-1
        )
    elif offset < 0:
        result = jnp.concatenate(
            [jnp.zeros(field.shape[:-1] + (-offset,), field.dtype), field[..., : cells + offset]],
            axis=-1,
        )
    else:
        result = field
    if col_shift != 0:
        column = jnp.arange(cells) % width
        inside = (column + col_shift >= 0) & (column + col_shift < width)
        result = jnp.where(inside, result, jnp.zeros((), field.dtype))
    return result


def upsample_matrix(half_side):
    rows_out = jnp.arange(2 * half_side)[:, None]
    cols_in = jnp.arange(half_side)[None, :]
    centre = rows_out // 2
    beside = centre - 1 + 2 * (rows_out % 2)
    return (
        jnp.where(cols_in == centre, 0.75, 0.0) + jnp.where(cols_in == beside, 0.25, 0.0)
    ).astype(jnp.float32)


def alternate(phases, half_side):
    stacked = jnp.stack(phases)
    out_rows, batch_count = (stacked.shape[1], stacked.shape[2])
    blocked = stacked.reshape(2, 2, out_rows, batch_count, half_side, half_side)
    return blocked.transpose(2, 3, 4, 0, 5, 1).reshape(
        out_rows, batch_count, 4 * half_side * half_side
    )


def split_phases(field, half_side):
    out_rows, batch_count = (field.shape[0], field.shape[1])
    blocked = field.reshape(out_rows, batch_count, half_side, 2, half_side, 2)
    return [
        blocked[:, :, :, row_phase, :, col_phase].reshape(
            out_rows, batch_count, half_side * half_side
        )
        for row_phase, col_phase in phase_pairs
    ]


def up_conv(inputs, weight, half_side):
    shifted_inputs = {}
    for row_shift in (0, 1):
        for col_shift in (0, 1):
            shifted_inputs[row_shift, col_shift] = shifted(inputs, row_shift, col_shift, half_side)
    phases = []
    for row_phase, col_phase in phase_pairs:
        summed = None
        for row_tap, row_shift in phase_taps[row_phase]:
            for col_tap, col_shift in phase_taps[col_phase]:
                product = jnp.einsum(
                    "oc,cbp->obp",
                    weight[row_tap * 3 + col_tap],
                    shifted_inputs[row_shift, col_shift],
                    preferred_element_type=jnp.float32,
                )
                summed = product if summed is None else summed + product
        phases.append(summed)
    return alternate(phases, half_side)


def phase_grads(grad_field, half_side):
    grad_phases = split_phases(grad_field, half_side)
    shifted_grads = [None] * 9
    for phase_index in range(4):
        row_phase, col_phase = phase_pairs[phase_index]
        for row_tap, row_shift in phase_taps[row_phase]:
            for col_tap, col_shift in phase_taps[col_phase]:
                shifted_grads[row_tap * 3 + col_tap] = shifted(
                    grad_phases[phase_index], -row_shift, -col_shift, half_side
                )
    return shifted_grads


def flat_conv(inputs, weight, width):
    summed = None
    for tap_index in range(9):
        product = jnp.einsum(
            "oc,cbp->obp", weight[tap_index], inputs, preferred_element_type=jnp.float32
        )
        product = shifted(product, tap_index // 3 - 1, tap_index % 3 - 1, width)
        summed = product if summed is None else summed + product
    return summed


def body(
    feat_in,
    rgb_in,
    latent,
    noise_first,
    noise_second,
    live_count,
    conv_first,
    conv_second,
    style_weight,
    style_bias,
    rgb_weight,
    conv_bias,
    rgb_bias,
    noise_gain,
    feat_grad,
    rgb_grad,
):
    local_ch, images, half_pix = feat_in.shape
    pixels = feat_grad.shape[2]
    half_side = HALF
    full_side = SIDE
    chan_rank = lax.axis_index("chan")
    live_mask = (jnp.arange(images) < live_count[0]).astype(jnp.float32)
    styles = (
        jnp.einsum("bw,jwc->jbc", latent, style_weight, precision=precise) + style_bias[:, None, :]
    )
    first_all, second_all = (
        lax.all_gather(styles[0], "chan", axis=1, tiled=True),
        lax.all_gather(styles[1], "chan", axis=1, tiled=True),
    )
    weight_one = conv_first.astype(jnp.float32)
    weight_two = conv_second.astype(jnp.float32)
    squares_one = jnp.sum(weight_one * weight_one, axis=0)
    squares_two = jnp.sum(weight_two * weight_two, axis=0)
    demod_one = lax.rsqrt(
        jnp.dot(first_all * first_all, squares_one.T, precision=precise) + epsilon
    )
    demod_two = lax.rsqrt(
        jnp.dot(second_all * second_all, squares_two.T, precision=precise) + epsilon
    )
    scaled_one = (feat_in.astype(jnp.float32) * styles[0].T[:, :, None]).astype(jnp.bfloat16)
    gathered_one = lax.all_gather(scaled_one, "chan", axis=0, tiled=True)
    raised = up_conv(gathered_one, conv_first, half_side)
    pre_one = (
        raised * demod_one.T[:, :, None]
        + noise_gain[0] * noise_first[None, :, :]
        + conv_bias[0][:, None, None]
    )
    act_one = leaky_silu(pre_one)
    scaled_two = (act_one * styles[1].T[:, :, None]).astype(jnp.bfloat16)
    gathered_two = lax.all_gather(scaled_two, "chan", axis=0, tiled=True)
    convolved = flat_conv(gathered_two, conv_second, full_side)
    pre_two = (
        convolved * demod_two.T[:, :, None]
        + noise_gain[1] * noise_second[None, :, :]
        + conv_bias[1][:, None, None]
    )
    act_two = leaky_silu(pre_two)
    feat_out = (act_two * live_mask[None, :, None]).astype(jnp.bfloat16)
    scaled_rgb = (act_two * styles[2].T[:, :, None]).astype(jnp.bfloat16)
    color_part = jnp.einsum(
        "ko,obp->bkp", rgb_weight, scaled_rgb, preferred_element_type=jnp.float32
    )
    color = lax.psum_scatter(color_part, "chan", scatter_dimension=2, tiled=True)
    shard_pix = color.shape[2]
    lift_matrix = upsample_matrix(half_side)
    skip_up = jnp.einsum(
        "up,bkpq,vq->bkuv",
        lift_matrix,
        rgb_in.reshape(images, 3, half_side, half_side),
        lift_matrix,
        precision=precise,
    ).reshape(images, 3, pixels)
    skip_mine = lax.dynamic_slice_in_dim(skip_up, chan_rank * shard_pix, shard_pix, 2)
    rgb_out = (color + rgb_bias[None, :, None] + skip_mine) * live_mask[:, None, None]
    rgb_cot = rgb_grad * live_mask[:, None, None]
    color_cot = rgb_cot.astype(jnp.bfloat16)
    rgb_in_grad = jnp.einsum(
        "up,bkuv,vq->bkpq",
        lift_matrix,
        rgb_cot.reshape(images, 3, full_side, full_side),
        lift_matrix,
        precision=precise,
    ).reshape(images, 3, half_pix)
    rgb_bias_part = jnp.sum(rgb_cot, axis=(0, 2))
    rgb_weight_part = jnp.einsum(
        "bkp,obp->ko", color_cot, scaled_rgb, preferred_element_type=jnp.float32
    )
    back_rgb = jnp.einsum("ko,bkp->obp", rgb_weight, color_cot, preferred_element_type=jnp.float32)
    style_rgb_grad = jnp.sum(back_rgb * act_two, axis=2).T
    grad_pre_two = (
        feat_grad.astype(jnp.float32) * live_mask[None, :, None]
        + back_rgb * styles[2].T[:, :, None]
    ) * leaky_slope(pre_two)
    cot_two = (grad_pre_two * demod_two.T[:, :, None]).astype(jnp.bfloat16)
    inner_two = (
        -0.5 * demod_two * demod_two * demod_two * jnp.sum(grad_pre_two * convolved, axis=2).T
    )
    taps_two = jnp.stack(
        [
            shifted(cot_two, 1 - tap_index // 3, 1 - tap_index % 3, full_side)
            for tap_index in range(9)
        ]
    )
    squares_two_grad = jnp.dot(inner_two.T, second_all * second_all, precision=precise)
    conv_two_grad = (
        jnp.einsum("tobp,cbp->toc", taps_two, gathered_two, preferred_element_type=jnp.float32)
        + 2.0 * weight_two * squares_two_grad[None]
    )
    style_two_demod = 2.0 * second_all * jnp.dot(inner_two, squares_two, precision=precise)
    columns = conv_second
    back_two = lax.psum_scatter(
        jnp.einsum("toc,tobp->cbp", columns, taps_two, preferred_element_type=jnp.float32),
        "chan",
        scatter_dimension=0,
        tiled=True,
    )
    style_two_conv = jnp.sum(back_two * act_one, axis=2).T
    grad_pre_one = back_two * styles[1].T[:, :, None] * leaky_slope(pre_one)
    cot_one = (grad_pre_one * demod_one.T[:, :, None]).astype(jnp.bfloat16)
    inner_one = -0.5 * demod_one * demod_one * demod_one * jnp.sum(grad_pre_one * raised, axis=2).T
    taps_one = jnp.stack(phase_grads(cot_one, half_side))
    squares_one_grad = jnp.dot(inner_one.T, first_all * first_all, precision=precise)
    conv_one_grad = (
        jnp.einsum("tobp,cbp->toc", taps_one, gathered_one, preferred_element_type=jnp.float32)
        + 2.0 * weight_one * squares_one_grad[None]
    )
    style_one_demod = 2.0 * first_all * jnp.dot(inner_one, squares_one, precision=precise)
    columns = conv_first
    back_one = lax.psum_scatter(
        jnp.einsum("toc,tobp->cbp", columns, taps_one, preferred_element_type=jnp.float32),
        "chan",
        scatter_dimension=0,
        tiled=True,
    )
    feat_in_grad = back_one * styles[0].T[:, :, None]
    style_one_conv = jnp.sum(back_one * feat_in.astype(jnp.float32), axis=2).T
    demod_one_sum, demod_two_sum = (
        lax.psum_scatter(style_one_demod, "chan", scatter_dimension=1, tiled=True),
        lax.psum_scatter(style_two_demod, "chan", scatter_dimension=1, tiled=True),
    )
    style_grads = jnp.stack(
        [style_one_conv + demod_one_sum, style_two_conv + demod_two_sum, style_rgb_grad]
    )
    latent_part = jnp.einsum("jbc,jwc->bw", style_grads, style_weight, precision=precise)
    gain_part = jnp.stack(
        [
            jnp.sum(grad_pre_one * noise_first[None, :, :]),
            jnp.sum(grad_pre_two * noise_second[None, :, :]),
        ]
    )
    latent_grad, gain_chan = lax.psum((latent_part, gain_part), "chan")
    style_weight_part = jnp.einsum("bw,jbc->jwc", latent, style_grads, precision=precise)
    style_bias_part = jnp.sum(style_grads, axis=1)
    conv_bias_part = jnp.stack(
        [jnp.sum(grad_pre_one, axis=(1, 2)), jnp.sum(grad_pre_two, axis=(1, 2))]
    )
    totals = lax.psum(
        (
            conv_one_grad,
            conv_two_grad,
            style_weight_part,
            style_bias_part,
            rgb_weight_part,
            conv_bias_part,
            rgb_bias_part,
            gain_chan,
        ),
        "dp",
    )
    return (feat_out, rgb_out, feat_in_grad, rgb_in_grad, latent_grad) + tuple(totals)


BF = jnp.bfloat16
F32 = jnp.float32
TILE = 256
ROWS = 16
ANY = pl.BlockSpec(memory_space=pl.ANY)
SMEM = pl.BlockSpec(memory_space=pltpu.SMEM)
LIMIT = 60 * 1024 * 1024


def whole(shape):
    return pl.BlockSpec(shape, lambda j: (0,) * len(shape))


def dot(a, b):
    return jnp.dot(a, b, preferred_element_type=F32)


def dot_nt(a, b):
    return lax.dot_general(a, b, (((1,), (1,)), ((), ())), preferred_element_type=F32)


def wide(column):
    return jnp.concatenate([column] * (TILE // 128), axis=1)


def move(field, row_shift, col_shift):
    offset = row_shift * HALF + col_shift
    if offset == 0:
        return field
    cells = field.shape[1]
    lane = lax.broadcasted_iota(jnp.int32, field.shape, 1)
    row, col = lane // HALF, lane % HALF
    inside = (row + row_shift >= 0) & (row + row_shift < HALF)
    inside = inside & (col + col_shift >= 0) & (col + col_shift < HALF)
    rolled = pltpu.roll(field.astype(F32), (-offset) % cells, 1)
    return jnp.where(inside, rolled, 0.0).astype(field.dtype)


def near(parity, step):
    other = (parity + step) % 2
    return other, (parity + step - other) // 2


def copy_index(phase, row_step, col_step):
    a, r = near(phase // 2, row_step)
    b, q = near(phase % 2, col_step)
    return ((a * 2 + b) * 2 + abs(r)) * 2 + abs(q)


def make_copies(source, copies):
    chunk = 32

    @pl.loop(0, source.shape[1] // chunk)
    def _(i):
        rows = pl.ds(pl.multiple_of(i * chunk, chunk), chunk)
        for phase in range(4):
            field = source[phase, rows, :]
            row_sign = 1 if phase // 2 == 0 else -1
            col_sign = 1 if phase % 2 == 0 else -1
            for r in (0, 1):
                for q in (0, 1):
                    copies[(phase * 2 + r) * 2 + q, rows, :] = move(
                        field, row_sign * r, col_sign * q
                    )


def demodulate(full, square_row, demod):
    chunk = 32

    @pl.loop(0, full.shape[1] // chunk)
    def _(i):
        rows = pl.ds(pl.multiple_of(i * chunk, chunk), chunk)
        total = None
        for t in range(9):
            value = full[t, rows, :].astype(F32)
            total = value * value if total is None else total + value * value
        total = jnp.sum(total * square_row, axis=1, keepdims=True)
        demod[rows, :] = jnp.broadcast_to(lax.rsqrt(total + epsilon), (chunk, 128))


def chan_peer(me, k):
    if k == 1:
        return me + 1 - 2 * (me % 2)
    return (me + 2) % 4 if k == 2 else 3 - me


def rows_of(base, size):
    return pl.ds(pl.multiple_of(base, size), size)


def take_rows(packs, rows_ref, cols):
    for d in range(4):
        here = slice(d * 128, (d + 1) * 128)
        pack = packs[d]
        rows_ref[:, here] = pack
        for j in range(3, 8):
            cols[j - 3, here, :] = jnp.broadcast_to(pack[j : j + 1, :], (128, 128)).T


def take_phases(plain, order, stacked, noise, color_phases):
    lanes = 512
    for n in range(plain.shape[1] // lanes):
        here = slice(n * lanes, (n + 1) * lanes)
        value = plain[:, here]
        first = value.astype(BF)
        rest = value - first.astype(F32)
        second = rest.astype(BF)
        third = rest - second.astype(F32)
        part = jnp.concatenate([first.astype(F32), second.astype(F32)], axis=0).astype(BF)
        stacked[:, here] = part
        high = dot(part, order[...])
        low = dot(jnp.concatenate([third, third], axis=0).astype(BF), order[...])
        for phase in range(4):
            grouped = slice(phase * 128, (phase + 1) * 128)
            out = slice(n * 128, (n + 1) * 128)
            color_phases[phase, :, out] = high[:, grouped].astype(BF)
            for i in (0, 1):
                noise[4 * i + phase : 4 * i + phase + 1, out] = (
                    high[3 + i : 4 + i, grouped] + high[11 + i : 12 + i, grouped] + low[3 + i : 4 + i, grouped]
                )


def block_kernel(gains, pack, x_in, own1, own2, feat_grad, plain, order_back, order, style_weight, shared,
                 raised_out, conv_out, feat_natural, full1_out, arrived, x_out, scaled_one_out, by_image, feat_all,
                 feat_out, back_all, grad1_out, grad2_out, color_in, every, every_shared, latent_grad,
                 demod1, demod2, color, rgb_grad, cols, rows_ref, noise, color_phases, packs, stacked,
                 full1, full2, copies, tile, grad_tile, field, total, back,
                 core1, core2, first1, first2, quad1, quad2, zsum1, zsum2, zin1, zin2, out1, out2,
                 sums2, sums1, sums0, inner2, inner1, style_sums, vectors, owned, latent_in, raw,
                 load_sem, store_sem, tile_sem, pack_send, pack_recv, x_send, x_recv, w_send, w_recv,
                 swap_send, swap_recv, grad_send, grad_recv, feat_send, feat_recv, back_send, back_recv,
                 core_send, core_recv, quad_send, quad_recv, z_send, z_recv, across_send, across_recv, twin_send, twin_recv,
                 first_send, first_recv, beside_send, beside_recv,
                 shared_send, shared_recv, every_send, every_recv, owned_send, owned_recv, latent_send, latent_recv,
                 color_send, color_recv, raw_sem, image_sem):
    me = lax.axis_index("chan")
    row = lax.axis_index("dp")
    core = row % 2
    depth = row // 2
    twin = row + 1 - 2 * core
    mesh_id = pl.DeviceIdType.MESH
    chans = [me] + [chan_peer(me, k) for k in (1, 2, 3)]
    depths = [depth] + [chan_peer(depth, k) for k in (1, 2, 3)]
    lines = [depths[k] * 2 + core for k in (1, 2, 3)] + [twin] + [depths[k] * 2 + 1 - core for k in (1, 2, 3)]
    barrier = pltpu.get_barrier_semaphore()
    for k in (1, 2, 3):
        pl.semaphore_signal(barrier, inc=1, device_id={"chan": chans[k]}, device_id_type=mesh_id)
    for line in lines:
        pl.semaphore_signal(barrier, inc=1, device_id={"dp": line}, device_id_type=mesh_id)
    pl.semaphore_wait(barrier, 10)

    def remote(source, target, sent, received, where):
        return pltpu.make_async_remote_copy(source, target, sent, received, device_id=where, device_id_type=mesh_id)

    x_all, scaled_one, scaled = grad_tile.at[1], grad_tile.at[0], field
    pack_moves = [
        remote(pack.at[chans[k]], packs.at[me], pack_send.at[k - 1], pack_recv.at[k - 1], {"chan": chans[k]})
        for k in (1, 2, 3)
    ]
    x_moves = [
        remote(x_in.at[chans[k]], x_all.at[rows_of(me * 128, 128), :], x_send.at[k - 1], x_recv.at[k - 1],
               {"chan": chans[k]})
        for k in (1, 2, 3)
    ]
    for item in pack_moves + x_moves:
        item.start()

    def half_rows(k):
        return rows_of(chans[k] * 128 + core * 64, 64)

    fulls, owns = (full1, full2), (own1, own2)
    cut = 5

    def near_move(c, k):
        return remote(owns[c].at[:, rows_of(core * 64, 64), :], fulls[c].at[:, half_rows(0), :],
                      w_send.at[c, k - 1], w_recv.at[c, k - 1], {"chan": chans[k]})

    def relay_move(c, k):
        part = fulls[c].at[pl.ds(0, cut) if k == 1 else pl.ds(cut, 9 - cut), half_rows(k), :]
        return remote(part, part, w_send.at[c, 1 + k], w_recv.at[c, 1 + k], {"chan": chans[3 - k]})

    def swap_move(c, k):
        part = fulls[c].at[:, half_rows(k), :]
        return remote(part, part, swap_send.at[c, k - 1], swap_recv.at[c, k - 1], {"dp": twin})

    near = [[near_move(c, k) for k in (1, 2)] for c in (0, 1)]
    relay = [[relay_move(c, k) for k in (1, 2)] for c in (0, 1)]
    swap = [[swap_move(c, k) for k in (1, 2, 3)] for c in (0, 1)]

    for item in near[0]:
        item.start()
    loads = [
        pltpu.make_async_copy(pack.at[me], packs.at[me], load_sem.at[0]),
        pltpu.make_async_copy(x_in.at[me], x_all.at[rows_of(me * 128, 128), :], load_sem.at[1]),
        pltpu.make_async_copy(own1, full1.at[:, rows_of(me * 128, 128), :], load_sem.at[2]),
        pltpu.make_async_copy(own2, full2.at[:, rows_of(me * 128, 128), :], load_sem.at[3]),
    ]
    for item in loads:
        item.start()

    def raw_in(n):
        return pltpu.make_async_copy(
            feat_grad.at[:, :, n * 512 : (n + 1) * 512], raw.at[n % 2], raw_sem.at[n % 2]
        )

    def image_store(n, half):
        return pltpu.make_async_copy(
            core1.at[n % 4 * 2 + half], by_image.at[half * 256 : (half + 1) * 256, n * 512 : (n + 1) * 512],
            image_sem.at[n % 4, half],
        )

    raw_in(0).start()
    raw_in(1).start()
    take_phases(plain, order_back, stacked, noise, color_phases)
    for n in range(8):
        if n >= 4:
            image_store(n - 4, 0).wait()
            image_store(n - 4, 1).wait()
        raw_in(n).wait()

        @pl.loop(0, 8)
        def _(i):
            value = jnp.swapaxes(raw[n % 2, rows_of(i * 16, 16), :, :], 0, 1)
            for image in range(4):
                core1[n % 4 * 2 + image // 2, rows_of(image % 2 * 128 + i * 16, 16), :] = value[image]

        image_store(n, 0).start()
        image_store(n, 1).start()
        if n + 2 < 8:
            raw_in(n + 2).start()
    loads[0].wait()
    for item in pack_moves:
        item.wait_recv()
    take_rows(packs, rows_ref, cols)
    loads[1].wait()
    for item in x_moves:
        item.wait_recv()

    @pl.loop(0, x_all.shape[0] // 32)
    def _(i):
        rows = rows_of(i * 32, 32)
        style = jnp.concatenate([cols[0, rows, :]] * 8, axis=1)
        value = (x_all[rows, :].astype(F32) * style).astype(BF)
        scaled_one[rows, :] = value
        for r in (0, 1):
            for q in (0, 1):
                copies[2 * r + q, rows, :] = move(value, r, q)

    for k in (0, 1):
        near[0][k].wait_recv()
        relay[0][k].start()
        swap[0][k].start()
    for item in near[1]:
        item.start()
    for item in relay[0]:
        item.wait_recv()
    swap[0][2].start()
    loads[2].wait()
    for item in swap[0]:
        item.wait_recv()
    store1 = pltpu.make_async_copy(full1, full1_out, store_sem.at[0])
    store1.start()
    demodulate(full1, rows_ref[3:4, :] * rows_ref[3:4, :], demod1)

    def part_of(j):
        return rows_of(j * 4 * TILE, 4 * TILE)

    def grad_move(j, k):
        return remote(by_image.at[rows_of(chans[k] * 128, 128), part_of(j)], arrived.at[rows_of(me * 128, 128), part_of(j)],
                      grad_send.at[j, k - 1], grad_recv.at[j, k - 1], {"chan": chans[k]})

    for n in range(4, 8):
        image_store(n, 0).wait()
        image_store(n, 1).wait()
    local3 = pltpu.make_async_copy(by_image.at[rows_of(me * 128, 128), :], arrived.at[rows_of(me * 128, 128), :], store_sem.at[4])
    stores = [
        pltpu.make_async_copy(x_all, x_out, store_sem.at[1]),
        pltpu.make_async_copy(scaled_one, scaled_one_out, store_sem.at[2]),
    ]
    for item in stores:
        item.start()
    tiles = copies.shape[2] // TILE
    channels = cols.shape[1]

    def raised_store(j, slot):
        return pltpu.make_async_copy(tile.at[slot], raised_out.at[:, :, rows_of(j * TILE, TILE)], tile_sem.at[0, slot])

    @pl.loop(0, tiles)
    def _(j):
        here = rows_of(j * TILE, TILE)
        slot = j % 2

        @pl.when(j >= 2)
        def _():
            raised_store(j - 2, slot).wait()

        for phase, (row_phase, col_phase) in enumerate(phase_pairs):
            summed = None
            for k, r in phase_taps[row_phase]:
                for l, q in phase_taps[col_phase]:
                    term = dot(full1[3 * k + l], copies[2 * r + q, :, here])
                    summed = term if summed is None else summed + term
            tile[slot, phase] = summed
            noise_row = gains[0] * noise[phase : phase + 1, here]
            for i in range(channels // ROWS):
                rows = slice(i * ROWS, (i + 1) * ROWS)
                pre = tile[slot, phase, rows, :] * wide(demod1[rows, :]) + noise_row + wide(cols[3, rows, :])
                act = pre * (0.6 * root_two + 0.4 * root_two * jnp.tanh(0.5 * pre))
                scaled[phase, rows, here] = (act * wide(cols[1, rows, :])).astype(BF)

        raised_store(j, slot).start()

        @pl.when(j == 1)
        def _():
            for k in (0, 1):
                near[1][k].wait_recv()
                relay[1][k].start()
                swap[1][k].start()
            for part in range(4):
                for k in (1, 2, 3):
                    grad_move(part, k).start()
            local3.start()

    make_copies(scaled, copies)
    for item in relay[1]:
        item.wait_recv()
    swap[1][2].start()
    loads[3].wait()
    for item in swap[1]:
        item.wait_recv()
    demodulate(full2, rows_ref[4:5, :] * rows_ref[4:5, :], demod2)
    rgb_rows = jnp.concatenate([rows_ref[...] * rows_ref[5:6, :]] * 2, axis=0).astype(BF)
    live = gains[2]
    rgb_grad[...] = jnp.zeros_like(rgb_grad)

    def tile_stores(j, slot):
        return (
            pltpu.make_async_copy(tile.at[slot], conv_out.at[:, :, rows_of(j * TILE, TILE)], tile_sem.at[0, slot]),
            pltpu.make_async_copy(grad_tile.at[slot], feat_natural.at[:, part_of(j)], tile_sem.at[1, slot]),
        )

    raised_store(2, 0).wait()
    raised_store(3, 1).wait()
    for item in stores:
        item.wait()

    @pl.loop(0, tiles)
    def _(j):
        here = rows_of(j * TILE, TILE)
        slot = j % 2

        @pl.when(j >= 2)
        def _():
            for item in tile_stores(j - 2, slot):
                item.wait()

        for phase in range(4):
            summed = None
            for t in range(9):
                term = dot(full2[t], copies[copy_index(phase, t // 3 - 1, t % 3 - 1), :, here])
                summed = term if summed is None else summed + term
            tile[slot, phase] = summed
            noise_row = gains[1] * noise[4 + phase : 5 + phase, here]
            for i in range(channels // ROWS):
                rows = slice(i * ROWS, (i + 1) * ROWS)
                pre = tile[slot, phase, rows, :] * wide(demod2[rows, :]) + noise_row + wide(cols[4, rows, :])
                act = pre * (0.6 * root_two + 0.4 * root_two * jnp.tanh(0.5 * pre))
                out = (act * live).astype(BF)
                low = slice(i * ROWS % 256, i * ROWS % 256 + ROWS)
                for half in range(TILE // 128):
                    core1[2 * half + i * ROWS // 256, low, phase * 128 : (phase + 1) * 128] = (
                        out[:, half * 128 : (half + 1) * 128]
                    )
        for half in range(TILE // 128):
            image = dot(core1[2 * half : 2 * half + 2].reshape(channels, 512), order[...]).astype(BF)
            grad_tile[slot, :, half * 512 : (half + 1) * 512] = image
            pixels = rows_of(j * 4 * TILE + half * 512, 512)
            color[:, pixels] = dot(rgb_rows, image)
            rgb_grad[...] += dot_nt(stacked[:, pixels], image)
        for item in tile_stores(j, slot):
            item.start()

    for j in (2, 3):
        for item in tile_stores(j, j % 2):
            item.wait()
    store1.wait()
    for item in pack_moves + x_moves + near[0] + near[1] + relay[0] + relay[1] + swap[0] + swap[1]:
        item.wait_send()

    shared_moves = [
        remote(shared, every_shared.at[row], shared_send.at[i], shared_recv.at[i], {"dp": line})
        for i, line in enumerate(lines)
    ]
    for item in shared_moves:
        item.start()
    every_shared[row] = shared[...]

    quarter = color.shape[1] // 4
    color_moves = [
        remote(color.at[0:8, rows_of(chans[k] * quarter, quarter)], color_in.at[me],
               color_send.at[k - 1], color_recv.at[k - 1], {"chan": chans[k]})
        for k in (1, 2, 3)
    ]
    for item in color_moves:
        item.start()
    color_own = pltpu.make_async_copy(color.at[0:8, rows_of(me * quarter, quarter)], color_in.at[me], load_sem.at[9])
    color_own.start()

    feat_moves = [
        remote(feat_natural.at[rows_of(chans[k] * 128, 128), :], feat_all.at[rows_of(me * 128, 128), :],
               feat_send.at[k - 1], feat_recv.at[k - 1], {"chan": chans[k]})
        for k in (1, 2, 3)
    ]
    for item in feat_moves:
        item.start()
    feat_own = pltpu.make_async_copy(
        feat_natural.at[rows_of(me * 128, 128), :], feat_all.at[rows_of(me * 128, 128), :], load_sem.at[0]
    )
    feat_own.start()
    weight, keep, send = full2, full1.at[:, 0:256, :], full1.at[:, 256:512, :]

    def tiles_in(source, j, slot):
        return pltpu.make_async_copy(source.at[:, :, rows_of(j * TILE, TILE)], tile.at[slot], tile_sem.at[0, slot])

    def grads_in(j, slot):
        return pltpu.make_async_copy(
            arrived.at[:, part_of(j)], grad_tile.at[slot], tile_sem.at[1, slot]
        )

    def grads_ready(j):
        for k in (1, 2, 3):
            grad_move(j, k).wait_recv()
        grads_in(j, j % 2).start()

    tiles_in(conv_out, 0, 0).start()
    local3.wait()
    grads_ready(0)
    sums2[...] = jnp.zeros_like(sums2)
    sums1[...] = jnp.zeros_like(sums1)
    style_sums[...] = jnp.zeros_like(style_sums)
    is_color = lax.broadcasted_iota(jnp.int32, (16, channels), 0) < 3
    rgb_rows = jnp.where(is_color, jnp.concatenate([rows_ref[...]] * 2, axis=0), 0.0).astype(BF)

    def add_sums(sums, rows, values):
        for n, value in enumerate(values):
            sums[n, rows, :] += value[:, :128] + value[:, 128:]

    @pl.loop(0, tiles)
    def _(j):
        slot = j % 2

        @pl.when(j + 1 < tiles)
        def _():
            tiles_in(conv_out, j + 1, 1 - slot).start()
            grads_ready(j + 1)

        tiles_in(conv_out, j, slot).wait()
        grads_in(j, slot).wait()
        here = rows_of(j * TILE, TILE)
        for half in range(TILE // 128):
            total[half] = dot(grad_tile[slot, :, half * 512 : (half + 1) * 512], order_back[...])
        for phase in range(4):
            noise_plain = noise[4 + phase : 5 + phase, here]
            noise_row = gains[1] * noise_plain
            back[phase % 2] = lax.dot_general(
                rgb_rows, color_phases[phase, :, here], (((0,), (0,)), ((), ())), preferred_element_type=F32
            )
            for i in range(channels // ROWS):
                rows = slice(i * ROWS, (i + 1) * ROWS)
                conv = tile[slot, phase, rows, :]
                scale = wide(demod2[rows, :])
                pre = conv * scale + noise_row + wide(cols[4, rows, :])
                sigma = 0.5 + 0.5 * jnp.tanh(0.5 * pre)
                slope = root_two * (0.2 + 0.8 * sigma * (1.0 + pre * (1.0 - sigma)))
                grad_feat = jnp.concatenate(
                    [total[half, rows, phase * 128 : (phase + 1) * 128] for half in range(TILE // 128)], axis=1
                )
                grad = (grad_feat * live + back[phase % 2, rows, :] * wide(cols[2, rows, :])) * slope
                copies[4 * phase, rows, here] = (grad * scale).astype(BF)
                add_sums(sums2, rows, (grad * conv, grad, grad * noise_plain))

    tiles_in(raised_out, 0, 0).start()
    late = [
        pltpu.make_async_copy(scaled_one_out, grad_tile.at[0], load_sem.at[4]),
        pltpu.make_async_copy(x_out, grad_tile.at[1], load_sem.at[5]),
    ]
    for item in late:
        item.start()

    def inner_of(sums, demod, inner):
        scale = demod[...]
        inner[...] = -0.5 * scale * scale * scale * jnp.sum(sums[0], axis=1, keepdims=True)

    inner_of(sums2, demod2, inner2)

    def spread_copies():
        chunk = 32

        @pl.loop(0, channels // chunk)
        def _(i):
            rows = rows_of(i * chunk, chunk)
            for phase in range(4):
                value = copies[4 * phase, rows, :]
                row_sign = 1 if phase // 2 == 0 else -1
                col_sign = 1 if phase % 2 == 0 else -1
                for r, q in ((0, 1), (1, 0), (1, 1)):
                    copies[4 * phase + 2 * r + q, rows, :] = move(value, row_sign * r, col_sign * q)

    spread_copies()

    def split(c, slot, t, inner, square_row):
        for k in range(4):
            base = chans[k] * 128
            for out, start in ((keep, base + core * 64), (send, base + 64 - core * 64)):
                rows = rows_of(start, 64)
                column = jnp.concatenate([inner[rows, :]] * 4, axis=1)
                plain = weight[t, rows, :].astype(F32)
                scaled = plain * column
                value = (total[slot, rows, :] + scaled * square_row).astype(BF)
                out[t, k * 32 : (k + 1) * 32, :] = value[:32]
                out[t, 128 + k * 32 : 160 + k * 32, :] = value[32:]
                scaled = plain * scaled
                style_sums[c] += sum(scaled[i * 8 : (i + 1) * 8, :] for i in range(8))

    cores, quads, zsums, zins, outs = (core1, core2), (quad1, quad2), (zsum1, zsum2), (zin1, zin2), (out1, out2)
    firsts = (first1, first2)
    low, high = depth % 2, depth // 2
    beside, across = {"dp": depths[1] * 2 + core}, {"dp": depths[2] * 2 + core}

    def taps(g):
        return pl.ds(3 * g, 3)

    def core_move(c, g):
        return remote(send.at[taps(g)], cores[c].at[taps(g)], core_send.at[c, g], core_recv.at[c, g], {"dp": twin})

    def first_move(c, g):
        return remote(keep.at[taps(g), rows_of(128 - low * 128, 128), :], firsts[c].at[taps(g)],
                      first_send.at[c, g], first_recv.at[c, g], beside)

    def quad_move(c, g, k):
        return remote(keep.at[taps(g), rows_of(low * 128 + k * 32, 32), :], quads[c].at[taps(g), k - 1],
                      quad_send.at[c, g, k - 1], quad_recv.at[c, g, k - 1], {"chan": chans[k]})

    def z_move(c, g):
        return remote(zsums[c].at[taps(g), rows_of(16 - high * 16, 16), :], zins[c].at[taps(g)],
                      z_send.at[c, g], z_recv.at[c, g], across)

    def across_move(c, g):
        part = outs[c].at[taps(g), rows_of(core * 64 + low * 32 + high * 16, 16), :]
        return remote(part, part, across_send.at[c, g], across_recv.at[c, g], across)

    def beside_move(c, g):
        part = outs[c].at[taps(g), rows_of(core * 64 + low * 32, 32), :]
        return remote(part, part, beside_send.at[c, g], beside_recv.at[c, g], beside)

    def twin_move(c, g):
        part = outs[c].at[taps(g), rows_of(core * 64, 64), :]
        return remote(part, part, twin_send.at[c, g], twin_recv.at[c, g], {"dp": twin})

    def join_cores(c, g):
        core_move(c, g).wait_recv()
        for i in range(3):
            t = 3 * g + i
            keep[t] = (keep[t].astype(F32) + cores[c][t].astype(F32)).astype(BF)
        first_move(c, g).start()

    def join_first(c, g):
        first_move(c, g).wait_recv()
        rows = rows_of(low * 128, 128)
        for i in range(3):
            t = 3 * g + i
            keep[t, rows, :] = (keep[t, rows, :].astype(F32) + firsts[c][t].astype(F32)).astype(BF)
        for k in (1, 2, 3):
            quad_move(c, g, k).start()

    def join_quad(c, g):
        for k in (1, 2, 3):
            quad_move(c, g, k).wait_recv()
        for i in range(3):
            t = 3 * g + i
            value = keep[t, rows_of(low * 128, 32), :].astype(F32)
            for k in range(3):
                value = value + quads[c][t, k].astype(F32)
            zsums[c][t] = value.astype(BF)
        z_move(c, g).start()

    def join_depth(c, g):
        z_move(c, g).wait_recv()
        for i in range(3):
            t = 3 * g + i
            value = zsums[c][t, rows_of(high * 16, 16), :].astype(F32) + zins[c][t].astype(F32)
            outs[c][t, rows_of(core * 64 + low * 32 + high * 16, 16), :] = value.astype(BF)
        across_move(c, g).start()

    def join_across(c, g):
        across_move(c, g).wait_recv()
        beside_move(c, g).start()

    def join_beside(c, g):
        beside_move(c, g).wait_recv()
        twin_move(c, g).start()

    def weight_grad(c, product, inner, square_row):
        @pl.loop(0, 3)
        def _(g):
            t = 3 * g
            total[0] = product(t)
            total[1] = product(t + 1)
            split(c, 0, t, inner, square_row)
            total[0] = product(t + 2)
            split(c, 1, t + 1, inner, square_row)
            split(c, 0, t + 2, inner, square_row)
            core_move(c, g).start()

            @pl.when(g >= 1)
            def _():
                join_cores(c, g - 1)

        join_cores(c, 2)
        for g in range(3):
            core_move(c, g).wait_send()

    def second_product(t):
        row_step, col_step = 1 - t // 3, 1 - t % 3
        summed = None
        for phase in range(4):
            a, b = phase // 2, phase % 2
            far_row = (row_step * (2 * a - 1) + 1) // 2 * (row_step * row_step)
            far_col = (col_step * (2 * b - 1) + 1) // 2 * (col_step * col_step)
            index = (((a + row_step + 2) % 2 * 2 + (b + col_step + 2) % 2) * 2 + far_row) * 2 + far_col
            term = dot_nt(copies[index], field[phase])
            summed = term if summed is None else summed + term
        return summed

    weight_grad(1, second_product, inner2, 2.0 * rows_ref[4:5, :] * rows_ref[4:5, :])

    def turn():
        @pl.loop(0, 9)
        def _(t):
            weight[t] = weight[t].T

    turn()

    @pl.loop(0, tiles)
    def _(j):
        slot = j % 2

        @pl.when(j + 1 < tiles)
        def _():
            tiles_in(raised_out, j + 1, 1 - slot).start()

        tiles_in(raised_out, j, slot).wait()
        here = rows_of(j * TILE, TILE)
        for phase in range(4):
            summed = None
            for t in range(9):
                term = dot(weight[t], copies[copy_index(phase, 1 - t // 3, 1 - t % 3), :, here])
                summed = term if summed is None else summed + term
            back[phase % 2] = summed
            noise_plain = noise[phase : phase + 1, here]
            noise_row = gains[0] * noise_plain
            for i in range(channels // ROWS):
                rows = slice(i * ROWS, (i + 1) * ROWS)
                conv = tile[slot, phase, rows, :]
                scale = wide(demod1[rows, :])
                pre = conv * scale + noise_row + wide(cols[3, rows, :])
                sigma = 0.5 + 0.5 * jnp.tanh(0.5 * pre)
                act = root_two * (pre * (0.2 + 0.8 * sigma))
                slope = root_two * (0.2 + 0.8 * sigma * (1.0 + pre * (1.0 - sigma)))
                value = back[phase % 2, rows, :]
                grad = value * wide(cols[1, rows, :]) * slope
                field[phase, rows, here] = (grad * scale).astype(BF)
                add_sums(sums1, rows, (grad * conv, grad, grad * noise_plain, value * act))

        @pl.when(j == 0)
        def _():
            join_first(1, 0)
            join_first(1, 1)

        @pl.when(j == 1)
        def _():
            join_first(1, 2)

        @pl.when(j == 2)
        def _():
            join_quad(1, 0)
            join_quad(1, 1)

    inner_of(sums1, demod1, inner1)
    load1 = pltpu.make_async_copy(full1_out, weight, load_sem.at[1])
    load1.start()

    @pl.loop(0, channels // 32)
    def _(i):
        rows = rows_of(i * 32, 32)
        for phase, (row_phase, col_phase) in enumerate(phase_pairs):
            value = field[phase, rows, :]
            for k, r in phase_taps[row_phase]:
                for l, q in phase_taps[col_phase]:
                    copies[3 * k + l, rows, :] = move(value, -r, -q)

    join_quad(1, 2)
    for g in range(3):
        for k in (1, 2, 3):
            quad_move(1, g, k).wait_send()
        first_move(1, g).wait_send()
    load1.wait()
    for item in late:
        item.wait()
    weight_grad(0, lambda t: dot_nt(copies[t], grad_tile[0]), inner1, 2.0 * rows_ref[3:4, :] * rows_ref[3:4, :])
    style_loads = [
        pltpu.make_async_copy(style_weight.at[j], total.at[0, :, j * 128 : (j + 1) * 128], load_sem.at[6 + j])
        for j in range(3)
    ]
    for item in style_loads:
        item.start()
    for g in range(3):
        join_depth(1, g)
    turn()

    for n in range(tiles):
        here = slice(n * TILE, (n + 1) * TILE)
        summed = None
        for t in range(9):
            term = dot(weight[t], copies[t, :, here])
            summed = term if summed is None else summed + term
        back[n % 2] = summed
        for i in range(channels // ROWS):
            rows = slice(i * ROWS, (i + 1) * ROWS)
            value = back[n % 2, rows, :]
            copies[9, rows, here] = (value * wide(cols[0, rows, :])).astype(BF)
            item = value * grad_tile[1, rows, here].astype(F32)
            item = item[:, :128] + item[:, 128:]
            sums0[rows, :] = item if n == 0 else sums0[rows, :] + item
        if n == 1:
            join_first(0, 0)
        if n == 3:
            join_first(0, 1)
    back_moves = [
        remote(copies.at[9, rows_of(chans[k] * 128, 128), :], back_all.at[me],
               back_send.at[k - 1], back_recv.at[k - 1], {"chan": chans[k]})
        for k in (1, 2, 3)
    ]
    for item in back_moves:
        item.start()
    back_own = pltpu.make_async_copy(copies.at[9, rows_of(me * 128, 128), :], back_all.at[me], load_sem.at[2])
    back_own.start()

    def as_row(sums):
        return jnp.sum(sums[...].T, axis=0, keepdims=True)

    style_two, style_one = as_row(sums1.at[3]), as_row(sums0)
    color_grad = rgb_grad[0:8, :]
    vector_rows = [
        style_one + 2.0 * rows_ref[3:4, :] * jnp.sum(style_sums[0], axis=0, keepdims=True),
        style_two + 2.0 * rows_ref[4:5, :] * jnp.sum(style_sums[1], axis=0, keepdims=True),
        sum(rows_ref[k : k + 1, :] * color_grad[k : k + 1, :] for k in range(3)),
        as_row(sums1.at[1]),
        as_row(sums2.at[1]),
        jnp.broadcast_to(jnp.sum(as_row(sums1.at[2]), axis=1, keepdims=True), (1, channels)),
        jnp.broadcast_to(jnp.sum(as_row(sums2.at[2]), axis=1, keepdims=True), (1, channels)),
        jnp.zeros((1, channels), F32),
    ]
    for i, value in enumerate(vector_rows):
        for d in range(4):
            vectors[d, i : i + 1, :] = value[:, d * 128 : (d + 1) * 128]
    color_grad = color_grad * rows_ref[5:6, :]
    for d in range(4):
        vectors[d, 8:16, :] = color_grad[:, d * 128 : (d + 1) * 128]
    owned_moves = [
        remote(vectors.at[chans[k]], owned.at[me], owned_send.at[k - 1], owned_recv.at[k - 1], {"chan": chans[k]})
        for k in (1, 2, 3)
    ]
    for item in owned_moves:
        item.start()
    owned[me] = vectors[me]

    for g in range(3):
        join_across(1, g)
    join_quad(0, 0)
    join_first(0, 2)
    for item in owned_moves:
        item.wait_recv()
    for item in style_loads:
        item.wait()
    latent_part = None
    for j in range(3):
        value = jnp.concatenate([owned[d, j : j + 1, :] for d in range(4)] + [jnp.zeros((4, 128), F32)], axis=0)
        term = lax.dot_general(
            value, total[0, :, j * 128 : (j + 1) * 128], (((1,), (1,)), ((), ())), precision=precise, preferred_element_type=F32
        )
        latent_part = term if latent_part is None else latent_part + term
    latent_in[3] = latent_part
    latent_moves = [
        remote(latent_in.at[3], latent_in.at[k - 1], latent_send.at[k - 1], latent_recv.at[k - 1], {"chan": chans[k]})
        for k in (1, 2, 3)
    ]
    every_moves = [
        remote(owned, every.at[row], every_send.at[i], every_recv.at[i], {"dp": line})
        for i, line in enumerate(lines)
    ]
    for item in latent_moves + every_moves:
        item.start()
    every[row] = owned[...]
    join_depth(0, 0)
    join_quad(0, 1)
    for g in range(3):
        join_beside(1, g)

    for item in feat_moves:
        item.wait_recv()
    feat_own.wait()

    def feat_in(n, half):
        return pltpu.make_async_copy(
            feat_all.at[half * 256 : (half + 1) * 256, n * 512 : (n + 1) * 512], core2.at[n % 4 * 2 + half],
            image_sem.at[n % 4, half],
        )

    def feat_store(n):
        return pltpu.make_async_copy(
            raw.at[n % 2], feat_out.at[:, :, n * 512 : (n + 1) * 512], raw_sem.at[n % 2]
        )

    for n in range(4):
        feat_in(n, 0).start()
        feat_in(n, 1).start()
    for n in range(8):
        if n >= 2:
            feat_store(n - 2).wait()
        feat_in(n, 0).wait()
        feat_in(n, 1).wait()

        @pl.loop(0, 8)
        def _(i):
            value = jnp.stack(
                [core2[n % 4 * 2 + image // 2, rows_of(image % 2 * 128 + i * 16, 16), :] for image in range(4)]
            )
            raw[n % 2, rows_of(i * 16, 16), :, :] = jnp.swapaxes(value, 0, 1)

        feat_store(n).start()
        if n + 4 < 8:
            feat_in(n + 4, 0).start()
            feat_in(n + 4, 1).start()
        if n == 2:
            join_depth(0, 1)
        if n == 4:
            join_across(0, 0)
            join_quad(0, 2)
        if n == 6:
            join_across(0, 1)
            join_beside(0, 0)
    join_depth(0, 2)
    join_beside(0, 1)
    for g in range(3):
        twin_move(1, g).wait()
    store2 = pltpu.make_async_copy(out2, grad2_out, load_sem.at[1])
    store2.start()
    join_across(0, 2)
    for item in latent_moves:
        item.wait_recv()
    latent_grad[...] = latent_in[0] + latent_in[1] + latent_in[2] + latent_in[3]
    join_beside(0, 2)
    for g in range(3):
        twin_move(0, g).wait()
    store1 = pltpu.make_async_copy(out1, grad1_out, load_sem.at[3])
    store1.start()
    feat_store(6).wait()
    feat_store(7).wait()
    for c in (0, 1):
        for g in range(3):
            if c == 0:
                first_move(c, g).wait_send()
                for k in (1, 2, 3):
                    quad_move(c, g, k).wait_send()
            z_move(c, g).wait_send()
            across_move(c, g).wait_send()
            beside_move(c, g).wait_send()
    for item in feat_moves:
        item.wait_send()
    for item in back_moves + shared_moves + every_moves + color_moves:
        item.wait()
    for item in owned_moves + latent_moves:
        item.wait_send()
    for j in range(4):
        for k in (1, 2, 3):
            grad_move(j, k).wait_send()
    for item in (back_own, color_own, store2, store1):
        item.wait()


def pick(value, index, axis):
    return lax.dynamic_index_in_dim(value, index, axis, keepdims=False)


def phase_order():
    place = jnp.arange(512)
    row, col = place // SIDE, place % SIDE
    grouped = ((row % 2) * 2 + col % 2) * 128 + (row // 2) * HALF + col // 2
    return (jnp.arange(512)[:, None] == grouped[None, :]).astype(BF)


def image_body(
    feat_in,
    rgb_in,
    latent,
    noise_first,
    noise_second,
    live_count,
    conv_first,
    conv_second,
    style_weight,
    style_bias,
    rgb_weight,
    conv_bias,
    rgb_bias,
    noise_gain,
    feat_grad,
    rgb_grad,
):
    local_ch, images, half_pix = feat_in.shape
    channels = 4 * local_ch
    pixels = feat_grad.shape[2]
    me = lax.axis_index("chan")
    live_mask = (jnp.arange(images) < live_count[0]).astype(F32)
    live = (me < live_count[0]).astype(F32)
    gains = jnp.concatenate([noise_gain, live[None]])
    styles = jnp.einsum("bw,jwc->bjc", latent, style_weight, precision=precise) + style_bias[None]

    def each_image(value):
        return jnp.broadcast_to(value[None], (images,) + value.shape)

    pack = jnp.concatenate([each_image(rgb_weight.astype(F32)), styles, each_image(conv_bias)], axis=1)
    plain = jnp.concatenate(
        [pick(rgb_grad, me, 0) * live, pick(noise_first, me, 0)[None], pick(noise_second, me, 0)[None],
         jnp.zeros((3, pixels), F32)]
    )
    x_by_image = feat_in.transpose(1, 0, 2)
    order = phase_order()

    vmem = pl.BlockSpec(memory_space=pltpu.VMEM)
    field, wide_weight = (4, channels, half_pix), (9, channels, channels)
    rgb_cot = rgb_grad * live_mask[:, None, None]
    rgb_bias_part = jnp.sum(rgb_cot, axis=(0, 2))
    shared = jnp.concatenate([latent, jnp.broadcast_to(jnp.pad(rgb_bias_part, (0, 509))[None], (4, 512))])
    outs = (
        (field, F32), (field, F32), ((channels, pixels), BF), (wide_weight, BF), ((channels, pixels), BF),
        ((channels, half_pix), BF), ((channels, half_pix), BF), ((channels, pixels), BF), ((channels, pixels), BF),
        (feat_grad.shape, BF), ((4, local_ch, half_pix), BF), ((9, local_ch, channels), BF),
        ((9, local_ch, channels), BF), ((4, 8, pixels // 4), F32), ((8, 4, 16, 128), F32), ((8, 8, 512), F32),
        ((8, 512), F32),
    )
    vector = ((channels, 128), F32)
    scratch = (
        vector, vector, ((16, pixels), F32), ((16, channels), F32), ((5, channels, 128), F32), ((8, channels), F32),
        ((8, half_pix), F32), ((4, 16, half_pix), BF), ((4, 8, 128), F32), ((16, pixels), BF),
        (wide_weight, BF), (wide_weight, BF), ((16, channels, half_pix), BF), ((2, 4, channels, TILE), F32),
        ((2, channels, 4 * TILE), BF), (field, BF), ((2, channels, channels), F32), ((2, channels, TILE), F32),
        ((9, 256, channels), BF), ((9, 256, channels), BF), ((9, 128, channels), BF), ((9, 128, channels), BF),
        ((9, 3, 32, channels), BF), ((9, 3, 32, channels), BF), ((9, 32, channels), BF), ((9, 32, channels), BF),
        ((9, 16, channels), BF), ((9, 16, channels), BF),
        ((9, local_ch, channels), BF), ((9, local_ch, channels), BF),
        ((3, channels, 128), F32), ((4, channels, 128), F32), vector, vector, vector, ((2, 8, channels), F32),
        ((4, 16, 128), F32), ((4, 16, 128), F32), ((4, 8, 512), F32), ((2, local_ch, 4, 512), BF),
    )
    counts = (
        [(10,), (5,), (2, 2)] + [(3,)] * 4 + [(2, 4)] * 2 + [(2, 3)] * 2 + [(4, 3)] * 2 + [(3,)] * 4
        + [(2, 3)] * 2 + [(2, 3, 3)] * 2 + [(2, 3)] * 10 + [(7,)] * 4 + [(3,)] * 6 + [(2,), (4, 2)]
    )
    results = pl.pallas_call(
        block_kernel,
        in_specs=[SMEM] + [ANY] * 5 + [vmem] * 3 + [ANY, vmem],
        out_specs=[ANY] * 14 + [vmem] * 3,
        out_shape=[jax.ShapeDtypeStruct(shape, dtype) for shape, dtype in outs],
        scratch_shapes=[pltpu.VMEM(shape, dtype) for shape, dtype in scratch]
        + [pltpu.SemaphoreType.DMA(count) for count in counts],
        compiler_params=pltpu.CompilerParams(vmem_limit_bytes=LIMIT, collective_id=0, has_side_effects=True),
        cost_estimate=pl.CostEstimate(flops=int(150e9), bytes_accessed=12 << 20, transcendentals=0),
    )(gains, pack, x_by_image, conv_first, conv_second, feat_grad, plain, order.T, order, style_weight, shared)
    feat_out, back_all, grad_one, grad_two, color_in, every, every_shared, latent_grad = results[9:]
    feat_in_grad = back_all.transpose(1, 0, 2).astype(F32)
    grad_one, grad_two = grad_one.astype(F32), grad_two.astype(F32)

    lift_matrix = upsample_matrix(HALF)
    shard_pix = pixels // 4
    skip_up = jnp.einsum(
        "up,bkpq,vq->bkuv",
        lift_matrix,
        rgb_in.reshape(images, 3, HALF, HALF),
        lift_matrix,
        precision=precise,
    ).reshape(images, 3, pixels)
    skip_mine = lax.dynamic_slice_in_dim(skip_up, me * shard_pix, shard_pix, 2)
    rgb_out = (color_in[:, :3] + rgb_bias[None, :, None] + skip_mine) * live_mask[:, None, None]
    rgb_in_grad = jnp.einsum(
        "up,bkuv,vq->bkpq",
        lift_matrix,
        rgb_cot.reshape(images, 3, SIDE, SIDE),
        lift_matrix,
        precision=precise,
    ).reshape(images, 3, half_pix)

    summed = jnp.sum(every, axis=(0, 1))
    style_weight_grad = jnp.einsum("gbw,gbjc->jwc", every_shared[:, :4], every[:, :, :3], precision=precise)
    return (
        feat_out,
        rgb_out,
        feat_in_grad,
        rgb_in_grad,
        latent_grad[:4],
        grad_one,
        grad_two,
        style_weight_grad,
        summed[:3],
        summed[8:11],
        summed[3:5],
        jnp.sum(every_shared[:, 4, :3], axis=0),
        summed[5:7, 0],
    )


def solution(mesh):
    alone = mesh.shape["chan"] == 4 and mesh.shape["dp"] == 8
    return jax.shard_map(
        image_body if alone else body,
        mesh=mesh,
        in_specs=(
            P("chan", "dp", None),
            P("dp", None, None),
            P("dp", None),
            P("dp", None),
            P("dp", None),
            P("dp"),
            P(None, "chan", None),
            P(None, "chan", None),
            P(None, None, "chan"),
            P(None, "chan"),
            P(None, "chan"),
            P(None, "chan"),
            P(),
            P(),
            P("chan", "dp", None),
            P("dp", None, None),
        ),
        out_specs=(
            P("chan", "dp", None),
            P("dp", None, "chan"),
            P("chan", "dp", None),
            P("dp", None, None),
            P("dp", None),
            P(None, "chan", None),
            P(None, "chan", None),
            P(None, None, "chan"),
            P(None, "chan"),
            P(None, "chan"),
            P(None, "chan"),
            P(),
            P(),
        ),
        check_vma=False,
    )
```

```python
import functools

import jax
import jax.numpy as jnp
from jax import lax
from jax.experimental import pallas as pl
from jax.experimental.pallas import tpu as pltpu
from jax.sharding import PartitionSpec as P

SIDE = 64
HALF = 32


precise = lax.Precision.HIGHEST
epsilon = 1e-08
root_two = 1.4142135623730951
phase_taps = (((1, 0),), ((2, 0), (0, 1)))
phase_pairs = ((0, 0), (0, 1), (1, 0), (1, 1))


def leaky_silu(value):
    return root_two * (0.2 * value + 0.8 * jax.nn.silu(value))


def leaky_slope(value):
    sigma = jax.nn.sigmoid(value)
    return root_two * (0.2 + 0.8 * sigma * (1.0 + value * (1.0 - sigma)))


def shifted(field, row_shift, col_shift, width):
    cells = field.shape[-1]
    offset = row_shift * width + col_shift
    if offset > 0:
        result = jnp.concatenate(
            [field[..., offset:], jnp.zeros(field.shape[:-1] + (offset,), field.dtype)], axis=-1
        )
    elif offset < 0:
        result = jnp.concatenate(
            [jnp.zeros(field.shape[:-1] + (-offset,), field.dtype), field[..., : cells + offset]],
            axis=-1,
        )
    else:
        result = field
    if col_shift != 0:
        column = jnp.arange(cells) % width
        inside = (column + col_shift >= 0) & (column + col_shift < width)
        result = jnp.where(inside, result, jnp.zeros((), field.dtype))
    return result


def upsample_matrix(half_side):
    rows_out = jnp.arange(2 * half_side)[:, None]
    cols_in = jnp.arange(half_side)[None, :]
    centre = rows_out // 2
    beside = centre - 1 + 2 * (rows_out % 2)
    return (
        jnp.where(cols_in == centre, 0.75, 0.0) + jnp.where(cols_in == beside, 0.25, 0.0)
    ).astype(jnp.float32)


def alternate(phases, half_side):
    stacked = jnp.stack(phases)
    out_rows, batch_count = (stacked.shape[1], stacked.shape[2])
    blocked = stacked.reshape(2, 2, out_rows, batch_count, half_side, half_side)
    return blocked.transpose(2, 3, 4, 0, 5, 1).reshape(
        out_rows, batch_count, 4 * half_side * half_side
    )


def split_phases(field, half_side):
    out_rows, batch_count = (field.shape[0], field.shape[1])
    blocked = field.reshape(out_rows, batch_count, half_side, 2, half_side, 2)
    return [
        blocked[:, :, :, row_phase, :, col_phase].reshape(
            out_rows, batch_count, half_side * half_side
        )
        for row_phase, col_phase in phase_pairs
    ]


def up_conv(inputs, weight, half_side):
    shifted_inputs = {}
    for row_shift in (0, 1):
        for col_shift in (0, 1):
            shifted_inputs[row_shift, col_shift] = shifted(inputs, row_shift, col_shift, half_side)
    phases = []
    for row_phase, col_phase in phase_pairs:
        summed = None
        for row_tap, row_shift in phase_taps[row_phase]:
            for col_tap, col_shift in phase_taps[col_phase]:
                product = jnp.einsum(
                    "oc,cbp->obp",
                    weight[row_tap * 3 + col_tap],
                    shifted_inputs[row_shift, col_shift],
                    preferred_element_type=jnp.float32,
                )
                summed = product if summed is None else summed + product
        phases.append(summed)
    return alternate(phases, half_side)


def phase_grads(grad_field, half_side):
    grad_phases = split_phases(grad_field, half_side)
    shifted_grads = [None] * 9
    for phase_index in range(4):
        row_phase, col_phase = phase_pairs[phase_index]
        for row_tap, row_shift in phase_taps[row_phase]:
            for col_tap, col_shift in phase_taps[col_phase]:
                shifted_grads[row_tap * 3 + col_tap] = shifted(
                    grad_phases[phase_index], -row_shift, -col_shift, half_side
                )
    return shifted_grads


def flat_conv(inputs, weight, width):
    summed = None
    for tap_index in range(9):
        product = jnp.einsum(
            "oc,cbp->obp", weight[tap_index], inputs, preferred_element_type=jnp.float32
        )
        product = shifted(product, tap_index // 3 - 1, tap_index % 3 - 1, width)
        summed = product if summed is None else summed + product
    return summed


def body(
    feat_in,
    rgb_in,
    latent,
    noise_first,
    noise_second,
    live_count,
    conv_first,
    conv_second,
    style_weight,
    style_bias,
    rgb_weight,
    conv_bias,
    rgb_bias,
    noise_gain,
    feat_grad,
    rgb_grad,
):
    local_ch, images, half_pix = feat_in.shape
    pixels = feat_grad.shape[2]
    half_side = HALF
    full_side = SIDE
    chan_rank = lax.axis_index("chan")
    live_mask = (jnp.arange(images) < live_count[0]).astype(jnp.float32)
    styles = (
        jnp.einsum("bw,jwc->jbc", latent, style_weight, precision=precise) + style_bias[:, None, :]
    )
    first_all, second_all = (
        lax.all_gather(styles[0], "chan", axis=1, tiled=True),
        lax.all_gather(styles[1], "chan", axis=1, tiled=True),
    )
    weight_one = conv_first.astype(jnp.float32)
    weight_two = conv_second.astype(jnp.float32)
    squares_one = jnp.sum(weight_one * weight_one, axis=0)
    squares_two = jnp.sum(weight_two * weight_two, axis=0)
    demod_one = lax.rsqrt(
        jnp.dot(first_all * first_all, squares_one.T, precision=precise) + epsilon
    )
    demod_two = lax.rsqrt(
        jnp.dot(second_all * second_all, squares_two.T, precision=precise) + epsilon
    )
    scaled_one = (feat_in.astype(jnp.float32) * styles[0].T[:, :, None]).astype(jnp.bfloat16)
    gathered_one = lax.all_gather(scaled_one, "chan", axis=0, tiled=True)
    raised = up_conv(gathered_one, conv_first, half_side)
    pre_one = (
        raised * demod_one.T[:, :, None]
        + noise_gain[0] * noise_first[None, :, :]
        + conv_bias[0][:, None, None]
    )
    act_one = leaky_silu(pre_one)
    scaled_two = (act_one * styles[1].T[:, :, None]).astype(jnp.bfloat16)
    gathered_two = lax.all_gather(scaled_two, "chan", axis=0, tiled=True)
    convolved = flat_conv(gathered_two, conv_second, full_side)
    pre_two = (
        convolved * demod_two.T[:, :, None]
        + noise_gain[1] * noise_second[None, :, :]
        + conv_bias[1][:, None, None]
    )
    act_two = leaky_silu(pre_two)
    feat_out = (act_two * live_mask[None, :, None]).astype(jnp.bfloat16)
    scaled_rgb = (act_two * styles[2].T[:, :, None]).astype(jnp.bfloat16)
    color_part = jnp.einsum(
        "ko,obp->bkp", rgb_weight, scaled_rgb, preferred_element_type=jnp.float32
    )
    color = lax.psum_scatter(color_part, "chan", scatter_dimension=2, tiled=True)
    shard_pix = color.shape[2]
    lift_matrix = upsample_matrix(half_side)
    skip_up = jnp.einsum(
        "up,bkpq,vq->bkuv",
        lift_matrix,
        rgb_in.reshape(images, 3, half_side, half_side),
        lift_matrix,
        precision=precise,
    ).reshape(images, 3, pixels)
    skip_mine = lax.dynamic_slice_in_dim(skip_up, chan_rank * shard_pix, shard_pix, 2)
    rgb_out = (color + rgb_bias[None, :, None] + skip_mine) * live_mask[:, None, None]
    rgb_cot = rgb_grad * live_mask[:, None, None]
    color_cot = rgb_cot.astype(jnp.bfloat16)
    rgb_in_grad = jnp.einsum(
        "up,bkuv,vq->bkpq",
        lift_matrix,
        rgb_cot.reshape(images, 3, full_side, full_side),
        lift_matrix,
        precision=precise,
    ).reshape(images, 3, half_pix)
    rgb_bias_part = jnp.sum(rgb_cot, axis=(0, 2))
    rgb_weight_part = jnp.einsum(
        "bkp,obp->ko", color_cot, scaled_rgb, preferred_element_type=jnp.float32
    )
    back_rgb = jnp.einsum("ko,bkp->obp", rgb_weight, color_cot, preferred_element_type=jnp.float32)
    style_rgb_grad = jnp.sum(back_rgb * act_two, axis=2).T
    grad_pre_two = (
        feat_grad.astype(jnp.float32) * live_mask[None, :, None]
        + back_rgb * styles[2].T[:, :, None]
    ) * leaky_slope(pre_two)
    cot_two = (grad_pre_two * demod_two.T[:, :, None]).astype(jnp.bfloat16)
    inner_two = (
        -0.5 * demod_two * demod_two * demod_two * jnp.sum(grad_pre_two * convolved, axis=2).T
    )
    taps_two = jnp.stack(
        [
            shifted(cot_two, 1 - tap_index // 3, 1 - tap_index % 3, full_side)
            for tap_index in range(9)
        ]
    )
    squares_two_grad = jnp.dot(inner_two.T, second_all * second_all, precision=precise)
    conv_two_grad = (
        jnp.einsum("tobp,cbp->toc", taps_two, gathered_two, preferred_element_type=jnp.float32)
        + 2.0 * weight_two * squares_two_grad[None]
    )
    style_two_demod = 2.0 * second_all * jnp.dot(inner_two, squares_two, precision=precise)
    columns = conv_second
    back_two = lax.psum_scatter(
        jnp.einsum("toc,tobp->cbp", columns, taps_two, preferred_element_type=jnp.float32),
        "chan",
        scatter_dimension=0,
        tiled=True,
    )
    style_two_conv = jnp.sum(back_two * act_one, axis=2).T
    grad_pre_one = back_two * styles[1].T[:, :, None] * leaky_slope(pre_one)
    cot_one = (grad_pre_one * demod_one.T[:, :, None]).astype(jnp.bfloat16)
    inner_one = -0.5 * demod_one * demod_one * demod_one * jnp.sum(grad_pre_one * raised, axis=2).T
    taps_one = jnp.stack(phase_grads(cot_one, half_side))
    squares_one_grad = jnp.dot(inner_one.T, first_all * first_all, precision=precise)
    conv_one_grad = (
        jnp.einsum("tobp,cbp->toc", taps_one, gathered_one, preferred_element_type=jnp.float32)
        + 2.0 * weight_one * squares_one_grad[None]
    )
    style_one_demod = 2.0 * first_all * jnp.dot(inner_one, squares_one, precision=precise)
    columns = conv_first
    back_one = lax.psum_scatter(
        jnp.einsum("toc,tobp->cbp", columns, taps_one, preferred_element_type=jnp.float32),
        "chan",
        scatter_dimension=0,
        tiled=True,
    )
    feat_in_grad = back_one * styles[0].T[:, :, None]
    style_one_conv = jnp.sum(back_one * feat_in.astype(jnp.float32), axis=2).T
    demod_one_sum, demod_two_sum = (
        lax.psum_scatter(style_one_demod, "chan", scatter_dimension=1, tiled=True),
        lax.psum_scatter(style_two_demod, "chan", scatter_dimension=1, tiled=True),
    )
    style_grads = jnp.stack(
        [style_one_conv + demod_one_sum, style_two_conv + demod_two_sum, style_rgb_grad]
    )
    latent_part = jnp.einsum("jbc,jwc->bw", style_grads, style_weight, precision=precise)
    gain_part = jnp.stack(
        [
            jnp.sum(grad_pre_one * noise_first[None, :, :]),
            jnp.sum(grad_pre_two * noise_second[None, :, :]),
        ]
    )
    latent_grad, gain_chan = lax.psum((latent_part, gain_part), "chan")
    style_weight_part = jnp.einsum("bw,jbc->jwc", latent, style_grads, precision=precise)
    style_bias_part = jnp.sum(style_grads, axis=1)
    conv_bias_part = jnp.stack(
        [jnp.sum(grad_pre_one, axis=(1, 2)), jnp.sum(grad_pre_two, axis=(1, 2))]
    )
    totals = lax.psum(
        (
            conv_one_grad,
            conv_two_grad,
            style_weight_part,
            style_bias_part,
            rgb_weight_part,
            conv_bias_part,
            rgb_bias_part,
            gain_chan,
        ),
        "dp",
    )
    return (feat_out, rgb_out, feat_in_grad, rgb_in_grad, latent_grad) + tuple(totals)


BF = jnp.bfloat16
F32 = jnp.float32
TILE = 256
ROWS = 16
ANY = pl.BlockSpec(memory_space=pl.ANY)
SMEM = pl.BlockSpec(memory_space=pltpu.SMEM)
LIMIT = 60 * 1024 * 1024


def whole(shape):
    return pl.BlockSpec(shape, lambda j: (0,) * len(shape))


def dot(a, b):
    return jnp.dot(a, b, preferred_element_type=F32)


def dot_nt(a, b):
    return lax.dot_general(a, b, (((1,), (1,)), ((), ())), preferred_element_type=F32)


def wide(column):
    return jnp.concatenate([column] * (TILE // 128), axis=1)


def move(field, row_shift, col_shift):
    offset = row_shift * HALF + col_shift
    if offset == 0:
        return field
    cells = field.shape[1]
    lane = lax.broadcasted_iota(jnp.int32, (1, cells), 1)
    row, col = lane // HALF, lane % HALF
    inside = (row + row_shift >= 0) & (row + row_shift < HALF)
    inside = inside & (col + col_shift >= 0) & (col + col_shift < HALF)
    rolled = pltpu.roll(field, (-offset) % cells, 1)
    return rolled * jnp.where(inside, 1.0, 0.0).astype(field.dtype)


def near(parity, step):
    other = (parity + step) % 2
    return other, (parity + step - other) // 2


def copy_index(phase, row_step, col_step):
    a, r = near(phase // 2, row_step)
    b, q = near(phase % 2, col_step)
    return ((a * 2 + b) * 2 + abs(r)) * 2 + abs(q)


def make_copies(source, copies):
    chunk = 32

    @pl.loop(0, source.shape[1] // chunk)
    def _(i):
        rows = pl.ds(pl.multiple_of(i * chunk, chunk), chunk)
        for phase in range(4):
            field = source[phase, rows, :]
            row_sign = 1 if phase // 2 == 0 else -1
            col_sign = 1 if phase % 2 == 0 else -1
            for r in (0, 1):
                for q in (0, 1):
                    copies[(phase * 2 + r) * 2 + q, rows, :] = move(
                        field, row_sign * r, col_sign * q
                    )


def demodulate(full, square_row, demod):
    chunk = 32

    @pl.loop(0, full.shape[1] // chunk)
    def _(i):
        rows = pl.ds(pl.multiple_of(i * chunk, chunk), chunk)
        total = None
        for t in range(9):
            value = full[t, rows, :].astype(F32)
            total = value * value if total is None else total + value * value
        total = jnp.sum(total * square_row, axis=1, keepdims=True)
        demod[rows, :] = jnp.broadcast_to(lax.rsqrt(total + epsilon), (chunk, 128))


def chan_peer(me, k):
    if k == 1:
        return me + 1 - 2 * (me % 2)
    return (me + 2) % 4 if k == 2 else 3 - me


def rows_of(base, size):
    return pl.ds(pl.multiple_of(base, size), size)


def take_rows(packs, rows_ref, cols):
    for d in range(4):
        here = slice(d * 128, (d + 1) * 128)
        pack = packs[d]
        rows_ref[:, here] = pack
        for j in range(3, 8):
            cols[j - 3, here, :] = jnp.broadcast_to(pack[j : j + 1, :], (128, 128)).T


def take_phases(plain, order, stacked, noise, color_phases):
    lanes = 512
    for n in range(plain.shape[1] // lanes):
        here = slice(n * lanes, (n + 1) * lanes)
        value = plain[:, here]
        first = value.astype(BF)
        rest = value - first.astype(F32)
        second = rest.astype(BF)
        third = rest - second.astype(F32)
        part = jnp.concatenate([first.astype(F32), second.astype(F32)], axis=0).astype(BF)
        stacked[:, here] = part
        high = dot(part, order[...])
        low = dot(jnp.concatenate([third, third], axis=0).astype(BF), order[...])
        for phase in range(4):
            grouped = slice(phase * 128, (phase + 1) * 128)
            out = slice(n * 128, (n + 1) * 128)
            color_phases[phase, :, out] = high[:, grouped].astype(BF)
            for i in (0, 1):
                noise[4 * i + phase : 4 * i + phase + 1, out] = (
                    high[3 + i : 4 + i, grouped] + high[11 + i : 12 + i, grouped] + low[3 + i : 4 + i, grouped]
                )


def block_kernel(gains, pack, x_in, own1, own2, feat_grad, plain, order_back, order, style_weight, shared,
                 raised_out, conv_out, feat_natural, full1_out, arrived, x_out, scaled_one_out, by_image, feat_all,
                 feat_out, back_all, grad1_out, grad2_out, color_in, every, every_shared, latent_grad,
                 demod1, demod2, color, rgb_grad, cols, rows_ref, noise, color_phases, packs, stacked,
                 full1, full2, copies, tile, grad_tile, field, total, back,
                 core1, core2, first1, first2, quad1, quad2, zsum1, zsum2, zin1, zin2, out1, out2,
                 sums2, sums1, sums0, inner2, inner1, style_sums, vectors, owned, latent_in, raw,
                 load_sem, store_sem, tile_sem, pack_send, pack_recv, x_send, x_recv, w_send, w_recv,
                 swap_send, swap_recv, grad_send, grad_recv, feat_send, feat_recv, back_send, back_recv,
                 core_send, core_recv, quad_send, quad_recv, z_send, z_recv, across_send, across_recv, twin_send, twin_recv,
                 first_send, first_recv, beside_send, beside_recv,
                 shared_send, shared_recv, every_send, every_recv, owned_send, owned_recv, latent_send, latent_recv,
                 color_send, color_recv, raw_sem, image_sem, side_send, side_recv):
    me = lax.axis_index("chan")
    row = lax.axis_index("dp")
    core = row % 2
    depth = row // 2
    twin = row + 1 - 2 * core
    mesh_id = pl.DeviceIdType.MESH
    chans = [me] + [chan_peer(me, k) for k in (1, 2, 3)]
    depths = [depth] + [chan_peer(depth, k) for k in (1, 2, 3)]
    lines = [depths[k] * 2 + core for k in (1, 2, 3)] + [twin] + [depths[k] * 2 + 1 - core for k in (1, 2, 3)]
    barrier = pltpu.get_barrier_semaphore()
    for k in (1, 2, 3):
        pl.semaphore_signal(barrier, inc=1, device_id={"chan": chans[k]}, device_id_type=mesh_id)
    for line in lines:
        pl.semaphore_signal(barrier, inc=1, device_id={"dp": line}, device_id_type=mesh_id)
    pl.semaphore_wait(barrier, 10)

    def remote(source, target, sent, received, where):
        return pltpu.make_async_remote_copy(source, target, sent, received, device_id=where, device_id_type=mesh_id)

    x_all, scaled_one, scaled = grad_tile.at[1], grad_tile.at[0], field
    pack_moves = [
        remote(pack.at[chans[k]], packs.at[me], pack_send.at[k - 1], pack_recv.at[k - 1], {"chan": chans[k]})
        for k in (1, 2, 3)
    ]
    x_moves = [
        remote(x_in.at[chans[k]], x_all.at[rows_of(me * 128, 128), :], x_send.at[k - 1], x_recv.at[k - 1],
               {"chan": chans[k]})
        for k in (1, 2, 3)
    ]
    for item in pack_moves:
        item.start()

    low, high = depth % 2, depth // 2
    beside, across = {"dp": depths[1] * 2 + core}, {"dp": depths[2] * 2 + core}

    def piece(k):
        return pl.ds(pl.multiple_of(chans[k] * 128 + core * 64 + low * 16, 16), 48)

    def outer(k, which):
        return rows_of(chans[k] * 128 + core * 64 + which * 48, 16)

    fulls, owns = (full1, full2), (own1, own2)
    cut = 5

    def near_move(c, k):
        return remote(owns[c].at[:, pl.ds(pl.multiple_of(core * 64 + low * 16, 16), 48), :], fulls[c].at[:, piece(0), :],
                      w_send.at[c, k - 1], w_recv.at[c, k - 1], {"chan": chans[k]})

    def relay_move(c, k):
        part = fulls[c].at[pl.ds(0, cut) if k == 1 else pl.ds(cut, 9 - cut), piece(k), :]
        return remote(part, part, w_send.at[c, 1 + k], w_recv.at[c, 1 + k], {"chan": chans[3 - k]})

    def side_move(c, k):
        part = fulls[c].at[:, outer(k, low), :]
        return remote(part, part, side_send.at[c, k - 1], side_recv.at[c, k - 1], beside)

    def swap_move(c, k, far):
        part = fulls[c].at[:, outer(k, 1 - low) if far else piece(k), :]
        n = k - 1 + 3 * far
        return remote(part, part, swap_send.at[c, n], swap_recv.at[c, n], {"dp": twin})

    near = [[near_move(c, k) for k in (1, 2)] for c in (0, 1)]
    relay = [[relay_move(c, k) for k in (1, 2)] for c in (0, 1)]
    side = [[side_move(c, k) for k in (1, 2, 3)] for c in (0, 1)]
    swap = [[swap_move(c, k, far) for far in (0, 1) for k in (1, 2, 3)] for c in (0, 1)]

    def weights_near(c):
        for k in (0, 1):
            near[c][k].wait_recv()
            relay[c][k].start()
            side[c][k].start()
            swap[c][k].start()

    def weights_diagonal(c):
        for item in relay[c]:
            item.wait_recv()
        side[c][2].start()
        swap[c][2].start()

    def weights_done(c):
        for k in range(3):
            side[c][k].wait_recv()
            swap[c][3 + k].start()
        loads[2 + c].wait()
        for item in swap[c]:
            item.wait_recv()

    for item in near[0]:
        item.start()
    loads = [
        pltpu.make_async_copy(pack.at[me], packs.at[me], load_sem.at[0]),
        pltpu.make_async_copy(x_in.at[me], x_all.at[rows_of(me * 128, 128), :], load_sem.at[1]),
        pltpu.make_async_copy(own1, full1.at[:, rows_of(me * 128, 128), :], load_sem.at[2]),
        pltpu.make_async_copy(own2, full2.at[:, rows_of(me * 128, 128), :], load_sem.at[3]),
    ]
    for item in loads:
        item.start()

    def raw_in(n):
        return pltpu.make_async_copy(
            feat_grad.at[:, :, n * 512 : (n + 1) * 512], raw.at[n % 2], raw_sem.at[n % 2]
        )

    def image_store(n, half):
        return pltpu.make_async_copy(
            core1.at[n % 4 * 2 + half], by_image.at[half * 256 : (half + 1) * 256, n * 512 : (n + 1) * 512],
            image_sem.at[n % 4, half],
        )

    raw_in(0).start()
    raw_in(1).start()
    take_phases(plain, order_back, stacked, noise, color_phases)
    for n in range(8):
        if n >= 4:
            image_store(n - 4, 0).wait()
            image_store(n - 4, 1).wait()
        raw_in(n).wait()

        @pl.loop(0, 8)
        def _(i):
            value = jnp.swapaxes(raw[n % 2, rows_of(i * 16, 16), :, :], 0, 1)
            for image in range(4):
                core1[n % 4 * 2 + image // 2, rows_of(image % 2 * 128 + i * 16, 16), :] = value[image]

        image_store(n, 0).start()
        image_store(n, 1).start()
        if n + 2 < 8:
            raw_in(n + 2).start()
        if n == 1:
            weights_near(0)
            for item in x_moves:
                item.start()
        if n == 6:
            weights_diagonal(0)
            for item in near[1]:
                item.start()
    loads[0].wait()
    for item in pack_moves:
        item.wait_recv()
    take_rows(packs, rows_ref, cols)
    loads[1].wait()
    for item in x_moves:
        item.wait_recv()

    @pl.loop(0, x_all.shape[0] // 32)
    def _(i):
        rows = rows_of(i * 32, 32)
        style = jnp.concatenate([cols[0, rows, :]] * 8, axis=1)
        value = (x_all[rows, :].astype(F32) * style).astype(BF)
        scaled_one[rows, :] = value
        for r in (0, 1):
            for q in (0, 1):
                copies[2 * r + q, rows, :] = move(value, r, q)

    weights_done(0)
    store1 = pltpu.make_async_copy(full1, full1_out, store_sem.at[0])
    store1.start()
    demodulate(full1, rows_ref[3:4, :] * rows_ref[3:4, :], demod1)

    def part_of(j):
        return rows_of(j * 4 * TILE, 4 * TILE)

    def grad_move(j, k):
        return remote(by_image.at[rows_of(chans[k] * 128, 128), part_of(j)], arrived.at[rows_of(me * 128, 128), part_of(j)],
                      grad_send.at[j, k - 1], grad_recv.at[j, k - 1], {"chan": chans[k]})

    for n in range(4, 8):
        image_store(n, 0).wait()
        image_store(n, 1).wait()
    local3 = pltpu.make_async_copy(by_image.at[rows_of(me * 128, 128), :], arrived.at[rows_of(me * 128, 128), :], store_sem.at[4])
    stores = [
        pltpu.make_async_copy(x_all, x_out, store_sem.at[1]),
        pltpu.make_async_copy(scaled_one, scaled_one_out, store_sem.at[2]),
    ]
    for item in stores:
        item.start()
    tiles = copies.shape[2] // TILE
    channels = cols.shape[1]

    def raised_store(j, slot):
        return pltpu.make_async_copy(tile.at[slot], raised_out.at[:, :, rows_of(j * TILE, TILE)], tile_sem.at[0, slot])

    @pl.loop(0, tiles)
    def _(j):
        here = rows_of(j * TILE, TILE)
        slot = j % 2

        @pl.when(j >= 2)
        def _():
            raised_store(j - 2, slot).wait()

        for phase, (row_phase, col_phase) in enumerate(phase_pairs):
            summed = None
            for k, r in phase_taps[row_phase]:
                for l, q in phase_taps[col_phase]:
                    term = dot(full1[3 * k + l], copies[2 * r + q, :, here])
                    summed = term if summed is None else summed + term
            tile[slot, phase] = summed
            noise_row = gains[0] * noise[phase : phase + 1, here]
            for i in range(channels // ROWS):
                rows = slice(i * ROWS, (i + 1) * ROWS)
                pre = tile[slot, phase, rows, :] * wide(demod1[rows, :]) + noise_row + wide(cols[3, rows, :])
                act = pre * (0.6 * root_two + 0.4 * root_two * jnp.tanh(0.5 * pre))
                scaled[phase, rows, here] = (act * wide(cols[1, rows, :])).astype(BF)

        raised_store(j, slot).start()

        @pl.when(j == 0)
        def _():
            weights_near(1)
            for part in range(4):
                for k in (1, 2, 3):
                    grad_move(part, k).start()
            local3.start()

        @pl.when(j == 1)
        def _():
            weights_diagonal(1)

    make_copies(scaled, copies)
    weights_done(1)
    demodulate(full2, rows_ref[4:5, :] * rows_ref[4:5, :], demod2)
    rgb_rows = jnp.concatenate([rows_ref[...] * rows_ref[5:6, :]] * 2, axis=0).astype(BF)
    live = gains[2]
    rgb_grad[...] = jnp.zeros_like(rgb_grad)

    def tile_stores(j, slot):
        return (
            pltpu.make_async_copy(tile.at[slot], conv_out.at[:, :, rows_of(j * TILE, TILE)], tile_sem.at[0, slot]),
            pltpu.make_async_copy(grad_tile.at[slot], feat_natural.at[:, part_of(j)], tile_sem.at[1, slot]),
        )

    raised_store(2, 0).wait()
    raised_store(3, 1).wait()
    for item in stores:
        item.wait()

    @pl.loop(0, tiles)
    def _(j):
        here = rows_of(j * TILE, TILE)
        slot = j % 2

        @pl.when(j >= 2)
        def _():
            for item in tile_stores(j - 2, slot):
                item.wait()

        for phase in range(4):
            summed = None
            for t in range(9):
                term = dot(full2[t], copies[copy_index(phase, t // 3 - 1, t % 3 - 1), :, here])
                summed = term if summed is None else summed + term
            tile[slot, phase] = summed
            noise_row = gains[1] * noise[4 + phase : 5 + phase, here]
            for i in range(channels // ROWS):
                rows = slice(i * ROWS, (i + 1) * ROWS)
                pre = tile[slot, phase, rows, :] * wide(demod2[rows, :]) + noise_row + wide(cols[4, rows, :])
                act = pre * (0.6 * root_two + 0.4 * root_two * jnp.tanh(0.5 * pre))
                out = (act * live).astype(BF)
                low = slice(i * ROWS % 256, i * ROWS % 256 + ROWS)
                for half in range(TILE // 128):
                    core1[2 * half + i * ROWS // 256, low, phase * 128 : (phase + 1) * 128] = (
                        out[:, half * 128 : (half + 1) * 128]
                    )
        for half in range(TILE // 128):
            image = dot(core1[2 * half : 2 * half + 2].reshape(channels, 512), order[...]).astype(BF)
            grad_tile[slot, :, half * 512 : (half + 1) * 512] = image
            pixels = rows_of(j * 4 * TILE + half * 512, 512)
            color[:, pixels] = dot(rgb_rows, image)
            rgb_grad[...] += dot_nt(stacked[:, pixels], image)
        for item in tile_stores(j, slot):
            item.start()

    for j in (2, 3):
        for item in tile_stores(j, j % 2):
            item.wait()
    store1.wait()
    for item in pack_moves + x_moves + near[0] + near[1] + relay[0] + relay[1] + side[0] + side[1] + swap[0] + swap[1]:
        item.wait_send()

    shared_moves = [
        remote(shared, every_shared.at[row], shared_send.at[i], shared_recv.at[i], {"dp": line})
        for i, line in enumerate(lines)
    ]
    for item in shared_moves:
        item.start()
    every_shared[row] = shared[...]

    quarter = color.shape[1] // 4
    color_moves = [
        remote(color.at[0:8, rows_of(chans[k] * quarter, quarter)], color_in.at[me],
               color_send.at[k - 1], color_recv.at[k - 1], {"chan": chans[k]})
        for k in (1, 2, 3)
    ]
    for item in color_moves:
        item.start()
    color_own = pltpu.make_async_copy(color.at[0:8, rows_of(me * quarter, quarter)], color_in.at[me], load_sem.at[9])
    color_own.start()

    feat_moves = [
        remote(feat_natural.at[rows_of(chans[k] * 128, 128), :], feat_all.at[rows_of(me * 128, 128), :],
               feat_send.at[k - 1], feat_recv.at[k - 1], {"chan": chans[k]})
        for k in (1, 2, 3)
    ]
    for item in feat_moves:
        item.start()
    feat_own = pltpu.make_async_copy(
        feat_natural.at[rows_of(me * 128, 128), :], feat_all.at[rows_of(me * 128, 128), :], load_sem.at[0]
    )
    feat_own.start()
    weight, keep, send = full2, full1.at[:, 0:256, :], full1.at[:, 256:512, :]

    def tiles_in(source, j, slot):
        return pltpu.make_async_copy(source.at[:, :, rows_of(j * TILE, TILE)], tile.at[slot], tile_sem.at[0, slot])

    def grads_in(j, slot):
        return pltpu.make_async_copy(
            arrived.at[:, part_of(j)], grad_tile.at[slot], tile_sem.at[1, slot]
        )

    def grads_ready(j):
        for k in (1, 2, 3):
            grad_move(j, k).wait_recv()
        grads_in(j, j % 2).start()

    tiles_in(conv_out, 0, 0).start()
    local3.wait()
    grads_ready(0)
    sums2[...] = jnp.zeros_like(sums2)
    sums1[...] = jnp.zeros_like(sums1)
    style_sums[...] = jnp.zeros_like(style_sums)
    is_color = lax.broadcasted_iota(jnp.int32, (16, channels), 0) < 3
    rgb_rows = jnp.where(is_color, jnp.concatenate([rows_ref[...]] * 2, axis=0), 0.0).astype(BF)

    def add_sums(sums, rows, values):
        for n, value in enumerate(values):
            sums[n, rows, :] += value[:, :128] + value[:, 128:]

    @pl.loop(0, tiles)
    def _(j):
        slot = j % 2

        @pl.when(j + 1 < tiles)
        def _():
            tiles_in(conv_out, j + 1, 1 - slot).start()
            grads_ready(j + 1)

        tiles_in(conv_out, j, slot).wait()
        grads_in(j, slot).wait()
        here = rows_of(j * TILE, TILE)
        for half in range(TILE // 128):
            total[half] = dot(grad_tile[slot, :, half * 512 : (half + 1) * 512], order_back[...])
        for phase in range(4):
            noise_plain = noise[4 + phase : 5 + phase, here]
            noise_row = gains[1] * noise_plain
            back[phase % 2] = lax.dot_general(
                rgb_rows, color_phases[phase, :, here], (((0,), (0,)), ((), ())), preferred_element_type=F32
            )
            for i in range(channels // ROWS):
                rows = slice(i * ROWS, (i + 1) * ROWS)
                conv = tile[slot, phase, rows, :]
                scale = wide(demod2[rows, :])
                pre = conv * scale + noise_row + wide(cols[4, rows, :])
                sigma = 0.5 + 0.5 * jnp.tanh(0.5 * pre)
                slope = root_two * (0.2 + 0.8 * sigma * (1.0 + pre * (1.0 - sigma)))
                grad_feat = jnp.concatenate(
                    [total[half, rows, phase * 128 : (phase + 1) * 128] for half in range(TILE // 128)], axis=1
                )
                grad = (grad_feat * live + back[phase % 2, rows, :] * wide(cols[2, rows, :])) * slope
                copies[4 * phase, rows, here] = (grad * scale).astype(BF)
                add_sums(sums2, rows, (grad * conv, grad, grad * noise_plain))

    tiles_in(raised_out, 0, 0).start()
    late = [
        pltpu.make_async_copy(scaled_one_out, grad_tile.at[0], load_sem.at[4]),
        pltpu.make_async_copy(x_out, grad_tile.at[1], load_sem.at[5]),
    ]
    for item in late:
        item.start()

    def inner_of(sums, demod, inner):
        scale = demod[...]
        inner[...] = -0.5 * scale * scale * scale * jnp.sum(sums[0], axis=1, keepdims=True)

    inner_of(sums2, demod2, inner2)

    def spread_copies():
        chunk = 32

        @pl.loop(0, channels // chunk)
        def _(i):
            rows = rows_of(i * chunk, chunk)
            for phase in range(4):
                value = copies[4 * phase, rows, :]
                row_sign = 1 if phase // 2 == 0 else -1
                col_sign = 1 if phase % 2 == 0 else -1
                for r, q in ((0, 1), (1, 0), (1, 1)):
                    copies[4 * phase + 2 * r + q, rows, :] = move(value, row_sign * r, col_sign * q)

    spread_copies()

    def split(c, slot, t, inner, square_row):
        for k in range(4):
            base = chans[k] * 128
            for out, start in ((keep, base + core * 64), (send, base + 64 - core * 64)):
                rows = rows_of(start, 64)
                column = jnp.concatenate([inner[rows, :]] * 4, axis=1)
                plain = weight[t, rows, :].astype(F32)
                scaled = plain * column
                value = (total[slot, rows, :] + scaled * square_row).astype(BF)
                out[t, k * 32 : (k + 1) * 32, :] = value[:32]
                out[t, 128 + k * 32 : 160 + k * 32, :] = value[32:]
                scaled = plain * scaled
                style_sums[c] += sum(scaled[i * 8 : (i + 1) * 8, :] for i in range(8))

    cores, quads, zsums, zins, outs = (core1, core2), (quad1, quad2), (zsum1, zsum2), (zin1, zin2), (out1, out2)
    firsts = (first1, first2)

    def taps(g):
        return pl.ds(3 * g, 3)

    def core_move(c, g):
        return remote(send.at[taps(g)], cores[c].at[taps(g)], core_send.at[c, g], core_recv.at[c, g], {"dp": twin})

    def first_move(c, g):
        return remote(keep.at[taps(g), rows_of(128 - low * 128, 128), :], firsts[c].at[taps(g)],
                      first_send.at[c, g], first_recv.at[c, g], beside)

    def quad_move(c, g, k):
        return remote(keep.at[taps(g), rows_of(low * 128 + k * 32, 32), :], quads[c].at[taps(g), k - 1],
                      quad_send.at[c, g, k - 1], quad_recv.at[c, g, k - 1], {"chan": chans[k]})

    def z_move(c, g):
        return remote(zsums[c].at[taps(g), rows_of(16 - high * 16, 16), :], zins[c].at[taps(g)],
                      z_send.at[c, g], z_recv.at[c, g], across)

    def across_move(c, g):
        part = outs[c].at[taps(g), rows_of(core * 64 + low * 32 + high * 16, 16), :]
        return remote(part, part, across_send.at[c, g], across_recv.at[c, g], across)

    def beside_move(c, g):
        part = outs[c].at[taps(g), rows_of(core * 64 + low * 32, 32), :]
        return remote(part, part, beside_send.at[c, g], beside_recv.at[c, g], beside)

    def twin_move(c, g):
        part = outs[c].at[taps(g), rows_of(core * 64, 64), :]
        return remote(part, part, twin_send.at[c, g], twin_recv.at[c, g], {"dp": twin})

    def join_cores(c, g):
        core_move(c, g).wait_recv()
        for i in range(3):
            t = 3 * g + i
            keep[t] = (keep[t].astype(F32) + cores[c][t].astype(F32)).astype(BF)
        first_move(c, g).start()

    def join_first(c, g):
        first_move(c, g).wait_recv()
        rows = rows_of(low * 128, 128)
        for i in range(3):
            t = 3 * g + i
            keep[t, rows, :] = (keep[t, rows, :].astype(F32) + firsts[c][t].astype(F32)).astype(BF)
        for k in (1, 2, 3):
            quad_move(c, g, k).start()

    def join_quad(c, g):
        for k in (1, 2, 3):
            quad_move(c, g, k).wait_recv()
        for i in range(3):
            t = 3 * g + i
            value = keep[t, rows_of(low * 128, 32), :].astype(F32)
            for k in range(3):
                value = value + quads[c][t, k].astype(F32)
            zsums[c][t] = value.astype(BF)
        z_move(c, g).start()

    def join_depth(c, g):
        z_move(c, g).wait_recv()
        for i in range(3):
            t = 3 * g + i
            value = zsums[c][t, rows_of(high * 16, 16), :].astype(F32) + zins[c][t].astype(F32)
            outs[c][t, rows_of(core * 64 + low * 32 + high * 16, 16), :] = value.astype(BF)
        across_move(c, g).start()

    def join_across(c, g):
        across_move(c, g).wait_recv()
        beside_move(c, g).start()

    def join_beside(c, g):
        beside_move(c, g).wait_recv()
        twin_move(c, g).start()

    def weight_grad(c, product, inner, square_row):
        @pl.loop(0, 3)
        def _(g):
            t = 3 * g
            total[0] = product(t)
            total[1] = product(t + 1)
            split(c, 0, t, inner, square_row)
            total[0] = product(t + 2)
            split(c, 1, t + 1, inner, square_row)
            split(c, 0, t + 2, inner, square_row)
            core_move(c, g).start()

            @pl.when(g >= 1)
            def _():
                join_cores(c, g - 1)

        join_cores(c, 2)
        for g in range(3):
            core_move(c, g).wait_send()

    def second_product(t):
        row_step, col_step = 1 - t // 3, 1 - t % 3
        summed = None
        for phase in range(4):
            a, b = phase // 2, phase % 2
            far_row = (row_step * (2 * a - 1) + 1) // 2 * (row_step * row_step)
            far_col = (col_step * (2 * b - 1) + 1) // 2 * (col_step * col_step)
            index = (((a + row_step + 2) % 2 * 2 + (b + col_step + 2) % 2) * 2 + far_row) * 2 + far_col
            term = dot_nt(copies[index], field[phase])
            summed = term if summed is None else summed + term
        return summed

    weight_grad(1, second_product, inner2, 2.0 * rows_ref[4:5, :] * rows_ref[4:5, :])

    def turn():
        @pl.loop(0, 9)
        def _(t):
            weight[t] = weight[t].T

    turn()

    @pl.loop(0, tiles)
    def _(j):
        slot = j % 2

        @pl.when(j + 1 < tiles)
        def _():
            tiles_in(raised_out, j + 1, 1 - slot).start()

        tiles_in(raised_out, j, slot).wait()
        here = rows_of(j * TILE, TILE)
        for phase in range(4):
            summed = None
            for t in range(9):
                term = dot(weight[t], copies[copy_index(phase, 1 - t // 3, 1 - t % 3), :, here])
                summed = term if summed is None else summed + term
            back[phase % 2] = summed
            noise_plain = noise[phase : phase + 1, here]
            noise_row = gains[0] * noise_plain
            for i in range(channels // ROWS):
                rows = slice(i * ROWS, (i + 1) * ROWS)
                conv = tile[slot, phase, rows, :]
                scale = wide(demod1[rows, :])
                pre = conv * scale + noise_row + wide(cols[3, rows, :])
                sigma = 0.5 + 0.5 * jnp.tanh(0.5 * pre)
                act = root_two * (pre * (0.2 + 0.8 * sigma))
                slope = root_two * (0.2 + 0.8 * sigma * (1.0 + pre * (1.0 - sigma)))
                value = back[phase % 2, rows, :]
                grad = value * wide(cols[1, rows, :]) * slope
                field[phase, rows, here] = (grad * scale).astype(BF)
                add_sums(sums1, rows, (grad * conv, grad, grad * noise_plain, value * act))

        @pl.when(j == 0)
        def _():
            join_first(1, 0)

        @pl.when(j == 1)
        def _():
            join_first(1, 1)
            join_quad(1, 0)

        @pl.when(j == 2)
        def _():
            join_first(1, 2)
            join_quad(1, 1)

    inner_of(sums1, demod1, inner1)
    load1 = pltpu.make_async_copy(full1_out, weight, load_sem.at[1])
    load1.start()

    @pl.loop(0, channels // 32)
    def _(i):
        rows = rows_of(i * 32, 32)
        for phase, (row_phase, col_phase) in enumerate(phase_pairs):
            value = field[phase, rows, :]
            for k, r in phase_taps[row_phase]:
                for l, q in phase_taps[col_phase]:
                    copies[3 * k + l, rows, :] = move(value, -r, -q)

    join_quad(1, 2)
    for g in range(3):
        for k in (1, 2, 3):
            quad_move(1, g, k).wait_send()
        first_move(1, g).wait_send()
    load1.wait()
    for item in late:
        item.wait()
    weight_grad(0, lambda t: dot_nt(copies[t], grad_tile[0]), inner1, 2.0 * rows_ref[3:4, :] * rows_ref[3:4, :])
    style_loads = [
        pltpu.make_async_copy(style_weight.at[j], total.at[0, :, j * 128 : (j + 1) * 128], load_sem.at[6 + j])
        for j in range(3)
    ]
    for item in style_loads:
        item.start()
    for g in range(3):
        join_depth(1, g)
    turn()

    for n in range(tiles):
        here = slice(n * TILE, (n + 1) * TILE)
        summed = None
        for t in range(9):
            term = dot(weight[t], copies[t, :, here])
            summed = term if summed is None else summed + term
        back[n % 2] = summed
        for i in range(channels // ROWS):
            rows = slice(i * ROWS, (i + 1) * ROWS)
            value = back[n % 2, rows, :]
            copies[9, rows, here] = (value * wide(cols[0, rows, :])).astype(BF)
            item = value * grad_tile[1, rows, here].astype(F32)
            item = item[:, :128] + item[:, 128:]
            sums0[rows, :] = item if n == 0 else sums0[rows, :] + item
        if n == 1:
            join_first(0, 0)
    back_moves = [
        remote(copies.at[9, rows_of(chans[k] * 128, 128), :], back_all.at[me],
               back_send.at[k - 1], back_recv.at[k - 1], {"chan": chans[k]})
        for k in (1, 2, 3)
    ]
    for item in back_moves:
        item.start()
    join_first(0, 1)
    back_own = pltpu.make_async_copy(copies.at[9, rows_of(me * 128, 128), :], back_all.at[me], load_sem.at[2])
    back_own.start()

    def as_row(sums):
        return jnp.sum(sums[...].T, axis=0, keepdims=True)

    style_two, style_one = as_row(sums1.at[3]), as_row(sums0)
    color_grad = rgb_grad[0:8, :]
    vector_rows = [
        style_one + 2.0 * rows_ref[3:4, :] * jnp.sum(style_sums[0], axis=0, keepdims=True),
        style_two + 2.0 * rows_ref[4:5, :] * jnp.sum(style_sums[1], axis=0, keepdims=True),
        sum(rows_ref[k : k + 1, :] * color_grad[k : k + 1, :] for k in range(3)),
        as_row(sums1.at[1]),
        as_row(sums2.at[1]),
        jnp.broadcast_to(jnp.sum(as_row(sums1.at[2]), axis=1, keepdims=True), (1, channels)),
        jnp.broadcast_to(jnp.sum(as_row(sums2.at[2]), axis=1, keepdims=True), (1, channels)),
        jnp.zeros((1, channels), F32),
    ]
    for i, value in enumerate(vector_rows):
        for d in range(4):
            vectors[d, i : i + 1, :] = value[:, d * 128 : (d + 1) * 128]
    color_grad = color_grad * rows_ref[5:6, :]
    for d in range(4):
        vectors[d, 8:16, :] = color_grad[:, d * 128 : (d + 1) * 128]
    owned_moves = [
        remote(vectors.at[chans[k]], owned.at[me], owned_send.at[k - 1], owned_recv.at[k - 1], {"chan": chans[k]})
        for k in (1, 2, 3)
    ]
    for item in owned_moves:
        item.start()
    owned[me] = vectors[me]

    for g in range(3):
        join_across(1, g)
    join_quad(0, 0)
    join_first(0, 2)
    for item in owned_moves:
        item.wait_recv()
    for item in style_loads:
        item.wait()
    latent_part = None
    for j in range(3):
        value = jnp.concatenate([owned[d, j : j + 1, :] for d in range(4)] + [jnp.zeros((4, 128), F32)], axis=0)
        term = lax.dot_general(
            value, total[0, :, j * 128 : (j + 1) * 128], (((1,), (1,)), ((), ())), precision=precise, preferred_element_type=F32
        )
        latent_part = term if latent_part is None else latent_part + term
    latent_in[3] = latent_part
    latent_moves = [
        remote(latent_in.at[3], latent_in.at[k - 1], latent_send.at[k - 1], latent_recv.at[k - 1], {"chan": chans[k]})
        for k in (1, 2, 3)
    ]
    every_moves = [
        remote(owned, every.at[row], every_send.at[i], every_recv.at[i], {"dp": line})
        for i, line in enumerate(lines)
    ]
    for item in latent_moves + every_moves:
        item.start()
    every[row] = owned[...]
    join_depth(0, 0)
    join_quad(0, 1)
    for g in range(3):
        join_beside(1, g)

    for item in feat_moves:
        item.wait_recv()
    feat_own.wait()

    def feat_in(n, half):
        return pltpu.make_async_copy(
            feat_all.at[half * 256 : (half + 1) * 256, n * 512 : (n + 1) * 512], core2.at[n % 4 * 2 + half],
            image_sem.at[n % 4, half],
        )

    def feat_store(n):
        return pltpu.make_async_copy(
            raw.at[n % 2], feat_out.at[:, :, n * 512 : (n + 1) * 512], raw_sem.at[n % 2]
        )

    for n in range(4):
        feat_in(n, 0).start()
        feat_in(n, 1).start()
    for n in range(8):
        if n >= 2:
            feat_store(n - 2).wait()
        feat_in(n, 0).wait()
        feat_in(n, 1).wait()

        @pl.loop(0, 8)
        def _(i):
            value = jnp.stack(
                [core2[n % 4 * 2 + image // 2, rows_of(image % 2 * 128 + i * 16, 16), :] for image in range(4)]
            )
            raw[n % 2, rows_of(i * 16, 16), :, :] = jnp.swapaxes(value, 0, 1)

        feat_store(n).start()
        if n + 4 < 8:
            feat_in(n + 4, 0).start()
            feat_in(n + 4, 1).start()
        if n == 2:
            join_depth(0, 1)
        if n == 4:
            join_across(0, 0)
            join_quad(0, 2)
        if n == 6:
            join_across(0, 1)
            join_beside(0, 0)
    join_depth(0, 2)
    join_beside(0, 1)
    for g in range(3):
        twin_move(1, g).wait()
    store2 = pltpu.make_async_copy(out2, grad2_out, load_sem.at[1])
    store2.start()
    join_across(0, 2)
    for item in latent_moves:
        item.wait_recv()
    latent_grad[...] = latent_in[0] + latent_in[1] + latent_in[2] + latent_in[3]
    join_beside(0, 2)
    for g in range(3):
        twin_move(0, g).wait()
    store1 = pltpu.make_async_copy(out1, grad1_out, load_sem.at[3])
    store1.start()
    feat_store(6).wait()
    feat_store(7).wait()
    for c in (0, 1):
        for g in range(3):
            if c == 0:
                first_move(c, g).wait_send()
                for k in (1, 2, 3):
                    quad_move(c, g, k).wait_send()
            z_move(c, g).wait_send()
            across_move(c, g).wait_send()
            beside_move(c, g).wait_send()
    for item in feat_moves:
        item.wait_send()
    for item in back_moves + shared_moves + every_moves + color_moves:
        item.wait()
    for item in owned_moves + latent_moves:
        item.wait_send()
    for j in range(4):
        for k in (1, 2, 3):
            grad_move(j, k).wait_send()
    for item in (back_own, color_own, store2, store1):
        item.wait()


def pick(value, index, axis):
    return lax.dynamic_index_in_dim(value, index, axis, keepdims=False)


def phase_order():
    place = jnp.arange(512)
    row, col = place // SIDE, place % SIDE
    grouped = ((row % 2) * 2 + col % 2) * 128 + (row // 2) * HALF + col // 2
    return (jnp.arange(512)[:, None] == grouped[None, :]).astype(BF)


def image_body(
    feat_in,
    rgb_in,
    latent,
    noise_first,
    noise_second,
    live_count,
    conv_first,
    conv_second,
    style_weight,
    style_bias,
    rgb_weight,
    conv_bias,
    rgb_bias,
    noise_gain,
    feat_grad,
    rgb_grad,
):
    local_ch, images, half_pix = feat_in.shape
    channels = 4 * local_ch
    pixels = feat_grad.shape[2]
    me = lax.axis_index("chan")
    live_mask = (jnp.arange(images) < live_count[0]).astype(F32)
    live = (me < live_count[0]).astype(F32)
    gains = jnp.concatenate([noise_gain, live[None]])
    styles = jnp.einsum("bw,jwc->bjc", latent, style_weight, precision=precise) + style_bias[None]

    def each_image(value):
        return jnp.broadcast_to(value[None], (images,) + value.shape)

    pack = jnp.concatenate([each_image(rgb_weight.astype(F32)), styles, each_image(conv_bias)], axis=1)
    plain = jnp.concatenate(
        [pick(rgb_grad, me, 0) * live, pick(noise_first, me, 0)[None], pick(noise_second, me, 0)[None],
         jnp.zeros((3, pixels), F32)]
    )
    x_by_image = feat_in.transpose(1, 0, 2)
    order = phase_order()

    vmem = pl.BlockSpec(memory_space=pltpu.VMEM)
    field, wide_weight = (4, channels, half_pix), (9, channels, channels)
    rgb_cot = rgb_grad * live_mask[:, None, None]
    rgb_bias_part = jnp.sum(rgb_cot, axis=(0, 2))
    shared = jnp.concatenate([latent, jnp.broadcast_to(jnp.pad(rgb_bias_part, (0, 509))[None], (4, 512))])
    outs = (
        (field, F32), (field, F32), ((channels, pixels), BF), (wide_weight, BF), ((channels, pixels), BF),
        ((channels, half_pix), BF), ((channels, half_pix), BF), ((channels, pixels), BF), ((channels, pixels), BF),
        (feat_grad.shape, BF), ((4, local_ch, half_pix), BF), ((9, local_ch, channels), BF),
        ((9, local_ch, channels), BF), ((4, 8, pixels // 4), F32), ((8, 4, 16, 128), F32), ((8, 8, 512), F32),
        ((8, 512), F32),
    )
    vector = ((channels, 128), F32)
    scratch = (
        vector, vector, ((16, pixels), F32), ((16, channels), F32), ((5, channels, 128), F32), ((8, channels), F32),
        ((8, half_pix), F32), ((4, 16, half_pix), BF), ((4, 8, 128), F32), ((16, pixels), BF),
        (wide_weight, BF), (wide_weight, BF), ((16, channels, half_pix), BF), ((2, 4, channels, TILE), F32),
        ((2, channels, 4 * TILE), BF), (field, BF), ((2, channels, channels), F32), ((2, channels, TILE), F32),
        ((9, 256, channels), BF), ((9, 256, channels), BF), ((9, 128, channels), BF), ((9, 128, channels), BF),
        ((9, 3, 32, channels), BF), ((9, 3, 32, channels), BF), ((9, 32, channels), BF), ((9, 32, channels), BF),
        ((9, 16, channels), BF), ((9, 16, channels), BF),
        ((9, local_ch, channels), BF), ((9, local_ch, channels), BF),
        ((3, channels, 128), F32), ((4, channels, 128), F32), vector, vector, vector, ((2, 8, channels), F32),
        ((4, 16, 128), F32), ((4, 16, 128), F32), ((4, 8, 512), F32), ((2, local_ch, 4, 512), BF),
    )
    counts = (
        [(10,), (5,), (2, 2)] + [(3,)] * 4 + [(2, 4)] * 2 + [(2, 6)] * 2 + [(4, 3)] * 2 + [(3,)] * 4
        + [(2, 3)] * 2 + [(2, 3, 3)] * 2 + [(2, 3)] * 10 + [(7,)] * 4 + [(3,)] * 6 + [(2,), (4, 2), (2, 3), (2, 3)]
    )
    results = pl.pallas_call(
        block_kernel,
        in_specs=[SMEM] + [ANY] * 5 + [vmem] * 3 + [ANY, vmem],
        out_specs=[ANY] * 14 + [vmem] * 3,
        out_shape=[jax.ShapeDtypeStruct(shape, dtype) for shape, dtype in outs],
        scratch_shapes=[pltpu.VMEM(shape, dtype) for shape, dtype in scratch]
        + [pltpu.SemaphoreType.DMA(count) for count in counts],
        compiler_params=pltpu.CompilerParams(vmem_limit_bytes=LIMIT, collective_id=0, has_side_effects=True),
        cost_estimate=pl.CostEstimate(flops=int(150e9), bytes_accessed=12 << 20, transcendentals=0),
    )(gains, pack, x_by_image, conv_first, conv_second, feat_grad, plain, order.T, order, style_weight, shared)
    feat_out, back_all, grad_one, grad_two, color_in, every, every_shared, latent_grad = results[9:]
    feat_in_grad = back_all.transpose(1, 0, 2).astype(F32)
    grad_one, grad_two = grad_one.astype(F32), grad_two.astype(F32)

    lift_matrix = upsample_matrix(HALF)
    shard_pix = pixels // 4
    skip_up = jnp.einsum(
        "up,bkpq,vq->bkuv",
        lift_matrix,
        rgb_in.reshape(images, 3, HALF, HALF),
        lift_matrix,
        precision=precise,
    ).reshape(images, 3, pixels)
    skip_mine = lax.dynamic_slice_in_dim(skip_up, me * shard_pix, shard_pix, 2)
    rgb_out = (color_in[:, :3] + rgb_bias[None, :, None] + skip_mine) * live_mask[:, None, None]
    rgb_in_grad = jnp.einsum(
        "up,bkuv,vq->bkpq",
        lift_matrix,
        rgb_cot.reshape(images, 3, SIDE, SIDE),
        lift_matrix,
        precision=precise,
    ).reshape(images, 3, half_pix)

    summed = jnp.sum(every, axis=(0, 1))
    style_weight_grad = jnp.einsum("gbw,gbjc->jwc", every_shared[:, :4], every[:, :, :3], precision=precise)
    return (
        feat_out,
        rgb_out,
        feat_in_grad,
        rgb_in_grad,
        latent_grad[:4],
        grad_one,
        grad_two,
        style_weight_grad,
        summed[:3],
        summed[8:11],
        summed[3:5],
        jnp.sum(every_shared[:, 4, :3], axis=0),
        summed[5:7, 0],
    )


def solution(mesh):
    alone = mesh.shape["chan"] == 4 and mesh.shape["dp"] == 8
    return jax.shard_map(
        image_body if alone else body,
        mesh=mesh,
        in_specs=(
            P("chan", "dp", None),
            P("dp", None, None),
            P("dp", None),
            P("dp", None),
            P("dp", None),
            P("dp"),
            P(None, "chan", None),
            P(None, "chan", None),
            P(None, None, "chan"),
            P(None, "chan"),
            P(None, "chan"),
            P(None, "chan"),
            P(),
            P(),
            P("chan", "dp", None),
            P("dp", None, None),
        ),
        out_specs=(
            P("chan", "dp", None),
            P("dp", None, "chan"),
            P("chan", "dp", None),
            P("dp", None, None),
            P("dp", None),
            P(None, "chan", None),
            P(None, "chan", None),
            P(None, None, "chan"),
            P(None, "chan"),
            P(None, "chan"),
            P(None, "chan"),
            P(),
            P(),
        ),
        check_vma=False,
    )
```

```python
import functools

import jax
import jax.numpy as jnp
from jax import lax
from jax.experimental import pallas as pl
from jax.experimental.pallas import tpu as pltpu
from jax.sharding import PartitionSpec as P

SIDE = 64
HALF = 32


precise = lax.Precision.HIGHEST
epsilon = 1e-08
root_two = 1.4142135623730951
phase_taps = (((1, 0),), ((2, 0), (0, 1)))
phase_pairs = ((0, 0), (0, 1), (1, 0), (1, 1))


def leaky_silu(value):
    return root_two * (0.2 * value + 0.8 * jax.nn.silu(value))


def leaky_slope(value):
    sigma = jax.nn.sigmoid(value)
    return root_two * (0.2 + 0.8 * sigma * (1.0 + value * (1.0 - sigma)))


def shifted(field, row_shift, col_shift, width):
    cells = field.shape[-1]
    offset = row_shift * width + col_shift
    if offset > 0:
        result = jnp.concatenate(
            [field[..., offset:], jnp.zeros(field.shape[:-1] + (offset,), field.dtype)], axis=-1
        )
    elif offset < 0:
        result = jnp.concatenate(
            [jnp.zeros(field.shape[:-1] + (-offset,), field.dtype), field[..., : cells + offset]],
            axis=-1,
        )
    else:
        result = field
    if col_shift != 0:
        column = jnp.arange(cells) % width
        inside = (column + col_shift >= 0) & (column + col_shift < width)
        result = jnp.where(inside, result, jnp.zeros((), field.dtype))
    return result


def upsample_matrix(half_side):
    rows_out = jnp.arange(2 * half_side)[:, None]
    cols_in = jnp.arange(half_side)[None, :]
    centre = rows_out // 2
    beside = centre - 1 + 2 * (rows_out % 2)
    return (
        jnp.where(cols_in == centre, 0.75, 0.0) + jnp.where(cols_in == beside, 0.25, 0.0)
    ).astype(jnp.float32)


def alternate(phases, half_side):
    stacked = jnp.stack(phases)
    out_rows, batch_count = (stacked.shape[1], stacked.shape[2])
    blocked = stacked.reshape(2, 2, out_rows, batch_count, half_side, half_side)
    return blocked.transpose(2, 3, 4, 0, 5, 1).reshape(
        out_rows, batch_count, 4 * half_side * half_side
    )


def split_phases(field, half_side):
    out_rows, batch_count = (field.shape[0], field.shape[1])
    blocked = field.reshape(out_rows, batch_count, half_side, 2, half_side, 2)
    return [
        blocked[:, :, :, row_phase, :, col_phase].reshape(
            out_rows, batch_count, half_side * half_side
        )
        for row_phase, col_phase in phase_pairs
    ]


def up_conv(inputs, weight, half_side):
    shifted_inputs = {}
    for row_shift in (0, 1):
        for col_shift in (0, 1):
            shifted_inputs[row_shift, col_shift] = shifted(inputs, row_shift, col_shift, half_side)
    phases = []
    for row_phase, col_phase in phase_pairs:
        summed = None
        for row_tap, row_shift in phase_taps[row_phase]:
            for col_tap, col_shift in phase_taps[col_phase]:
                product = jnp.einsum(
                    "oc,cbp->obp",
                    weight[row_tap * 3 + col_tap],
                    shifted_inputs[row_shift, col_shift],
                    preferred_element_type=jnp.float32,
                )
                summed = product if summed is None else summed + product
        phases.append(summed)
    return alternate(phases, half_side)


def phase_grads(grad_field, half_side):
    grad_phases = split_phases(grad_field, half_side)
    shifted_grads = [None] * 9
    for phase_index in range(4):
        row_phase, col_phase = phase_pairs[phase_index]
        for row_tap, row_shift in phase_taps[row_phase]:
            for col_tap, col_shift in phase_taps[col_phase]:
                shifted_grads[row_tap * 3 + col_tap] = shifted(
                    grad_phases[phase_index], -row_shift, -col_shift, half_side
                )
    return shifted_grads


def flat_conv(inputs, weight, width):
    summed = None
    for tap_index in range(9):
        product = jnp.einsum(
            "oc,cbp->obp", weight[tap_index], inputs, preferred_element_type=jnp.float32
        )
        product = shifted(product, tap_index // 3 - 1, tap_index % 3 - 1, width)
        summed = product if summed is None else summed + product
    return summed


def body(
    feat_in,
    rgb_in,
    latent,
    noise_first,
    noise_second,
    live_count,
    conv_first,
    conv_second,
    style_weight,
    style_bias,
    rgb_weight,
    conv_bias,
    rgb_bias,
    noise_gain,
    feat_grad,
    rgb_grad,
):
    local_ch, images, half_pix = feat_in.shape
    pixels = feat_grad.shape[2]
    half_side = HALF
    full_side = SIDE
    chan_rank = lax.axis_index("chan")
    live_mask = (jnp.arange(images) < live_count[0]).astype(jnp.float32)
    styles = (
        jnp.einsum("bw,jwc->jbc", latent, style_weight, precision=precise) + style_bias[:, None, :]
    )
    first_all, second_all = (
        lax.all_gather(styles[0], "chan", axis=1, tiled=True),
        lax.all_gather(styles[1], "chan", axis=1, tiled=True),
    )
    weight_one = conv_first.astype(jnp.float32)
    weight_two = conv_second.astype(jnp.float32)
    squares_one = jnp.sum(weight_one * weight_one, axis=0)
    squares_two = jnp.sum(weight_two * weight_two, axis=0)
    demod_one = lax.rsqrt(
        jnp.dot(first_all * first_all, squares_one.T, precision=precise) + epsilon
    )
    demod_two = lax.rsqrt(
        jnp.dot(second_all * second_all, squares_two.T, precision=precise) + epsilon
    )
    scaled_one = (feat_in.astype(jnp.float32) * styles[0].T[:, :, None]).astype(jnp.bfloat16)
    gathered_one = lax.all_gather(scaled_one, "chan", axis=0, tiled=True)
    raised = up_conv(gathered_one, conv_first, half_side)
    pre_one = (
        raised * demod_one.T[:, :, None]
        + noise_gain[0] * noise_first[None, :, :]
        + conv_bias[0][:, None, None]
    )
    act_one = leaky_silu(pre_one)
    scaled_two = (act_one * styles[1].T[:, :, None]).astype(jnp.bfloat16)
    gathered_two = lax.all_gather(scaled_two, "chan", axis=0, tiled=True)
    convolved = flat_conv(gathered_two, conv_second, full_side)
    pre_two = (
        convolved * demod_two.T[:, :, None]
        + noise_gain[1] * noise_second[None, :, :]
        + conv_bias[1][:, None, None]
    )
    act_two = leaky_silu(pre_two)
    feat_out = (act_two * live_mask[None, :, None]).astype(jnp.bfloat16)
    scaled_rgb = (act_two * styles[2].T[:, :, None]).astype(jnp.bfloat16)
    color_part = jnp.einsum(
        "ko,obp->bkp", rgb_weight, scaled_rgb, preferred_element_type=jnp.float32
    )
    color = lax.psum_scatter(color_part, "chan", scatter_dimension=2, tiled=True)
    shard_pix = color.shape[2]
    lift_matrix = upsample_matrix(half_side)
    skip_up = jnp.einsum(
        "up,bkpq,vq->bkuv",
        lift_matrix,
        rgb_in.reshape(images, 3, half_side, half_side),
        lift_matrix,
        precision=precise,
    ).reshape(images, 3, pixels)
    skip_mine = lax.dynamic_slice_in_dim(skip_up, chan_rank * shard_pix, shard_pix, 2)
    rgb_out = (color + rgb_bias[None, :, None] + skip_mine) * live_mask[:, None, None]
    rgb_cot = rgb_grad * live_mask[:, None, None]
    color_cot = rgb_cot.astype(jnp.bfloat16)
    rgb_in_grad = jnp.einsum(
        "up,bkuv,vq->bkpq",
        lift_matrix,
        rgb_cot.reshape(images, 3, full_side, full_side),
        lift_matrix,
        precision=precise,
    ).reshape(images, 3, half_pix)
    rgb_bias_part = jnp.sum(rgb_cot, axis=(0, 2))
    rgb_weight_part = jnp.einsum(
        "bkp,obp->ko", color_cot, scaled_rgb, preferred_element_type=jnp.float32
    )
    back_rgb = jnp.einsum("ko,bkp->obp", rgb_weight, color_cot, preferred_element_type=jnp.float32)
    style_rgb_grad = jnp.sum(back_rgb * act_two, axis=2).T
    grad_pre_two = (
        feat_grad.astype(jnp.float32) * live_mask[None, :, None]
        + back_rgb * styles[2].T[:, :, None]
    ) * leaky_slope(pre_two)
    cot_two = (grad_pre_two * demod_two.T[:, :, None]).astype(jnp.bfloat16)
    inner_two = (
        -0.5 * demod_two * demod_two * demod_two * jnp.sum(grad_pre_two * convolved, axis=2).T
    )
    taps_two = jnp.stack(
        [
            shifted(cot_two, 1 - tap_index // 3, 1 - tap_index % 3, full_side)
            for tap_index in range(9)
        ]
    )
    squares_two_grad = jnp.dot(inner_two.T, second_all * second_all, precision=precise)
    conv_two_grad = (
        jnp.einsum("tobp,cbp->toc", taps_two, gathered_two, preferred_element_type=jnp.float32)
        + 2.0 * weight_two * squares_two_grad[None]
    )
    style_two_demod = 2.0 * second_all * jnp.dot(inner_two, squares_two, precision=precise)
    columns = conv_second
    back_two = lax.psum_scatter(
        jnp.einsum("toc,tobp->cbp", columns, taps_two, preferred_element_type=jnp.float32),
        "chan",
        scatter_dimension=0,
        tiled=True,
    )
    style_two_conv = jnp.sum(back_two * act_one, axis=2).T
    grad_pre_one = back_two * styles[1].T[:, :, None] * leaky_slope(pre_one)
    cot_one = (grad_pre_one * demod_one.T[:, :, None]).astype(jnp.bfloat16)
    inner_one = -0.5 * demod_one * demod_one * demod_one * jnp.sum(grad_pre_one * raised, axis=2).T
    taps_one = jnp.stack(phase_grads(cot_one, half_side))
    squares_one_grad = jnp.dot(inner_one.T, first_all * first_all, precision=precise)
    conv_one_grad = (
        jnp.einsum("tobp,cbp->toc", taps_one, gathered_one, preferred_element_type=jnp.float32)
        + 2.0 * weight_one * squares_one_grad[None]
    )
    style_one_demod = 2.0 * first_all * jnp.dot(inner_one, squares_one, precision=precise)
    columns = conv_first
    back_one = lax.psum_scatter(
        jnp.einsum("toc,tobp->cbp", columns, taps_one, preferred_element_type=jnp.float32),
        "chan",
        scatter_dimension=0,
        tiled=True,
    )
    feat_in_grad = back_one * styles[0].T[:, :, None]
    style_one_conv = jnp.sum(back_one * feat_in.astype(jnp.float32), axis=2).T
    demod_one_sum, demod_two_sum = (
        lax.psum_scatter(style_one_demod, "chan", scatter_dimension=1, tiled=True),
        lax.psum_scatter(style_two_demod, "chan", scatter_dimension=1, tiled=True),
    )
    style_grads = jnp.stack(
        [style_one_conv + demod_one_sum, style_two_conv + demod_two_sum, style_rgb_grad]
    )
    latent_part = jnp.einsum("jbc,jwc->bw", style_grads, style_weight, precision=precise)
    gain_part = jnp.stack(
        [
            jnp.sum(grad_pre_one * noise_first[None, :, :]),
            jnp.sum(grad_pre_two * noise_second[None, :, :]),
        ]
    )
    latent_grad, gain_chan = lax.psum((latent_part, gain_part), "chan")
    style_weight_part = jnp.einsum("bw,jbc->jwc", latent, style_grads, precision=precise)
    style_bias_part = jnp.sum(style_grads, axis=1)
    conv_bias_part = jnp.stack(
        [jnp.sum(grad_pre_one, axis=(1, 2)), jnp.sum(grad_pre_two, axis=(1, 2))]
    )
    totals = lax.psum(
        (
            conv_one_grad,
            conv_two_grad,
            style_weight_part,
            style_bias_part,
            rgb_weight_part,
            conv_bias_part,
            rgb_bias_part,
            gain_chan,
        ),
        "dp",
    )
    return (feat_out, rgb_out, feat_in_grad, rgb_in_grad, latent_grad) + tuple(totals)


BF = jnp.bfloat16
F32 = jnp.float32
TILE = 256
ROWS = 16
ANY = pl.BlockSpec(memory_space=pl.ANY)
SMEM = pl.BlockSpec(memory_space=pltpu.SMEM)
LIMIT = 60 * 1024 * 1024


def whole(shape):
    return pl.BlockSpec(shape, lambda j: (0,) * len(shape))


def dot(a, b):
    return jnp.dot(a, b, preferred_element_type=F32)


def dot_nt(a, b):
    return lax.dot_general(a, b, (((1,), (1,)), ((), ())), preferred_element_type=F32)


def wide(column):
    return jnp.concatenate([column] * (TILE // 128), axis=1)


def move(field, row_shift, col_shift):
    offset = row_shift * HALF + col_shift
    if offset == 0:
        return field
    cells = field.shape[1]
    lane = lax.broadcasted_iota(jnp.int32, (1, cells), 1)
    row, col = lane // HALF, lane % HALF
    inside = (row + row_shift >= 0) & (row + row_shift < HALF)
    inside = inside & (col + col_shift >= 0) & (col + col_shift < HALF)
    rolled = pltpu.roll(field, (-offset) % cells, 1)
    return rolled * jnp.where(inside, 1.0, 0.0).astype(field.dtype)


def near(parity, step):
    other = (parity + step) % 2
    return other, (parity + step - other) // 2


def copy_index(phase, row_step, col_step):
    a, r = near(phase // 2, row_step)
    b, q = near(phase % 2, col_step)
    return ((a * 2 + b) * 2 + abs(r)) * 2 + abs(q)


def make_copies(source, copies):
    chunk = 32

    @pl.loop(0, source.shape[1] // chunk)
    def _(i):
        rows = pl.ds(pl.multiple_of(i * chunk, chunk), chunk)
        for phase in range(4):
            field = source[phase, rows, :]
            row_sign = 1 if phase // 2 == 0 else -1
            col_sign = 1 if phase % 2 == 0 else -1
            for r in (0, 1):
                for q in (0, 1):
                    copies[(phase * 2 + r) * 2 + q, rows, :] = move(
                        field, row_sign * r, col_sign * q
                    )


def demodulate(full, square_row, demod):
    chunk = 32

    @pl.loop(0, full.shape[1] // chunk)
    def _(i):
        rows = pl.ds(pl.multiple_of(i * chunk, chunk), chunk)
        total = None
        for t in range(9):
            value = full[t, rows, :].astype(F32)
            total = value * value if total is None else total + value * value
        total = jnp.sum(total * square_row, axis=1, keepdims=True)
        demod[rows, :] = jnp.broadcast_to(lax.rsqrt(total + epsilon), (chunk, 128))


def chan_peer(me, k):
    if k == 1:
        return me + 1 - 2 * (me % 2)
    return (me + 2) % 4 if k == 2 else 3 - me


def rows_of(base, size):
    return pl.ds(pl.multiple_of(base, size), size)


def take_rows(packs, rows_ref, cols):
    for d in range(4):
        here = slice(d * 128, (d + 1) * 128)
        pack = packs[d]
        rows_ref[:, here] = pack
        for j in range(3, 8):
            cols[j - 3, here, :] = jnp.broadcast_to(pack[j : j + 1, :], (128, 128)).T


def take_phases(plain, order, stacked, noise, color_phases):
    lanes = 512
    for n in range(plain.shape[1] // lanes):
        here = slice(n * lanes, (n + 1) * lanes)
        value = plain[:, here]
        first = value.astype(BF)
        rest = value - first.astype(F32)
        second = rest.astype(BF)
        third = rest - second.astype(F32)
        part = jnp.concatenate([first.astype(F32), second.astype(F32)], axis=0).astype(BF)
        stacked[:, here] = part
        high = dot(part, order[...])
        low = dot(jnp.concatenate([third, third], axis=0).astype(BF), order[...])
        for phase in range(4):
            grouped = slice(phase * 128, (phase + 1) * 128)
            out = slice(n * 128, (n + 1) * 128)
            color_phases[phase, :, out] = high[:, grouped].astype(BF)
            for i in (0, 1):
                noise[4 * i + phase : 4 * i + phase + 1, out] = (
                    high[3 + i : 4 + i, grouped] + high[11 + i : 12 + i, grouped] + low[3 + i : 4 + i, grouped]
                )


def block_kernel(gains, pack, x_in, own1, own2, feat_grad, plain, order_back, order, style_weight, shared,
                 raised_out, conv_out, feat_natural, full1_out, arrived, x_out, scaled_one_out, by_image, feat_all,
                 feat_out, back_all, grad1_out, grad2_out, color_in, style_out, sums_all, shared_sum, latent_grad,
                 demod1, demod2, color, rgb_grad, cols, rows_ref, noise, color_phases, packs, stacked,
                 full1, full2, copies, tile, grad_tile, field, total, back,
                 core1, core2, first1, first2, quad1, quad2, zsum1, zsum2, zin1, zin2, out1, out2,
                 sums2, sums1, sums0, inner2, inner1, style_sums, vectors, owned, latent_in, raw, every, every_shared,
                 load_sem, store_sem, tile_sem, pack_send, pack_recv, x_send, x_recv, w_send, w_recv,
                 swap_send, swap_recv, grad_send, grad_recv, feat_send, feat_recv, back_send, back_recv,
                 core_send, core_recv, quad_send, quad_recv, z_send, z_recv, across_send, across_recv, twin_send, twin_recv,
                 first_send, first_recv, beside_send, beside_recv,
                 shared_send, shared_recv, every_send, every_recv, owned_send, owned_recv, latent_send, latent_recv,
                 color_send, color_recv, raw_sem, image_sem, side_send, side_recv):
    me = lax.axis_index("chan")
    row = lax.axis_index("dp")
    core = row % 2
    depth = row // 2
    twin = row + 1 - 2 * core
    mesh_id = pl.DeviceIdType.MESH
    chans = [me] + [chan_peer(me, k) for k in (1, 2, 3)]
    depths = [depth] + [chan_peer(depth, k) for k in (1, 2, 3)]
    lines = [depths[k] * 2 + core for k in (1, 2, 3)] + [twin] + [depths[k] * 2 + 1 - core for k in (1, 2, 3)]
    barrier = pltpu.get_barrier_semaphore()
    for k in (1, 2, 3):
        pl.semaphore_signal(barrier, inc=1, device_id={"chan": chans[k]}, device_id_type=mesh_id)
    for line in lines:
        pl.semaphore_signal(barrier, inc=1, device_id={"dp": line}, device_id_type=mesh_id)
    pl.semaphore_wait(barrier, 10)

    def remote(source, target, sent, received, where):
        return pltpu.make_async_remote_copy(source, target, sent, received, device_id=where, device_id_type=mesh_id)

    x_all, scaled_one, scaled = grad_tile.at[1], grad_tile.at[0], field
    pack_moves = [
        remote(pack.at[chans[k]], packs.at[me], pack_send.at[k - 1], pack_recv.at[k - 1], {"chan": chans[k]})
        for k in (1, 2, 3)
    ]
    x_moves = [
        remote(x_in.at[chans[k]], x_all.at[rows_of(me * 128, 128), :], x_send.at[k - 1], x_recv.at[k - 1],
               {"chan": chans[k]})
        for k in (1, 2, 3)
    ]
    for item in pack_moves:
        item.start()

    low, high = depth % 2, depth // 2
    beside, across = {"dp": depths[1] * 2 + core}, {"dp": depths[2] * 2 + core}

    def piece(k):
        return pl.ds(pl.multiple_of(chans[k] * 128 + core * 64 + low * 16, 16), 48)

    def outer(k, which):
        return rows_of(chans[k] * 128 + core * 64 + which * 48, 16)

    fulls, owns = (full1, full2), (own1, own2)
    cut = 5

    def near_move(c, k):
        return remote(owns[c].at[:, pl.ds(pl.multiple_of(core * 64 + low * 16, 16), 48), :], fulls[c].at[:, piece(0), :],
                      w_send.at[c, k - 1], w_recv.at[c, k - 1], {"chan": chans[k]})

    def relay_move(c, k):
        part = fulls[c].at[pl.ds(0, cut) if k == 1 else pl.ds(cut, 9 - cut), piece(k), :]
        return remote(part, part, w_send.at[c, 1 + k], w_recv.at[c, 1 + k], {"chan": chans[3 - k]})

    def side_move(c, k):
        part = fulls[c].at[:, outer(k, low), :]
        return remote(part, part, side_send.at[c, k - 1], side_recv.at[c, k - 1], beside)

    def swap_move(c, k, far):
        part = fulls[c].at[:, outer(k, 1 - low) if far else piece(k), :]
        n = k - 1 + 3 * far
        return remote(part, part, swap_send.at[c, n], swap_recv.at[c, n], {"dp": twin})

    near = [[near_move(c, k) for k in (1, 2)] for c in (0, 1)]
    relay = [[relay_move(c, k) for k in (1, 2)] for c in (0, 1)]
    side = [[side_move(c, k) for k in (1, 2, 3)] for c in (0, 1)]
    swap = [[swap_move(c, k, far) for far in (0, 1) for k in (1, 2, 3)] for c in (0, 1)]

    def weights_near(c):
        for k in (0, 1):
            near[c][k].wait_recv()
            relay[c][k].start()
            side[c][k].start()
            swap[c][k].start()

    def weights_diagonal(c):
        for item in relay[c]:
            item.wait_recv()
        side[c][2].start()
        swap[c][2].start()

    def weights_done(c):
        for k in range(3):
            side[c][k].wait_recv()
            swap[c][3 + k].start()
        loads[2 + c].wait()
        for item in swap[c]:
            item.wait_recv()

    for item in near[0]:
        item.start()
    loads = [
        pltpu.make_async_copy(pack.at[me], packs.at[me], load_sem.at[0]),
        pltpu.make_async_copy(x_in.at[me], x_all.at[rows_of(me * 128, 128), :], load_sem.at[1]),
        pltpu.make_async_copy(own1, full1.at[:, rows_of(me * 128, 128), :], load_sem.at[2]),
        pltpu.make_async_copy(own2, full2.at[:, rows_of(me * 128, 128), :], load_sem.at[3]),
    ]
    for item in loads:
        item.start()

    def raw_in(n):
        return pltpu.make_async_copy(
            feat_grad.at[:, :, n * 512 : (n + 1) * 512], raw.at[n % 2], raw_sem.at[n % 2]
        )

    def image_store(n, half):
        return pltpu.make_async_copy(
            core1.at[n % 4 * 2 + half], by_image.at[half * 256 : (half + 1) * 256, n * 512 : (n + 1) * 512],
            image_sem.at[n % 4, half],
        )

    raw_in(0).start()
    raw_in(1).start()
    take_phases(plain, order_back, stacked, noise, color_phases)
    for n in range(8):
        if n >= 4:
            image_store(n - 4, 0).wait()
            image_store(n - 4, 1).wait()
        raw_in(n).wait()

        @pl.loop(0, 8)
        def _(i):
            value = jnp.swapaxes(raw[n % 2, rows_of(i * 16, 16), :, :], 0, 1)
            for image in range(4):
                core1[n % 4 * 2 + image // 2, rows_of(image % 2 * 128 + i * 16, 16), :] = value[image]

        image_store(n, 0).start()
        image_store(n, 1).start()
        if n + 2 < 8:
            raw_in(n + 2).start()
        if n == 1:
            weights_near(0)
            for item in x_moves:
                item.start()
        if n == 6:
            weights_diagonal(0)
            for item in near[1]:
                item.start()
    loads[0].wait()
    for item in pack_moves:
        item.wait_recv()
    take_rows(packs, rows_ref, cols)
    loads[1].wait()
    for item in x_moves:
        item.wait_recv()

    @pl.loop(0, x_all.shape[0] // 32)
    def _(i):
        rows = rows_of(i * 32, 32)
        style = jnp.concatenate([cols[0, rows, :]] * 8, axis=1)
        value = (x_all[rows, :].astype(F32) * style).astype(BF)
        scaled_one[rows, :] = value
        for r in (0, 1):
            for q in (0, 1):
                copies[2 * r + q, rows, :] = move(value, r, q)

    weights_done(0)
    store1 = pltpu.make_async_copy(full1, full1_out, store_sem.at[0])
    store1.start()
    demodulate(full1, rows_ref[3:4, :] * rows_ref[3:4, :], demod1)

    def part_of(j):
        return rows_of(j * 4 * TILE, 4 * TILE)

    def grad_move(j, k):
        return remote(by_image.at[rows_of(chans[k] * 128, 128), part_of(j)], arrived.at[rows_of(me * 128, 128), part_of(j)],
                      grad_send.at[j, k - 1], grad_recv.at[j, k - 1], {"chan": chans[k]})

    for n in range(4, 8):
        image_store(n, 0).wait()
        image_store(n, 1).wait()
    local3 = pltpu.make_async_copy(by_image.at[rows_of(me * 128, 128), :], arrived.at[rows_of(me * 128, 128), :], store_sem.at[4])
    stores = [
        pltpu.make_async_copy(x_all, x_out, store_sem.at[1]),
        pltpu.make_async_copy(scaled_one, scaled_one_out, store_sem.at[2]),
    ]
    for item in stores:
        item.start()
    tiles = copies.shape[2] // TILE
    channels = cols.shape[1]

    def raised_store(j, slot):
        return pltpu.make_async_copy(tile.at[slot], raised_out.at[:, :, rows_of(j * TILE, TILE)], tile_sem.at[0, slot])

    @pl.loop(0, tiles)
    def _(j):
        here = rows_of(j * TILE, TILE)
        slot = j % 2

        @pl.when(j >= 2)
        def _():
            raised_store(j - 2, slot).wait()

        for phase, (row_phase, col_phase) in enumerate(phase_pairs):
            summed = None
            for k, r in phase_taps[row_phase]:
                for l, q in phase_taps[col_phase]:
                    term = dot(full1[3 * k + l], copies[2 * r + q, :, here])
                    summed = term if summed is None else summed + term
            tile[slot, phase] = summed
            noise_row = gains[0] * noise[phase : phase + 1, here]
            for i in range(channels // ROWS):
                rows = slice(i * ROWS, (i + 1) * ROWS)
                pre = tile[slot, phase, rows, :] * wide(demod1[rows, :]) + noise_row + wide(cols[3, rows, :])
                act = pre * (0.6 * root_two + 0.4 * root_two * jnp.tanh(0.5 * pre))
                scaled[phase, rows, here] = (act * wide(cols[1, rows, :])).astype(BF)

        raised_store(j, slot).start()

        @pl.when(j == 0)
        def _():
            weights_near(1)
            for part in range(4):
                for k in (1, 2, 3):
                    grad_move(part, k).start()
            local3.start()

        @pl.when(j == 1)
        def _():
            weights_diagonal(1)

    make_copies(scaled, copies)
    weights_done(1)
    demodulate(full2, rows_ref[4:5, :] * rows_ref[4:5, :], demod2)
    rgb_rows = jnp.concatenate([rows_ref[...] * rows_ref[5:6, :]] * 2, axis=0).astype(BF)
    live = gains[2]
    rgb_grad[...] = jnp.zeros_like(rgb_grad)

    def tile_stores(j, slot):
        return (
            pltpu.make_async_copy(tile.at[slot], conv_out.at[:, :, rows_of(j * TILE, TILE)], tile_sem.at[0, slot]),
            pltpu.make_async_copy(grad_tile.at[slot], feat_natural.at[:, part_of(j)], tile_sem.at[1, slot]),
        )

    raised_store(2, 0).wait()
    raised_store(3, 1).wait()
    for item in stores:
        item.wait()

    @pl.loop(0, tiles)
    def _(j):
        here = rows_of(j * TILE, TILE)
        slot = j % 2

        @pl.when(j >= 2)
        def _():
            for item in tile_stores(j - 2, slot):
                item.wait()

        for phase in range(4):
            summed = None
            for t in range(9):
                term = dot(full2[t], copies[copy_index(phase, t // 3 - 1, t % 3 - 1), :, here])
                summed = term if summed is None else summed + term
            tile[slot, phase] = summed
            noise_row = gains[1] * noise[4 + phase : 5 + phase, here]
            for i in range(channels // ROWS):
                rows = slice(i * ROWS, (i + 1) * ROWS)
                pre = tile[slot, phase, rows, :] * wide(demod2[rows, :]) + noise_row + wide(cols[4, rows, :])
                act = pre * (0.6 * root_two + 0.4 * root_two * jnp.tanh(0.5 * pre))
                out = (act * live).astype(BF)
                low = slice(i * ROWS % 256, i * ROWS % 256 + ROWS)
                for half in range(TILE // 128):
                    core1[2 * half + i * ROWS // 256, low, phase * 128 : (phase + 1) * 128] = (
                        out[:, half * 128 : (half + 1) * 128]
                    )
        for half in range(TILE // 128):
            image = dot(core1[2 * half : 2 * half + 2].reshape(channels, 512), order[...]).astype(BF)
            grad_tile[slot, :, half * 512 : (half + 1) * 512] = image
            pixels = rows_of(j * 4 * TILE + half * 512, 512)
            color[:, pixels] = dot(rgb_rows, image)
            rgb_grad[...] += dot_nt(stacked[:, pixels], image)
        for item in tile_stores(j, slot):
            item.start()

    for j in (2, 3):
        for item in tile_stores(j, j % 2):
            item.wait()
    store1.wait()
    for item in pack_moves + x_moves + near[0] + near[1] + relay[0] + relay[1] + side[0] + side[1] + swap[0] + swap[1]:
        item.wait_send()

    shared_moves = [
        remote(shared, every_shared.at[row], shared_send.at[i], shared_recv.at[i], {"dp": line})
        for i, line in enumerate(lines)
    ]
    for item in shared_moves:
        item.start()
    every_shared[row] = shared[...]

    quarter = color.shape[1] // 4
    color_moves = [
        remote(color.at[0:8, rows_of(chans[k] * quarter, quarter)], color_in.at[me],
               color_send.at[k - 1], color_recv.at[k - 1], {"chan": chans[k]})
        for k in (1, 2, 3)
    ]
    for item in color_moves:
        item.start()
    color_own = pltpu.make_async_copy(color.at[0:8, rows_of(me * quarter, quarter)], color_in.at[me], load_sem.at[9])
    color_own.start()

    feat_moves = [
        remote(feat_natural.at[rows_of(chans[k] * 128, 128), :], feat_all.at[rows_of(me * 128, 128), :],
               feat_send.at[k - 1], feat_recv.at[k - 1], {"chan": chans[k]})
        for k in (1, 2, 3)
    ]
    for item in feat_moves:
        item.start()
    feat_own = pltpu.make_async_copy(
        feat_natural.at[rows_of(me * 128, 128), :], feat_all.at[rows_of(me * 128, 128), :], load_sem.at[0]
    )
    feat_own.start()
    weight, keep, send = full2, full1.at[:, 0:256, :], full1.at[:, 256:512, :]

    def tiles_in(source, j, slot):
        return pltpu.make_async_copy(source.at[:, :, rows_of(j * TILE, TILE)], tile.at[slot], tile_sem.at[0, slot])

    def grads_in(j, slot):
        return pltpu.make_async_copy(
            arrived.at[:, part_of(j)], grad_tile.at[slot], tile_sem.at[1, slot]
        )

    def grads_ready(j):
        for k in (1, 2, 3):
            grad_move(j, k).wait_recv()
        grads_in(j, j % 2).start()

    tiles_in(conv_out, 0, 0).start()
    local3.wait()
    grads_ready(0)
    sums2[...] = jnp.zeros_like(sums2)
    sums1[...] = jnp.zeros_like(sums1)
    style_sums[...] = jnp.zeros_like(style_sums)
    is_color = lax.broadcasted_iota(jnp.int32, (16, channels), 0) < 3
    rgb_rows = jnp.where(is_color, jnp.concatenate([rows_ref[...]] * 2, axis=0), 0.0).astype(BF)

    def add_sums(sums, rows, values):
        for n, value in enumerate(values):
            sums[n, rows, :] += value[:, :128] + value[:, 128:]

    @pl.loop(0, tiles)
    def _(j):
        slot = j % 2

        @pl.when(j + 1 < tiles)
        def _():
            tiles_in(conv_out, j + 1, 1 - slot).start()
            grads_ready(j + 1)

        tiles_in(conv_out, j, slot).wait()
        grads_in(j, slot).wait()
        here = rows_of(j * TILE, TILE)
        for half in range(TILE // 128):
            total[half] = dot(grad_tile[slot, :, half * 512 : (half + 1) * 512], order_back[...])
        for phase in range(4):
            noise_plain = noise[4 + phase : 5 + phase, here]
            noise_row = gains[1] * noise_plain
            back[phase % 2] = lax.dot_general(
                rgb_rows, color_phases[phase, :, here], (((0,), (0,)), ((), ())), preferred_element_type=F32
            )
            for i in range(channels // ROWS):
                rows = slice(i * ROWS, (i + 1) * ROWS)
                conv = tile[slot, phase, rows, :]
                scale = wide(demod2[rows, :])
                pre = conv * scale + noise_row + wide(cols[4, rows, :])
                sigma = 0.5 + 0.5 * jnp.tanh(0.5 * pre)
                slope = root_two * (0.2 + 0.8 * sigma * (1.0 + pre * (1.0 - sigma)))
                grad_feat = jnp.concatenate(
                    [total[half, rows, phase * 128 : (phase + 1) * 128] for half in range(TILE // 128)], axis=1
                )
                grad = (grad_feat * live + back[phase % 2, rows, :] * wide(cols[2, rows, :])) * slope
                copies[4 * phase, rows, here] = (grad * scale).astype(BF)
                add_sums(sums2, rows, (grad * conv, grad, grad * noise_plain))

    tiles_in(raised_out, 0, 0).start()
    late = [
        pltpu.make_async_copy(scaled_one_out, grad_tile.at[0], load_sem.at[4]),
        pltpu.make_async_copy(x_out, grad_tile.at[1], load_sem.at[5]),
    ]
    for item in late:
        item.start()

    def inner_of(sums, demod, inner):
        scale = demod[...]
        inner[...] = -0.5 * scale * scale * scale * jnp.sum(sums[0], axis=1, keepdims=True)

    inner_of(sums2, demod2, inner2)

    def spread_copies():
        chunk = 32

        @pl.loop(0, channels // chunk)
        def _(i):
            rows = rows_of(i * chunk, chunk)
            for phase in range(4):
                value = copies[4 * phase, rows, :]
                row_sign = 1 if phase // 2 == 0 else -1
                col_sign = 1 if phase % 2 == 0 else -1
                for r, q in ((0, 1), (1, 0), (1, 1)):
                    copies[4 * phase + 2 * r + q, rows, :] = move(value, row_sign * r, col_sign * q)

    spread_copies()

    def split(c, slot, t, inner, square_row):
        for k in range(4):
            base = chans[k] * 128
            for out, start in ((keep, base + core * 64), (send, base + 64 - core * 64)):
                rows = rows_of(start, 64)
                column = jnp.concatenate([inner[rows, :]] * 4, axis=1)
                plain = weight[t, rows, :].astype(F32)
                scaled = plain * column
                value = (total[slot, rows, :] + scaled * square_row).astype(BF)
                out[t, k * 32 : (k + 1) * 32, :] = value[:32]
                out[t, 128 + k * 32 : 160 + k * 32, :] = value[32:]
                scaled = plain * scaled
                style_sums[c] += sum(scaled[i * 8 : (i + 1) * 8, :] for i in range(8))

    cores, quads, zsums, zins, outs = (core1, core2), (quad1, quad2), (zsum1, zsum2), (zin1, zin2), (out1, out2)
    firsts = (first1, first2)

    def taps(g):
        return pl.ds(3 * g, 3)

    def core_move(c, g):
        return remote(send.at[taps(g)], cores[c].at[taps(g)], core_send.at[c, g], core_recv.at[c, g], {"dp": twin})

    def first_move(c, g):
        return remote(keep.at[taps(g), rows_of(128 - low * 128, 128), :], firsts[c].at[taps(g)],
                      first_send.at[c, g], first_recv.at[c, g], beside)

    def quad_move(c, g, k):
        return remote(keep.at[taps(g), rows_of(low * 128 + k * 32, 32), :], quads[c].at[taps(g), k - 1],
                      quad_send.at[c, g, k - 1], quad_recv.at[c, g, k - 1], {"chan": chans[k]})

    def z_move(c, g):
        return remote(zsums[c].at[taps(g), rows_of(16 - high * 16, 16), :], zins[c].at[taps(g)],
                      z_send.at[c, g], z_recv.at[c, g], across)

    def across_move(c, g):
        part = outs[c].at[taps(g), rows_of(core * 64 + low * 32 + high * 16, 16), :]
        return remote(part, part, across_send.at[c, g], across_recv.at[c, g], across)

    def beside_move(c, g):
        part = outs[c].at[taps(g), rows_of(core * 64 + low * 32, 32), :]
        return remote(part, part, beside_send.at[c, g], beside_recv.at[c, g], beside)

    def twin_move(c, g):
        part = outs[c].at[taps(g), rows_of(core * 64, 64), :]
        return remote(part, part, twin_send.at[c, g], twin_recv.at[c, g], {"dp": twin})

    def join_cores(c, g):
        core_move(c, g).wait_recv()
        for i in range(3):
            t = 3 * g + i
            keep[t] = (keep[t].astype(F32) + cores[c][t].astype(F32)).astype(BF)
        first_move(c, g).start()

    def join_first(c, g):
        first_move(c, g).wait_recv()
        rows = rows_of(low * 128, 128)
        for i in range(3):
            t = 3 * g + i
            keep[t, rows, :] = (keep[t, rows, :].astype(F32) + firsts[c][t].astype(F32)).astype(BF)
        for k in (1, 2, 3):
            quad_move(c, g, k).start()

    def join_quad(c, g):
        for k in (1, 2, 3):
            quad_move(c, g, k).wait_recv()
        for i in range(3):
            t = 3 * g + i
            value = keep[t, rows_of(low * 128, 32), :].astype(F32)
            for k in range(3):
                value = value + quads[c][t, k].astype(F32)
            zsums[c][t] = value.astype(BF)
        z_move(c, g).start()

    def join_depth(c, g):
        z_move(c, g).wait_recv()
        for i in range(3):
            t = 3 * g + i
            value = zsums[c][t, rows_of(high * 16, 16), :].astype(F32) + zins[c][t].astype(F32)
            outs[c][t, rows_of(core * 64 + low * 32 + high * 16, 16), :] = value.astype(BF)
        across_move(c, g).start()

    def join_across(c, g):
        across_move(c, g).wait_recv()
        beside_move(c, g).start()

    def join_beside(c, g):
        beside_move(c, g).wait_recv()
        twin_move(c, g).start()

    def weight_grad(c, product, inner, square_row):
        @pl.loop(0, 3)
        def _(g):
            t = 3 * g
            total[0] = product(t)
            total[1] = product(t + 1)
            split(c, 0, t, inner, square_row)
            total[0] = product(t + 2)
            split(c, 1, t + 1, inner, square_row)
            split(c, 0, t + 2, inner, square_row)
            core_move(c, g).start()

            @pl.when(g >= 1)
            def _():
                join_cores(c, g - 1)

        join_cores(c, 2)
        for g in range(3):
            core_move(c, g).wait_send()

    def second_product(t):
        row_step, col_step = 1 - t // 3, 1 - t % 3
        summed = None
        for phase in range(4):
            a, b = phase // 2, phase % 2
            far_row = (row_step * (2 * a - 1) + 1) // 2 * (row_step * row_step)
            far_col = (col_step * (2 * b - 1) + 1) // 2 * (col_step * col_step)
            index = (((a + row_step + 2) % 2 * 2 + (b + col_step + 2) % 2) * 2 + far_row) * 2 + far_col
            term = dot_nt(copies[index], field[phase])
            summed = term if summed is None else summed + term
        return summed

    weight_grad(1, second_product, inner2, 2.0 * rows_ref[4:5, :] * rows_ref[4:5, :])

    def turn():
        @pl.loop(0, 9)
        def _(t):
            weight[t] = weight[t].T

    turn()

    @pl.loop(0, tiles)
    def _(j):
        slot = j % 2

        @pl.when(j + 1 < tiles)
        def _():
            tiles_in(raised_out, j + 1, 1 - slot).start()

        tiles_in(raised_out, j, slot).wait()
        here = rows_of(j * TILE, TILE)
        for phase in range(4):
            summed = None
            for t in range(9):
                term = dot(weight[t], copies[copy_index(phase, 1 - t // 3, 1 - t % 3), :, here])
                summed = term if summed is None else summed + term
            back[phase % 2] = summed
            noise_plain = noise[phase : phase + 1, here]
            noise_row = gains[0] * noise_plain
            for i in range(channels // ROWS):
                rows = slice(i * ROWS, (i + 1) * ROWS)
                conv = tile[slot, phase, rows, :]
                scale = wide(demod1[rows, :])
                pre = conv * scale + noise_row + wide(cols[3, rows, :])
                sigma = 0.5 + 0.5 * jnp.tanh(0.5 * pre)
                act = root_two * (pre * (0.2 + 0.8 * sigma))
                slope = root_two * (0.2 + 0.8 * sigma * (1.0 + pre * (1.0 - sigma)))
                value = back[phase % 2, rows, :]
                grad = value * wide(cols[1, rows, :]) * slope
                field[phase, rows, here] = (grad * scale).astype(BF)
                add_sums(sums1, rows, (grad * conv, grad, grad * noise_plain, value * act))

        @pl.when(j == 0)
        def _():
            join_first(1, 0)

        @pl.when(j == 1)
        def _():
            join_first(1, 1)
            join_quad(1, 0)

        @pl.when(j == 2)
        def _():
            join_first(1, 2)
            join_quad(1, 1)

    inner_of(sums1, demod1, inner1)
    load1 = pltpu.make_async_copy(full1_out, weight, load_sem.at[1])
    load1.start()

    @pl.loop(0, channels // 32)
    def _(i):
        rows = rows_of(i * 32, 32)
        for phase, (row_phase, col_phase) in enumerate(phase_pairs):
            value = field[phase, rows, :]
            for k, r in phase_taps[row_phase]:
                for l, q in phase_taps[col_phase]:
                    copies[3 * k + l, rows, :] = move(value, -r, -q)

    join_quad(1, 2)
    for g in range(3):
        for k in (1, 2, 3):
            quad_move(1, g, k).wait_send()
        first_move(1, g).wait_send()
    load1.wait()
    for item in late:
        item.wait()
    weight_grad(0, lambda t: dot_nt(copies[t], grad_tile[0]), inner1, 2.0 * rows_ref[3:4, :] * rows_ref[3:4, :])
    style_loads = [
        pltpu.make_async_copy(style_weight.at[j], total.at[0, :, j * 128 : (j + 1) * 128], load_sem.at[6 + j])
        for j in range(3)
    ]
    for item in style_loads:
        item.start()
    for g in range(3):
        join_depth(1, g)
    turn()

    for n in range(tiles):
        here = slice(n * TILE, (n + 1) * TILE)
        summed = None
        for t in range(9):
            term = dot(weight[t], copies[t, :, here])
            summed = term if summed is None else summed + term
        back[n % 2] = summed
        for i in range(channels // ROWS):
            rows = slice(i * ROWS, (i + 1) * ROWS)
            value = back[n % 2, rows, :]
            copies[9, rows, here] = (value * wide(cols[0, rows, :])).astype(BF)
            item = value * grad_tile[1, rows, here].astype(F32)
            item = item[:, :128] + item[:, 128:]
            sums0[rows, :] = item if n == 0 else sums0[rows, :] + item
        if n == 1:
            join_first(0, 0)
    back_moves = [
        remote(copies.at[9, rows_of(chans[k] * 128, 128), :], back_all.at[me],
               back_send.at[k - 1], back_recv.at[k - 1], {"chan": chans[k]})
        for k in (1, 2, 3)
    ]
    for item in back_moves:
        item.start()
    join_first(0, 1)
    back_own = pltpu.make_async_copy(copies.at[9, rows_of(me * 128, 128), :], back_all.at[me], load_sem.at[2])
    back_own.start()

    def as_row(sums):
        return jnp.sum(sums[...].T, axis=0, keepdims=True)

    style_two, style_one = as_row(sums1.at[3]), as_row(sums0)
    color_grad = rgb_grad[0:8, :]
    vector_rows = [
        style_one + 2.0 * rows_ref[3:4, :] * jnp.sum(style_sums[0], axis=0, keepdims=True),
        style_two + 2.0 * rows_ref[4:5, :] * jnp.sum(style_sums[1], axis=0, keepdims=True),
        sum(rows_ref[k : k + 1, :] * color_grad[k : k + 1, :] for k in range(3)),
        as_row(sums1.at[1]),
        as_row(sums2.at[1]),
        jnp.broadcast_to(jnp.sum(as_row(sums1.at[2]), axis=1, keepdims=True), (1, channels)),
        jnp.broadcast_to(jnp.sum(as_row(sums2.at[2]), axis=1, keepdims=True), (1, channels)),
        jnp.zeros((1, channels), F32),
    ]
    for i, value in enumerate(vector_rows):
        for d in range(4):
            vectors[d, i : i + 1, :] = value[:, d * 128 : (d + 1) * 128]
    color_grad = color_grad * rows_ref[5:6, :]
    for d in range(4):
        vectors[d, 8:16, :] = color_grad[:, d * 128 : (d + 1) * 128]
    owned_moves = [
        remote(vectors.at[chans[k]], owned.at[me], owned_send.at[k - 1], owned_recv.at[k - 1], {"chan": chans[k]})
        for k in (1, 2, 3)
    ]
    for item in owned_moves:
        item.start()
    owned[me] = vectors[me]

    for g in range(3):
        join_across(1, g)
    join_quad(0, 0)
    join_first(0, 2)
    for item in owned_moves:
        item.wait_recv()
    for item in style_loads:
        item.wait()
    latent_part = None
    for j in range(3):
        value = jnp.concatenate([owned[d, j : j + 1, :] for d in range(4)] + [jnp.zeros((4, 128), F32)], axis=0)
        term = lax.dot_general(
            value, total[0, :, j * 128 : (j + 1) * 128], (((1,), (1,)), ((), ())), precision=precise, preferred_element_type=F32
        )
        latent_part = term if latent_part is None else latent_part + term
    latent_in[3] = latent_part
    latent_moves = [
        remote(latent_in.at[3], latent_in.at[k - 1], latent_send.at[k - 1], latent_recv.at[k - 1], {"chan": chans[k]})
        for k in (1, 2, 3)
    ]
    every_moves = [
        remote(owned, every.at[row], every_send.at[i], every_recv.at[i], {"dp": line})
        for i, line in enumerate(lines)
    ]
    for item in latent_moves + every_moves:
        item.start()
    every[row] = owned[...]
    join_depth(0, 0)
    join_quad(0, 1)
    for g in range(3):
        join_beside(1, g)

    for item in feat_moves:
        item.wait_recv()
    feat_own.wait()

    def feat_in(n, half):
        return pltpu.make_async_copy(
            feat_all.at[half * 256 : (half + 1) * 256, n * 512 : (n + 1) * 512], core2.at[n % 4 * 2 + half],
            image_sem.at[n % 4, half],
        )

    def feat_store(n):
        return pltpu.make_async_copy(
            raw.at[n % 2], feat_out.at[:, :, n * 512 : (n + 1) * 512], raw_sem.at[n % 2]
        )

    for n in range(4):
        feat_in(n, 0).start()
        feat_in(n, 1).start()
    for n in range(8):
        if n >= 2:
            feat_store(n - 2).wait()
        feat_in(n, 0).wait()
        feat_in(n, 1).wait()

        @pl.loop(0, 8)
        def _(i):
            value = jnp.stack(
                [core2[n % 4 * 2 + image // 2, rows_of(image % 2 * 128 + i * 16, 16), :] for image in range(4)]
            )
            raw[n % 2, rows_of(i * 16, 16), :, :] = jnp.swapaxes(value, 0, 1)

        feat_store(n).start()
        if n + 4 < 8:
            feat_in(n + 4, 0).start()
            feat_in(n + 4, 1).start()
        if n == 2:
            join_depth(0, 1)
        if n == 4:
            join_across(0, 0)
            join_quad(0, 2)
        if n == 6:
            join_across(0, 1)
            join_beside(0, 0)
    join_depth(0, 2)
    join_beside(0, 1)

    for item in shared_moves + every_moves:
        item.wait_recv()
    sums_all[...] = sum(every[r, b] for r in range(8) for b in range(4))
    shared_sum[...] = sum(every_shared[r] for r in range(8))
    latents = jnp.concatenate([every_shared[r, 0:4, :] for r in range(8)], axis=0)
    style_stores = []
    for j in range(3):
        value = jnp.concatenate([every[r, b, j : j + 1, :] for r in range(8) for b in range(4)], axis=0)
        total[0, :, j * 128 : (j + 1) * 128] = lax.dot_general(
            latents, value, (((0,), (0,)), ((), ())), precision=precise, preferred_element_type=F32
        )
        style_stores.append(
            pltpu.make_async_copy(total.at[0, :, j * 128 : (j + 1) * 128], style_out.at[j], load_sem.at[6 + j])
        )
        style_stores[j].start()
    for g in range(3):
        twin_move(1, g).wait()
    store2 = pltpu.make_async_copy(out2, grad2_out, load_sem.at[1])
    store2.start()
    join_across(0, 2)
    for item in latent_moves:
        item.wait_recv()
    latent_grad[...] = latent_in[0] + latent_in[1] + latent_in[2] + latent_in[3]
    join_beside(0, 2)
    for g in range(3):
        twin_move(0, g).wait()
    store1 = pltpu.make_async_copy(out1, grad1_out, load_sem.at[3])
    store1.start()
    feat_store(6).wait()
    feat_store(7).wait()
    for c in (0, 1):
        for g in range(3):
            if c == 0:
                first_move(c, g).wait_send()
                for k in (1, 2, 3):
                    quad_move(c, g, k).wait_send()
            z_move(c, g).wait_send()
            across_move(c, g).wait_send()
            beside_move(c, g).wait_send()
    for item in feat_moves:
        item.wait_send()
    for item in back_moves + color_moves + style_stores:
        item.wait()
    for item in shared_moves + every_moves:
        item.wait_send()
    for item in owned_moves + latent_moves:
        item.wait_send()
    for j in range(4):
        for k in (1, 2, 3):
            grad_move(j, k).wait_send()
    for item in (back_own, color_own, store2, store1):
        item.wait()


def pick(value, index, axis):
    return lax.dynamic_index_in_dim(value, index, axis, keepdims=False)


def phase_order():
    place = jnp.arange(512)
    row, col = place // SIDE, place % SIDE
    grouped = ((row % 2) * 2 + col % 2) * 128 + (row // 2) * HALF + col // 2
    return (jnp.arange(512)[:, None] == grouped[None, :]).astype(BF)


def image_body(
    feat_in,
    rgb_in,
    latent,
    noise_first,
    noise_second,
    live_count,
    conv_first,
    conv_second,
    style_weight,
    style_bias,
    rgb_weight,
    conv_bias,
    rgb_bias,
    noise_gain,
    feat_grad,
    rgb_grad,
):
    local_ch, images, half_pix = feat_in.shape
    channels = 4 * local_ch
    pixels = feat_grad.shape[2]
    me = lax.axis_index("chan")
    live_mask = (jnp.arange(images) < live_count[0]).astype(F32)
    live = (me < live_count[0]).astype(F32)
    gains = jnp.concatenate([noise_gain, live[None]])
    styles = jnp.einsum("bw,jwc->bjc", latent, style_weight, precision=precise) + style_bias[None]

    def each_image(value):
        return jnp.broadcast_to(value[None], (images,) + value.shape)

    pack = jnp.concatenate([each_image(rgb_weight.astype(F32)), styles, each_image(conv_bias)], axis=1)
    plain = jnp.concatenate(
        [pick(rgb_grad, me, 0) * live, pick(noise_first, me, 0)[None], pick(noise_second, me, 0)[None],
         jnp.zeros((3, pixels), F32)]
    )
    x_by_image = feat_in.transpose(1, 0, 2)
    order = phase_order()

    vmem = pl.BlockSpec(memory_space=pltpu.VMEM)
    field, wide_weight = (4, channels, half_pix), (9, channels, channels)
    rgb_cot = rgb_grad * live_mask[:, None, None]
    rgb_bias_part = jnp.sum(rgb_cot, axis=(0, 2))
    shared = jnp.concatenate([latent, jnp.broadcast_to(jnp.pad(rgb_bias_part, (0, 509))[None], (4, 512))])
    outs = (
        (field, F32), (field, F32), ((channels, pixels), BF), (wide_weight, BF), ((channels, pixels), BF),
        ((channels, half_pix), BF), ((channels, half_pix), BF), ((channels, pixels), BF), ((channels, pixels), BF),
        (feat_grad.shape, BF), ((4, local_ch, half_pix), BF), ((9, local_ch, channels), BF),
        ((9, local_ch, channels), BF), ((4, 8, pixels // 4), F32), (style_weight.shape, F32), ((16, 128), F32), ((8, 512), F32),
        ((8, 512), F32),
    )
    vector = ((channels, 128), F32)
    scratch = (
        vector, vector, ((16, pixels), F32), ((16, channels), F32), ((5, channels, 128), F32), ((8, channels), F32),
        ((8, half_pix), F32), ((4, 16, half_pix), BF), ((4, 8, 128), F32), ((16, pixels), BF),
        (wide_weight, BF), (wide_weight, BF), ((16, channels, half_pix), BF), ((2, 4, channels, TILE), F32),
        ((2, channels, 4 * TILE), BF), (field, BF), ((2, channels, channels), F32), ((2, channels, TILE), F32),
        ((9, 256, channels), BF), ((9, 256, channels), BF), ((9, 128, channels), BF), ((9, 128, channels), BF),
        ((9, 3, 32, channels), BF), ((9, 3, 32, channels), BF), ((9, 32, channels), BF), ((9, 32, channels), BF),
        ((9, 16, channels), BF), ((9, 16, channels), BF),
        ((9, local_ch, channels), BF), ((9, local_ch, channels), BF),
        ((3, channels, 128), F32), ((4, channels, 128), F32), vector, vector, vector, ((2, 8, channels), F32),
        ((4, 16, 128), F32), ((4, 16, 128), F32), ((4, 8, 512), F32), ((2, local_ch, 4, 512), BF),
        ((8, 4, 16, 128), F32), ((8, 8, 512), F32),
    )
    counts = (
        [(10,), (5,), (2, 2)] + [(3,)] * 4 + [(2, 4)] * 2 + [(2, 6)] * 2 + [(4, 3)] * 2 + [(3,)] * 4
        + [(2, 3)] * 2 + [(2, 3, 3)] * 2 + [(2, 3)] * 10 + [(7,)] * 4 + [(3,)] * 6 + [(2,), (4, 2), (2, 3), (2, 3)]
    )
    results = pl.pallas_call(
        block_kernel,
        in_specs=[SMEM] + [ANY] * 5 + [vmem] * 3 + [ANY, vmem],
        out_specs=[ANY] * 15 + [vmem] * 3,
        out_shape=[jax.ShapeDtypeStruct(shape, dtype) for shape, dtype in outs],
        scratch_shapes=[pltpu.VMEM(shape, dtype) for shape, dtype in scratch]
        + [pltpu.SemaphoreType.DMA(count) for count in counts],
        compiler_params=pltpu.CompilerParams(vmem_limit_bytes=LIMIT, collective_id=0, has_side_effects=True),
        cost_estimate=pl.CostEstimate(flops=int(150e9), bytes_accessed=12 << 20, transcendentals=0),
    )(gains, pack, x_by_image, conv_first, conv_second, feat_grad, plain, order.T, order, style_weight, shared)
    feat_out, back_all, grad_one, grad_two, color_in, style_weight_grad, summed, shared_sum, latent_grad = results[9:]
    feat_in_grad = back_all.transpose(1, 0, 2).astype(F32)
    grad_one, grad_two = grad_one.astype(F32), grad_two.astype(F32)

    lift_matrix = upsample_matrix(HALF)
    shard_pix = pixels // 4
    skip_up = jnp.einsum(
        "up,bkpq,vq->bkuv",
        lift_matrix,
        rgb_in.reshape(images, 3, HALF, HALF),
        lift_matrix,
        precision=precise,
    ).reshape(images, 3, pixels)
    skip_mine = lax.dynamic_slice_in_dim(skip_up, me * shard_pix, shard_pix, 2)
    rgb_out = (color_in[:, :3] + rgb_bias[None, :, None] + skip_mine) * live_mask[:, None, None]
    rgb_in_grad = jnp.einsum(
        "up,bkuv,vq->bkpq",
        lift_matrix,
        rgb_cot.reshape(images, 3, SIDE, SIDE),
        lift_matrix,
        precision=precise,
    ).reshape(images, 3, half_pix)

    return (
        feat_out,
        rgb_out,
        feat_in_grad,
        rgb_in_grad,
        latent_grad[:4],
        grad_one,
        grad_two,
        style_weight_grad,
        summed[:3],
        summed[8:11],
        summed[3:5],
        shared_sum[4, :3],
        summed[5:7, 0],
    )


def solution(mesh):
    alone = mesh.shape["chan"] == 4 and mesh.shape["dp"] == 8
    return jax.shard_map(
        image_body if alone else body,
        mesh=mesh,
        in_specs=(
            P("chan", "dp", None),
            P("dp", None, None),
            P("dp", None),
            P("dp", None),
            P("dp", None),
            P("dp"),
            P(None, "chan", None),
            P(None, "chan", None),
            P(None, None, "chan"),
            P(None, "chan"),
            P(None, "chan"),
            P(None, "chan"),
            P(),
            P(),
            P("chan", "dp", None),
            P("dp", None, None),
        ),
        out_specs=(
            P("chan", "dp", None),
            P("dp", None, "chan"),
            P("chan", "dp", None),
            P("dp", None, None),
            P("dp", None),
            P(None, "chan", None),
            P(None, "chan", None),
            P(None, None, "chan"),
            P(None, "chan"),
            P(None, "chan"),
            P(None, "chan"),
            P(),
            P(),
        ),
        check_vma=False,
    )
```
